32 devices in a mesh: dp: 16 (over z, y, core), mp: 2 (over x).
Axes of the slice: x: 2, y: 2, z: 4, core: 2. Of those that a mesh axis runs over, the one named last changes fastest.
Arguments:
- patches: bfloat16 [256, 49, 768], P(('dp', 'mp')), may hold values from -6 to 6
- token_valid: int32 [256, 49], P(('dp', 'mp')), may hold values from 0 to 1, as said below
- ln1_gain: float32 [768], replicated, may hold values from 0.5 to 1.5
- ln1_shift: float32 [768], replicated, may hold values from -2.5 to 2.5
- qkv_weight: bfloat16 [768, 3, 768], P(None, None, 'mp'), may hold values from -0.21875 to 0.21875
- qv_bias: float32 [2, 768], P(None, 'mp'), may hold values from -2.5 to 2.5
- bias_table: float32 [169, 24], P(None, 'mp'), may hold values from -3 to 3
- proj_weight: bfloat16 [768, 768], P('mp'), may hold values from -1 to 1
- proj_bias: float32 [768], replicated, may hold values from -2.5 to 2.5
- ln2_gain: float32 [768], replicated, may hold values from 0.5 to 1.5
- ln2_shift: float32 [768], replicated, may hold values from -2.5 to 2.5
- fc1_weight: bfloat16 [768, 3072], P(None, 'mp'), may hold values from -0.21875 to 0.21875
- fc1_bias: float32 [3072], P('mp'), may hold values from -2.5 to 2.5
- fc2_weight: bfloat16 [3072, 768], P('mp'), may hold values from -0.109375 to 0.109375
- fc2_bias: float32 [768], replicated, may hold values from -2.5 to 2.5
- cotangent: bfloat16 [256, 49, 768], P(('dp', 'mp')), may hold values from -6 to 6
Outputs:
- output: bfloat16 [256, 49, 768], P(('dp', 'mp'))
- g_patches: bfloat16 [256, 49, 768], P(('dp', 'mp'))
- g_ln1_gain: float32 [768], replicated
- g_ln1_shift: float32 [768], replicated
- g_qkv_weight: float32 [768, 3, 768], P(None, None, 'mp')
- g_qv_bias: float32 [2, 768], P(None, 'mp')
- g_bias_table: float32 [169, 24], P(None, 'mp')
- g_proj_weight: float32 [768, 768], P('mp')
- g_proj_bias: float32 [768], replicated
- g_ln2_gain: float32 [768], replicated
- g_ln2_shift: float32 [768], replicated
- g_fc1_weight: float32 [768, 3072], P(None, 'mp')
- g_fc1_bias: float32 [3072], P('mp')
- g_fc2_weight: float32 [3072, 768], P('mp')
- g_fc2_bias: float32 [768], replicated
The draws below stay inside these ranges and needn't reach their ends.
Inputs may be any that keep to these rules, and one draw needn't show every extreme that they name: `token_valid`: in each window the valid patches fill the top-left rows and columns of its 7 x 7 grid, at least 3 x 3 of them; the first patch is always valid.
All inputs are finite; a program needn't handle non-finite values.
Results may differ from the reference program's by a relative error of at most 0.02.
Values may be sent and summed in bfloat16 or wider, within the bound.
No kernel may reach another device: no remote copies, remote signals or barrier semaphores. Data moves between devices by JAX's collectives and lax.ppermute only.
A program may use at most 192 MiB of HBM per device.

```python
import jax
import jax.numpy as jnp
from jax import lax

C = 768
HEADS = 24
HEAD = 32
FF = 3072
WSIDE = 7
WIN = 49
REL = 169
GROUP_WIN = 16
WINDOWS = 256
N_DP = 16


def draw_token_valid(key, part):
    key = jax.random.fold_in(key, 5)
    key_full, key_rows, key_cols = jax.random.split(key, 3)
    full_flag = jax.random.randint(key_full, (WINDOWS,), 0, 2)
    row_limit = jax.random.randint(key_rows, (WINDOWS,), 3, WSIDE + 1)
    col_limit = jax.random.randint(key_cols, (WINDOWS,), 3, WSIDE + 1)
    row_limit = jnp.where(full_flag == 1, WSIDE, row_limit)
    col_limit = jnp.where(full_flag == 1, WSIDE, col_limit)
    places = jnp.arange(WIN, dtype=jnp.int32)
    inside = (places[None, :] // WSIDE < row_limit[:, None]) & (places[None, :] % WSIDE < col_limit[:, None])
    return inside.astype(jnp.int32)


def shard_levels(rng, shape, shards, least, high):
    factor_of, own = 1.0, jax.random.fold_in(rng, 6)
    for position, parts in shards:
        draws = jnp.exp(jax.random.uniform(jax.random.fold_in(own, position), (parts,), jnp.float32, least / len(shards), high / len(shards)))
        factor_of = factor_of * jnp.repeat(draws, shape[position] // parts).reshape([-1 if axis == position else 1 for axis in range(len(shape))])
    return factor_of


def gaussian(rng, extent, spread, most, pieces=(), kind=jnp.bfloat16):
    loudness = shard_levels(rng, extent, pieces, -0.22, 0.18) if pieces else 1.0
    values = jax.random.normal(rng, extent, jnp.float32) * spread * loudness
    return jnp.minimum(jnp.maximum(values, -most), most).astype(kind)


def setup_inputs(seed: int = 0) -> dict:
    arg_keys = jax.random.split(jax.random.key(seed), 17)
    return {
        "patches": gaussian(arg_keys[0], (WINDOWS, WIN, C), 1.0, 6.0, ((0, 32),)),
        "token_valid": draw_token_valid(jax.random.fold_in(arg_keys[16], 71), 0),
        "ln1_gain": jnp.clip(1.0 + 0.1 * jax.random.normal(arg_keys[2], (C,), jnp.float32), 0.5, 1.5),
        "ln1_shift": gaussian(arg_keys[3], (C,), 0.3, 2.5, (), jnp.float32),
        "qkv_weight": gaussian(arg_keys[4], (C, 3, C), C ** -0.5, 0.21875, ((2, 2),)),
        "qv_bias": gaussian(arg_keys[5], (2, C), 0.3, 2.5, ((1, 2),), jnp.float32),
        "bias_table": gaussian(arg_keys[6], (REL, HEADS), 0.5, 3.0, ((1, 2),), jnp.float32),
        "proj_weight": gaussian(arg_keys[7], (C, C), HEAD ** -0.5, 1.0, ((0, 2),)),
        "proj_bias": gaussian(arg_keys[8], (C,), 0.3, 2.5, (), jnp.float32),
        "ln2_gain": jnp.clip(1.0 + 0.1 * jax.random.normal(arg_keys[9], (C,), jnp.float32), 0.5, 1.5),
        "ln2_shift": gaussian(arg_keys[10], (C,), 0.3, 2.5, (), jnp.float32),
        "fc1_weight": gaussian(arg_keys[11], (C, FF), C ** -0.5, 0.21875, ((1, 2),)),
        "fc1_bias": gaussian(arg_keys[12], (FF,), 0.3, 2.5, ((0, 2),), jnp.float32),
        "fc2_weight": gaussian(arg_keys[13], (FF, C), FF ** -0.5, 0.109375, ((0, 2),)),
        "fc2_bias": gaussian(arg_keys[14], (C,), 0.3, 2.5, (), jnp.float32),
        "cotangent": gaussian(arg_keys[15], (WINDOWS, WIN, C), 1.0, 6.0, ((0, 32),)),
    }


@jax.custom_vjp
def low(v):
    return lax.optimization_barrier(v.astype(jnp.bfloat16)).astype(jnp.float32)

@jax.custom_vjp
def low_back(v):
    return v

def low_keep(v):
    return (low(v), None)

def low_pass(kept, grad):
    return (grad,)

def back_keep(v):
    return (v, None)

def back_low(kept, grad):
    return (low(grad),)
low.defvjp(low_keep, low_pass)
low_back.defvjp(back_keep, back_low)
HIGH = lax.Precision.HIGHEST

def layer_norm(row_data, gain, shift):
    row_mean = lax.optimization_barrier(jnp.mean(row_data, axis=-1, keepdims=True))
    centred = row_data - row_mean
    variance = lax.optimization_barrier(jnp.mean(centred * centred, axis=-1, keepdims=True))
    return centred * lax.rsqrt(variance + 1e-05) * gain + shift

def relative_index():
    places = jnp.arange(WIN, dtype=jnp.int32)
    row_pos = places // WSIDE
    col_pos = places % WSIDE
    row_delta = row_pos[:, None] - row_pos[None, :] + (WSIDE - 1)
    col_delta = col_pos[:, None] - col_pos[None, :] + (WSIDE - 1)
    return (row_delta * (2 * WSIDE - 1) + col_delta).astype(jnp.int32)

def window_block(params, inputs, flag_rows):
    ln1_gain, ln1_shift, qkv_weight, qv_bias, bias_table, proj_weight, proj_bias, ln2_gain, ln2_shift, fc1_weight, fc1_bias, fc2_weight, fc2_bias = params
    win_count = inputs.shape[0]
    row_data = inputs.reshape(win_count * WIN, C)
    normed = low(layer_norm(row_data, ln1_gain, ln1_shift))
    packed = jnp.einsum('rc,cjd->rjd', normed, qkv_weight, precision=HIGH)
    head_shape = (win_count, WIN, HEADS, HEAD)
    queries = low_back(low(packed[:, 0] + qv_bias[0])).reshape(head_shape)
    key_vecs = low_back(low(packed[:, 1])).reshape(head_shape)
    values = low_back(low(packed[:, 2] + qv_bias[1])).reshape(head_shape)
    rel_table = bias_table[relative_index()]
    pos_bias = jnp.transpose(rel_table, (2, 0, 1))
    scores = jnp.einsum('bqhd,bkhd->bhqk', queries, key_vecs, precision=HIGH) * HEAD ** (-0.5) + pos_bias[None]
    scores = low_back(scores)
    scores = jnp.where(flag_rows[:, None, None, :] == 1, scores, -1000000000.0)
    attn_prob = low(jax.nn.softmax(scores, axis=-1))
    mixed = jnp.einsum('bhqk,bkhd->bqhd', attn_prob, values, precision=HIGH)
    mixed = low_back(low(mixed)).reshape(win_count * WIN, C)
    branch = low_back(jnp.dot(mixed, proj_weight, precision=HIGH))
    middle = row_data + branch + proj_bias
    normed_mid = low(layer_norm(middle, ln2_gain, ln2_shift))
    hidden_pre = low_back(jnp.dot(normed_mid, fc1_weight, precision=HIGH) + fc1_bias)
    hidden = low(jax.nn.gelu(hidden_pre, approximate=False))
    branch_mlp = low_back(jnp.dot(hidden, fc2_weight, precision=HIGH))
    return (middle + branch_mlp + fc2_bias).reshape(win_count, WIN, C)

def reference(patches, token_valid, ln1_gain, ln1_shift, qkv_weight, qv_bias, bias_table, proj_weight, proj_bias, ln2_gain, ln2_shift, fc1_weight, fc1_bias, fc2_weight, fc2_bias, cotangent):
    params = (ln1_gain, ln1_shift, qkv_weight.astype(jnp.float32), qv_bias, bias_table, proj_weight.astype(jnp.float32), proj_bias, ln2_gain, ln2_shift, fc1_weight.astype(jnp.float32), fc1_bias, fc2_weight.astype(jnp.float32), fc2_bias)

    def forward(weights, inputs):
        blocks = inputs.reshape(N_DP, GROUP_WIN, WIN, C)
        flag_blocks = token_valid.reshape(N_DP, GROUP_WIN, WIN)
        checked = jax.checkpoint(window_block)
        results = lax.map(lambda couple: checked(weights, couple[0], couple[1]), (blocks, flag_blocks))
        return results.reshape(WINDOWS, WIN, C)
    result, pullback = jax.vjp(forward, params, patches.astype(jnp.float32))
    grads, grad_input = pullback(cotangent.astype(jnp.float32))
    return (result.astype(jnp.bfloat16), grad_input.astype(jnp.bfloat16), grads[0], grads[1], grads[2], grads[3], grads[4], grads[5], grads[6], grads[7], grads[8], grads[9], grads[10], grads[11], grads[12])
```

```python
import functools

import jax
import jax.numpy as jnp
from jax import lax
from jax.experimental import pallas as pl
from jax.experimental.pallas import tpu as pltpu
from jax.sharding import PartitionSpec as P

HEAD = 32
WSIDE = 7
WIN = 49
REL = 169
SLOT = 64
GROUP = 4
LANES = 128
EPS = 1e-05
SCALING = HEAD ** (-0.5)
BF = jnp.bfloat16
F32 = jnp.float32
HIGH = lax.Precision.HIGHEST
VMEM_LIMIT = 28 * 1024 * 1024
ALL_VMEM = 58 * 1024 * 1024
BLOCK = 96
CORE, SIDE, LINE = 1, 2, 4

ROW_COL = (((1,), (0,)), ((), ()))
LAST_LAST = (((1,), (1,)), ((), ()))
ROWS_ROWS = (((0,), (0,)), ((), ()))


def mm(a, b, dims=ROW_COL):
    return lax.dot_general(a, b, dims, preferred_element_type=F32)


def norm_parts(rows):
    mean = jnp.mean(rows, axis=-1, keepdims=True)
    centred = rows - mean
    variance = jnp.mean(centred * centred, axis=-1, keepdims=True)
    inv = lax.rsqrt(variance + EPS)
    return centred * inv, inv


def norm_back(xhat, inv, gain, upstream):
    z = upstream * gain
    mean_z = jnp.mean(z, axis=-1, keepdims=True)
    mean_zx = jnp.mean(z * xhat, axis=-1, keepdims=True)
    return (z - mean_z - xhat * mean_zx) * inv


def head_masks():
    lane = lax.broadcasted_iota(jnp.int32, (SLOT, LANES), 1)
    return [jnp.where((lane >> 5) == h, 1.0, 0.0).astype(BF) for h in range(GROUP)]


def block_ones():
    row = lax.broadcasted_iota(jnp.int32, (GROUP * SLOT, GROUP * SLOT), 0)
    col = lax.broadcasted_iota(jnp.int32, (GROUP * SLOT, GROUP * SLOT), 1)
    return jnp.where((row >> 6) == (col >> 6), 1.0, 0.0).astype(BF)


def spread(tile, masks):
    return jnp.concatenate([tile * m for m in masks], axis=0)


def collect(full, masks_f):
    total = full[0:SLOT] * masks_f[0]
    for h in range(1, GROUP):
        total = total + full[h * SLOT : (h + 1) * SLOT] * masks_f[h]
    return total


def fill(scratch, rows):
    count = rows.shape[0]
    for g in range(scratch.shape[0]):
        scratch[g, 0:count, :] = rows[:, g * LANES : (g + 1) * LANES]
        scratch[g, count:, :] = jnp.zeros((scratch.shape[1] - count, LANES), rows.dtype)


def empty(scratch, count):
    return jnp.concatenate([scratch[g, 0:count, :] for g in range(scratch.shape[0])], axis=1).astype(BF)


def row_max(tile, low_half):
    low = jnp.max(jnp.where(low_half, tile, -3e38), axis=-1, keepdims=True)
    high = jnp.max(jnp.where(low_half, -3e38, tile), axis=-1, keepdims=True)
    return jnp.where(low_half, low, high)


def ds(start, size):
    unit = 384 if size % 384 == 0 else 48
    return pl.ds(pl.multiple_of(start, unit), size)


def each_block(me, *by_core):
    for c_rel, target in enumerate(by_core):
        for y_rel in range(2):
            for z_rel in range(4):
                yield target, y_rel, z_rel, (me & 1) ^ c_rel, ((me >> 1) & 1) ^ y_rel, (me >> 2) ^ z_rel


def line(ref):
    return ref[...].reshape(1, -1)


def begin(sems, *pairs):
    copies = [pltpu.make_async_copy(a, b, sems.at[i]) for i, (a, b) in enumerate(pairs)]
    for copy in copies:
        copy.start()
    return copies


def finish_all(copies):
    for copy in copies:
        copy.wait()


def attn_forward_kernel(windows, x_in, gain_ref, shift_ref, w_in, bias_ref, pos_ref, valid_ref,
                        prob_ref, q_ref, k_ref, v_ref, mixed_ref, normed_t_ref,
                        mask_s, q_s, k_s, v_s, mixed_s, x_ref, w_ref, in_sems):
    copies = begin(in_sems, (x_in, x_ref), *[(w_in.at[p], w_ref.at[p]) for p in range(3)])
    mask_s[...] = jnp.zeros(mask_s.shape, F32)
    for h in range(GROUP):
        mask_s[:, h * SLOT : h * SLOT + WIN] = valid_ref[...].astype(F32)
    masks = head_masks()
    ones = block_ones()
    low_half = lax.broadcasted_iota(jnp.int32, (SLOT, LANES), 1) < SLOT
    copies[0].wait()
    x = x_ref[...].astype(F32)
    rows = x.shape[0]
    groups = q_s.shape[0]
    xhat, _ = norm_parts(x)
    normed = (xhat * line(gain_ref) + line(shift_ref)).astype(BF)
    normed_t_ref[...] = normed.T
    for part, scratch in enumerate((q_s, k_s, v_s)):
        copies[1 + part].wait()
        got = mm(normed, w_ref[part])
        if part != 1:
            got = got + bias_ref[part // 2 : part // 2 + 1, :]
        fill(scratch, got.astype(BF).astype(F32))

    def window(w, carry):
        allowed = jnp.broadcast_to(mask_s[pl.ds(w, 1), :], (SLOT, GROUP * SLOT)) > 0.5
        for g in range(groups):
            cols = slice(g * LANES, (g + 1) * LANES)
            places = pl.ds(w, SLOT, stride=windows)
            q = q_s[g, places, :].astype(BF)
            k = k_s[g, places, :].astype(BF)
            v = v_s[g, places, :].astype(BF)
            q_ref[w, :, cols] = q
            k_ref[w, :, cols] = k
            v_ref[w, :, cols] = v
            scores = mm(q, spread(k, masks), LAST_LAST) * SCALING + pos_ref[g]
            scores = jnp.where(allowed, scores, -1000000000.0)
            top = jnp.concatenate([row_max(scores[:, :LANES], low_half), row_max(scores[:, LANES:], low_half)], axis=1)
            e = jnp.exp(scores - top)
            total = mm(e.astype(BF), ones)
            prob = (e / total).astype(BF)
            prob_ref[w, g] = prob
            mixed_s[g, places, :] = mm(prob, spread(v, masks))
        return carry

    lax.fori_loop(0, windows, window, 0, unroll=2)
    mixed_ref[...] = empty(mixed_s, rows)


def middle_kernel(x_ref, own_ref, peer_ref, bias_ref, gain_ref, shift_ref, middle_ref, nm_ref):
    middle = x_ref[...].astype(F32) + (own_ref[...].astype(F32) + peer_ref[...].astype(F32)) + line(bias_ref)
    middle_ref[...] = middle
    xhat, _ = norm_parts(middle)
    nm_ref[...] = (xhat * line(gain_ref) + line(shift_ref)).astype(BF)


def mlp_kernel(nm_ref, cot_ref, fc1_ref, b1_ref, fc2_ref, hid_ref, gpre_ref, out_ref, gmid_ref):
    hidden_size = fc1_ref.shape[1]
    features = fc1_ref.shape[0]
    step = 256 if hidden_size % 256 == 0 else 128
    count = hidden_size // step

    nm = nm_ref[...]
    cot = cot_ref[...]

    def units(c, carry):
        cols = pl.ds(pl.multiple_of(c * step, step), step)
        pre = mm(nm, fc1_ref[:, cols]) + b1_ref[:, cols]
        phi = 0.5 * (1.0 + lax.erf(pre * (0.5 ** 0.5)))
        hid_ref[:, cols] = (pre * phi).astype(BF)
        slope = phi + pre * (jnp.exp(-0.5 * pre * pre) * 0.3989422804014327)
        gpre_ref[:, cols] = (mm(cot, fc2_ref[cols, :], LAST_LAST) * slope).astype(BF)
        return carry

    lax.fori_loop(0, count, units, 0)

    def tile(c, carry):
        cols = pl.ds(pl.multiple_of(c * 256, 256), 256)
        gmid_ref[:, cols] = mm(gpre_ref[...], fc1_ref[cols, :], LAST_LAST).astype(BF)
        out_ref[:, cols] = mm(hid_ref[...], fc2_ref[:, cols]).astype(BF)
        return carry

    lax.fori_loop(0, features // 256, tile, 0)

def mlp_weights_kernel(count, split, me_ref, *refs):
    inputs, refs = refs[: 4 * count], refs[4 * count :]
    n_out = 5 if split else 3
    gb1_ref, *outs = refs[:n_out]
    held = refs[n_out : n_out + 4 * count]
    nts = refs[n_out + 4 * count : n_out + 5 * count]
    g1_ref, g2_ref, in_sems, out_sems = refs[n_out + 5 * count :]
    order = [4 * b + k for k in (0, 2, 1, 3) for b in range(count)]
    copies = dict(zip(order, begin(in_sems, *[(inputs[i], held[i]) for i in order])))
    blocks = [held[4 * b : 4 * b + 4] for b in range(count)]
    hidden_size = g1_ref.shape[1]
    features = g1_ref.shape[0]
    step = 384 if hidden_size % 384 == 0 else 128
    wide = features if hidden_size % features == 0 else step
    finish_all([copies[4 * b] for b in range(count)])
    for block, nt in zip(blocks, nts):
        nt[...] = block[0][...].T
    finish_all([copies[4 * b + k] for k in (2, 1) for b in range(count)])

    def second(j, carry):
        cols = ds(j * step, step)
        g2_ref[cols, :] = sum(mm(hid_ref[:, cols], cot_ref[...], ROWS_ROWS) for _, cot_ref, hid_ref, _ in blocks).astype(BF)
        return carry

    def first(j, carry):
        cols = ds(j * wide, wide)
        g1_ref[:, cols] = sum(mm(nt[...], block[3][:, cols]) for nt, block in zip(nts, blocks)).astype(BF)
        return carry

    lax.fori_loop(0, hidden_size // step, second, 0)
    me = me_ref[0]
    sent = []

    def send(k, source, target):
        sent.append(pltpu.make_async_copy(source, target, out_sems.at[k]))
        sent[-1].start()

    if split:
        for i, (target, y_rel, z_rel, c, y, z) in enumerate(each_block(me, outs[2], outs[3])):
            send(i, g2_ref.at[ds(c * 768 + y * 384 + z * 96, 96), :], target.at[y_rel, z_rel])
    else:
        send(0, g2_ref, outs[1])
    finish_all([copies[4 * b + 3] for b in range(count)])
    gb1_ref[...] = sum(jnp.sum(block[3][...].astype(F32), axis=0, keepdims=True) for block in blocks)
    lax.fori_loop(0, hidden_size // wide, first, 0)
    if split:
        for i, (target, y_rel, z_rel, c, y, z) in enumerate(each_block(me, outs[0], outs[1])):
            send(16 + i, g1_ref.at[ds(y * 384 + z * 96, 96), ds(c * 768, 768)], target.at[y_rel, z_rel])
    else:
        send(1, g1_ref, outs[0])
    finish_all(sent)


def middle_back_kernel(own_ref, peer_ref, middle_ref, cot_ref, gain_ref, gmiddle_ref, branch_ref, sums_ref):
    upstream = cot_ref[...].astype(F32)
    xhat, inv = norm_parts(middle_ref[...])
    gmid = own_ref[...].astype(F32) + peer_ref[...].astype(F32)
    sums_ref[0:1, :] = jnp.sum(gmid * xhat, axis=0, keepdims=True)
    sums_ref[1:2, :] = jnp.sum(gmid, axis=0, keepdims=True)
    gmiddle = upstream + norm_back(xhat, inv, line(gain_ref), gmid)
    gmiddle_ref[...] = gmiddle
    branch_ref[...] = gmiddle.astype(BF)
    sums_ref[2:3, :] = jnp.sum(gmiddle, axis=0, keepdims=True)
    sums_ref[3:4, :] = jnp.sum(upstream, axis=0, keepdims=True)


def attn_backward_kernel(windows, branch_ref, x_ref, prob_ref, q_ref, k_ref, v_ref, w_ref, proj_ref,
                         grads_ref, gqv_ref, gpos_ref, part_ref, sums_ref, gm_s, gq_s, gk_s, gv_s):
    rows = branch_ref.shape[0]
    groups = gm_s.shape[0]
    gpos_ref[...] = jnp.zeros(gpos_ref.shape, F32)
    masks = head_masks()
    masks_f = [m.astype(F32) for m in masks]
    ones = block_ones()
    fill(gm_s, mm(branch_ref[...], proj_ref[...], LAST_LAST).astype(BF).astype(F32))

    def window(w, carry):
        for g in range(groups):
            cols = slice(g * LANES, (g + 1) * LANES)
            places = pl.ds(w, SLOT, stride=windows)
            gm = gm_s[g, places, :].astype(BF)
            q = q_ref[w, :, cols]
            k = k_ref[w, :, cols]
            v = v_ref[w, :, cols]
            prob = prob_ref[w, g]
            prob_f = prob.astype(F32)
            gprob = mm(gm, spread(v, masks), LAST_LAST)
            both = prob_f * gprob
            delta = mm(both.astype(BF), ones)
            gs = (both - prob_f * delta).astype(BF)
            gpos_ref[g] += gs.astype(F32)
            gq_s[g, places, :] = mm(gs, spread(k, masks)) * SCALING
            gk_s[g, places, :] = collect(mm(gs, q, ROWS_ROWS), masks_f) * SCALING
            gv_s[g, places, :] = collect(mm(prob, gm, ROWS_ROWS), masks_f)
        return carry

    lax.fori_loop(0, windows, window, 0, unroll=2)
    back = None
    for part, scratch in enumerate((gq_s, gk_s, gv_s)):
        grad = empty(scratch, rows)
        grads_ref[part] = grad
        if part != 1:
            width = grad.shape[1]
            lanes = slice(part // 2 * width, (part // 2 + 1) * width)
            gqv_ref[:, lanes] = jnp.sum(grad.astype(F32), axis=0, keepdims=True)
        term = mm(grad, w_ref[part], LAST_LAST)
        back = term if back is None else back + term
    part_ref[...] = back.astype(BF)
    xhat, _ = norm_parts(x_ref[...].astype(F32))
    sums_ref[0:1, :] = jnp.sum(back * xhat, axis=0, keepdims=True)
    sums_ref[1:2, :] = jnp.sum(back, axis=0, keepdims=True)


def place_offset(i):
    return i // WSIDE * (2 * WSIDE - 1) + i % WSIDE


def offset_picks():
    row = lax.broadcasted_iota(jnp.int32, (2 * LANES, 2 * SLOT), 0)
    col = lax.broadcasted_iota(jnp.int32, (2 * LANES, 2 * SLOT), 1)
    j = col & (SLOT - 1)
    line = (j * 37) >> 8
    offset = place_offset(WIN - 1) - line * (2 * WSIDE - 1) - (j - line * WSIDE)
    hit = ((row & (LANES - 1)) == offset) & ((row >> 7) == (col >> 6)) & (j < WIN)
    return jnp.where(hit, 1.0, 0.0).astype(BF)


def position_kernel(table_ref, pos_ref, table_s, rows_s):
    heads = table_ref.shape[0]
    table_s[...] = jnp.zeros(table_s.shape, F32)
    table_s[0:heads, 0:REL] = table_ref[...]
    table = table_s[...]
    lines = table.shape[0]
    rows_s[WIN * lines :, :] = jnp.zeros((rows_s.shape[0] - WIN * lines, LANES), F32)
    for i in range(WIN):
        turned = pltpu.roll(table, (2 * LANES - place_offset(i)) % (2 * LANES), 1)
        rows_s[i * lines : (i + 1) * lines, :] = turned[:, :LANES]
    picks = offset_picks()
    for pair in range(pos_ref.shape[0] * 2):
        pieces = [rows_s[pl.ds(2 * pair + k, SLOT, stride=lines), :] for k in range(2)]
        rest = jnp.concatenate(pieces, axis=1)
        total = jnp.zeros((SLOT, 2 * SLOT), F32)
        for _ in range(3):
            top = rest.astype(BF)
            total = total + mm(top, picks)
            rest = rest - top.astype(F32)
        pos_ref[pair // 2, :, pair % 2 * LANES : (pair % 2 + 1) * LANES] = total


def attn_weights_kernel(count, split, me_ref, sums2_ref, gb1_ref, *refs):
    blocks, refs = [refs[7 * b : 7 * b + 7] for b in range(count)], refs[7 * count :]
    *outs, small_ref = refs[:3]
    gw_ref, gproj_ref, rows_s, out_sems = refs[3:]
    gproj, gqv, gpos, sums = 0.0, 0.0, 0.0, 0.0
    for _, mixed_ref, branch_ref, _, gqv_ref, gpos_ref, sums_ref in blocks:
        gproj = gproj + mm(mixed_ref[...], branch_ref[...], ROWS_ROWS)
        gqv, gpos, sums = gqv + gqv_ref[...], gpos + gpos_ref[...], sums + sums_ref[...]
    width, features = gproj.shape
    gproj_ref[...] = gproj.astype(BF)
    hidden = gb1_ref.shape[1]
    lines = [sums[k : k + 1] for k in range(2)] + [sums2_ref[k : k + 1, :] for k in range(4)]
    lines.append(gqv)
    lines += [gb1_ref[:, k : min(k + features, hidden)] for k in range(0, hidden, features)]
    small = jnp.concatenate(
        [jnp.concatenate([line, jnp.zeros((1, features - line.shape[1]), F32)], axis=1) if line.shape[1] < features else line
         for line in lines] + [jnp.zeros((12 - len(lines), features), F32)], axis=0)
    picks = offset_picks()
    for pair in range(gpos.shape[0] * 2):
        rest = gpos[pair // 2][:, pair % 2 * LANES : (pair % 2 + 1) * LANES]
        total = jnp.zeros((SLOT, 2 * LANES), F32)
        for _ in range(2):
            top = rest.astype(BF)
            total = total + mm(top, picks, LAST_LAST)
            rest = rest - top.astype(F32)
        for k in range(2):
            rows_s[pl.ds(2 * pair + k, SLOT, stride=16), :] = total[:, k * LANES : (k + 1) * LANES]
    for h in range(gpos.shape[0] * 4, 16):
        rows_s[pl.ds(h, SLOT, stride=16), :] = jnp.zeros((SLOT, LANES), F32)
    table = jnp.zeros((16, 2 * LANES), F32)
    for i in range(WIN):
        row = jnp.concatenate([rows_s[i * 16 : (i + 1) * 16, :], jnp.zeros((16, LANES), F32)], axis=1)
        table = table + (pltpu.roll(row, place_offset(i), 1) if i else row)
    packed = [jnp.concatenate([table[3 * r + k : 3 * r + k + 1] for k in range(3)], axis=1) for r in range(4)]
    small_ref[...] = jnp.concatenate([small] + packed, axis=0).astype(BF)
    sent = []

    def send(k, source, target):
        sent.append(pltpu.make_async_copy(source, target, out_sems.at[k]))
        sent[-1].start()

    if split:
        for i, (target, y_rel, z_rel, c, y, z) in enumerate(each_block(me_ref[0], *outs)):
            send(i, gproj_ref.at[ds((c * 4 + y * 2 + (z >> 1)) * 48, 48), ds((z & 1) * 384, 384)],
                 target.at[y_rel, z_rel, 48:96, 384:768])
    else:
        send(0, gproj_ref, outs[1])
    for part in range(3):
        gw = 0.0
        for normed_t_ref, _, _, grads_ref, _, _, _ in blocks:
            gw = gw + mm(normed_t_ref[...], grads_ref[part])
        gw_ref[part] = gw.astype(BF)
        if split:
            for i, (target, y_rel, z_rel, c, y, z) in enumerate(each_block(me_ref[0], *outs)):
                send(16 * (part + 1) + i, gw_ref.at[part, ds(c * 384 + y * 192 + z * 48, 48), :],
                     target.at[y_rel, z_rel, part // 2 * 48 : part // 2 * 48 + 48, part % 2 * 384 : part % 2 * 384 + 384])
        else:
            send(1 + part, gw_ref.at[part], outs[0].at[part])
    finish_all(sent)


def input_back_kernel(own_ref, peer_ref, x_ref, gain_ref, gmiddle_ref, gpatch_ref):
    gnorm = own_ref[...].astype(F32) + peer_ref[...].astype(F32)
    xhat, inv = norm_parts(x_ref[...].astype(F32))
    gpatch_ref[...] = (gmiddle_ref[...] + norm_back(xhat, inv, line(gain_ref), gnorm)).astype(BF)


def finish_kernel(me_ref, *refs):
    sources, outs, held, wide, (in_sems, out_sems) = refs[:4], refs[4:6], refs[6:10], refs[10:12], refs[12:]
    copies = begin(in_sems, *zip(sources, held))
    sent = []

    def put(value, k, where):
        wide[k][where] = value.astype(F32)
        sent.append(pltpu.make_async_copy(wide[k].at[where], outs[k].at[where], out_sems.at[len(sent)]))
        sent[-1].start()

    for source, y_rel, z_rel, c, y, z in each_block(me_ref[0], (0, 1), (2, 3)):
        source = source[y_rel]
        if z_rel == 0:
            copies[source].wait()
        piece = held[source].at[z_rel]
        lines = ds(c * 384 + y * 192 + z * 48, 48)
        put(piece[0:48, 0:384], 0, (0, lines, slice(None)))
        put(piece[0:48, 384:768], 0, (1, lines, slice(None)))
        put(piece[48:96, 0:384], 0, (2, lines, slice(None)))
        put(piece[48:96, 384:768], 1, (ds((c * 4 + y * 2 + (z >> 1)) * 48, 48), ds((z & 1) * 384, 384)))
    finish_all(sent)


def finish_mlp_kernel(me_ref, *refs):
    sources, (g1_out, g2_out, small_ref), held, (g1_ref, g2_ref, small_s, in_sems, out_sems) = (
        refs[:4], refs[4:7], refs[7:11], refs[11:])
    copies = begin(in_sems, *zip(sources, held))
    sent = []

    def put(value, k, wide, out, where):
        wide[where] = value.astype(F32)
        sent.append(pltpu.make_async_copy(wide.at[where], out.at[where], out_sems.at[k, len(sent) // 2]))
        sent[-1].start()

    for source, y_rel, z_rel, c, y, z in each_block(me_ref[0], (0, 1), (2, 3)):
        source = source[y_rel]
        if z_rel == 0:
            copies[source].wait()
        piece = held[source].at[z_rel]
        put(piece[0:BLOCK, :], 0, g1_ref, g1_out, (ds(y * 384 + z * 96, 96), ds(c * 768, 768)))
        put(piece[BLOCK : 2 * BLOCK, :], 1, g2_ref, g2_out, (ds(c * 768 + y * 384 + z * 96, 96), slice(None)))
        small_s[z * 4 + y * 2 + c] = piece[2 * BLOCK :, :].astype(F32)
    total = small_s[0]
    for d in range(1, 16):
        total = total + small_s[d]
    small_ref[...] = total
    finish_all(sent)


def shape_of(*dims, dtype=F32):
    return jax.ShapeDtypeStruct(dims, dtype)


def call(kernel, outs, scratch, name, flops, smem, *args, far=(), far_outs=(), limit=VMEM_LIMIT):
    space = lambda is_far: pl.BlockSpec(memory_space=pltpu.HBM if is_far else pltpu.VMEM)
    in_specs = [pl.BlockSpec(memory_space=pltpu.SMEM)] * len(smem) + [space(i in far) for i in range(len(args))]
    return pl.pallas_call(
        kernel,
        out_shape=outs,
        in_specs=in_specs,
        out_specs=[space(i in far_outs) for i in range(len(outs))],
        scratch_shapes=scratch,
        compiler_params=pltpu.CompilerParams(vmem_limit_bytes=limit),
        cost_estimate=pl.CostEstimate(flops=flops, bytes_accessed=flops // 256, transcendentals=0),
        name=name,
    )(*smem, *args)


def like(*arrays):
    return [pltpu.VMEM(a.shape, a.dtype) for a in arrays]


def dma(*counts):
    return [pltpu.SemaphoreType.DMA(c if isinstance(c, tuple) else (c,)) for c in counts]


SMALL = 1000000


def position(table):
    heads = table.shape[0]
    groups = -(-heads // GROUP)
    return call(position_kernel, [shape_of(groups, SLOT, GROUP * SLOT)],
                [pltpu.VMEM((16, 2 * LANES), F32), pltpu.VMEM((16 * SLOT, LANES), F32)], "position", SMALL, (), table)[0]


def attn_forward(windows, x, ln1, qkv, qv_bias, pos, mask):
    rows, features = x.shape
    width = qkv.shape[2]
    groups = width // LANES
    tile = shape_of(windows, SLOT, width, dtype=BF)
    outs = [shape_of(windows, groups, SLOT, GROUP * SLOT, dtype=BF), tile, tile, tile, shape_of(rows, width, dtype=BF),
            shape_of(features, rows, dtype=BF)]
    scratch = [pltpu.VMEM((windows, GROUP * SLOT), F32)] + [pltpu.VMEM((groups, SLOT * windows, LANES), F32)] * 4
    scratch += like(x, qkv) + dma(4)
    return call(functools.partial(attn_forward_kernel, windows), outs, scratch, "attn_forward", SMALL, (),
                x, *ln1, qkv, qv_bias, pos, mask, far=(0, 3), limit=ALL_VMEM)


def middle_norm(x, own, peer, bias, ln2):
    rows, features = x.shape
    return call(middle_kernel, [shape_of(rows, features), shape_of(rows, features, dtype=BF)], [], "middle", SMALL, (),
                x, own, peer, bias, *ln2, limit=ALL_VMEM)


def mlp(nm, cot, fc1, fc1_bias, fc2):
    rows, features = nm.shape
    hidden = fc2.shape[0]
    outs = [shape_of(rows, hidden, dtype=BF)] * 2 + [shape_of(rows, features, dtype=BF)] * 2
    return call(mlp_kernel, outs, [], "mlp", SMALL, (), nm, cot, fc1, fc1_bias, fc2)


def mlp_weights(split, me, blocks):
    rows, features = blocks[0][0].shape
    hidden = blocks[0][2].shape[1]
    grads = [shape_of(features, hidden, dtype=BF), shape_of(hidden, features, dtype=BF)]
    outs = [shape_of(1, hidden)] + ([shape_of(2, 4, BLOCK, features, dtype=BF)] * 4 if split else grads)
    flat = [a for b in blocks for a in b]
    scratch = like(*flat) + [pltpu.VMEM((features, rows), BF)] * len(blocks) + like(*grads) + dma(len(flat), 32)
    return call(functools.partial(mlp_weights_kernel, len(blocks), split), outs, scratch, "mlp_weights", SMALL,
                (me,), *flat, far=range(len(flat)), far_outs=range(1, len(outs)), limit=ALL_VMEM)


def middle_back(own, peer, middle, cot, gain):
    rows, features = middle.shape
    return call(
        middle_back_kernel, [shape_of(rows, features), shape_of(rows, features, dtype=BF), shape_of(4, features)], [],
        "middle_back", 20000 * SMALL, (), own, peer, middle, cot, gain)


def attn_backward(windows, branch, x, kept, qkv, proj):
    rows, features = branch.shape
    width = proj.shape[0]
    groups = width // LANES
    outs = [shape_of(3, rows, width, dtype=BF), shape_of(1, 2 * width), shape_of(groups, SLOT, GROUP * SLOT),
            shape_of(rows, features, dtype=BF), shape_of(2, features)]
    scratch = [pltpu.VMEM((groups, SLOT * windows, LANES), F32)] * 4
    return call(functools.partial(attn_backward_kernel, windows), outs, scratch, "attn_backward", SMALL, (),
                branch, x, *kept, qkv, proj)


def attn_weights(split, me, sums2, gb1, blocks):
    features = blocks[0][0].shape[0]
    width = blocks[0][1].shape[1]
    grads = [shape_of(3, features, width, dtype=BF), shape_of(width, features, dtype=BF)]
    outs = ([shape_of(2, 4, BLOCK, features, dtype=BF)] * 2 if split else grads) + [shape_of(16, features, dtype=BF)]
    scratch = like(*grads) + [pltpu.VMEM((16 * SLOT, LANES), F32)]
    flat = [a for b in blocks for a in b]
    return call(functools.partial(attn_weights_kernel, len(blocks), split), outs, scratch + dma(64),
                "attn_weights", SMALL, (me,), sums2, gb1, *flat, far_outs=(0, 1))


def input_back(own, peer, x, gain, gmiddle):
    rows, features = x.shape
    return call(input_back_kernel, [shape_of(rows, features, dtype=BF)], [], "input_back", SMALL, (),
                own, peer, x, gain, gmiddle)[0]


def finish(me, sources, *outs):
    scratch = like(*sources, *outs) + dma(4, 16 * 4)
    return call(finish_kernel, list(outs), scratch, "finish", SMALL, (me,), *sources, far=range(4), far_outs=range(len(outs)))


def finish_mlp(me, sources):
    features = sources[0].shape[2]
    outs = [shape_of(features, 2 * features), shape_of(2 * features, features), shape_of(16, features)]
    scratch = like(*sources, *outs[:2]) + [pltpu.VMEM((16, 16, features), F32)] + dma(4, (2, 16))
    return call(finish_mlp_kernel, outs, scratch, "finish_mlp", SMALL, (me,), *sources, far=range(4), far_outs=(0, 1))


def across(v):
    return lax.ppermute(v, "mp", [(0, 1), (1, 0)])


def flip(v, bits):
    return lax.ppermute(v, "dp", [(i, i ^ bits) for i in range(16)])


def after(v, *others):
    return lax.optimization_barrier((v, *others))[0]


def total_of(terms):
    total = terms[0].astype(F32)
    for t in terms[1:]:
        total = total + t.astype(F32)
    return total.astype(BF)


def side_send(keep, got):
    return total_of([keep[1], got[1]])


def line_sends(keep, got, side):
    return [total_of([keep[0, k], got[0, k], side[k]]) for k in (1, 2, 3)]


def own_piece(keep, got, side, line):
    return total_of([keep[0, 0], got[0, 0], side[0], *line])


def flip_line(pieces):
    return [flip(p, LINE * k) for k, p in zip((1, 2, 3), pieces)]


def shards(
    dp_size,
    mp_size,
    patches,
    token_valid,
    ln1_gain,
    ln1_shift,
    qkv_weight,
    qv_bias,
    bias_table,
    proj_weight,
    proj_bias,
    ln2_gain,
    ln2_shift,
    fc1_weight,
    fc1_bias,
    fc2_weight,
    fc2_bias,
    cotangent,
):
    windows, _, features = patches.shape
    rows = windows * WIN
    width = proj_weight.shape[0]
    heads = width // HEAD
    fast = mp_size == 2 and dp_size == 16 and features == 768
    x = patches.transpose(1, 0, 2).reshape(rows, features)
    cot = cotangent.transpose(1, 0, 2).reshape(rows, features)
    row = lambda a: a.reshape(1, -1)
    extra = -width % LANES
    qkv = jnp.pad(qkv_weight.transpose(1, 0, 2), ((0, 0), (0, 0), (0, extra)))
    proj = jnp.pad(proj_weight, ((0, extra), (0, 0)))
    pos = position(bias_table.T)
    bias = jnp.pad(qv_bias, ((0, 0), (0, extra)))
    valid = token_valid.astype(F32)
    ln1, ln2 = (ln1_gain, ln1_shift), (ln2_gain, ln2_shift)

    def blocks_of(v):
        return [v, across(v)] if fast else list(lax.all_gather(v, "mp"))

    def own_sums(parts):
        if fast:
            return parts[0], across(parts[1])
        own = lax.psum_scatter(jnp.concatenate(parts), "mp", scatter_dimension=0, tiled=True)
        return own, jnp.zeros_like(own)

    index = lax.axis_index("dp").astype(jnp.int32)
    me = index.reshape(1)
    valids = blocks_of(valid)
    kept, xs = [], []
    for x_b, valid_b in zip(blocks_of(x), valids):
        if kept:
            x_b = after(x_b, kept[0][4])
            if fast:
                core = index & 1
                half = across(lax.dynamic_slice_in_dim(proj, core * (width // 2), width // 2, 0))
        xs.append(x_b)
        kept.append(attn_forward(windows, x_b, ln1, qkv, bias, pos, valid_b))
    project = lambda mixed, weight: jnp.dot(mixed, weight, preferred_element_type=F32).astype(BF)
    if fast:
        cots = [cot, across(after(cot, kept[0][4], valids[1], half))]
        mixed = across(after(kept[1][4], cots[1]))
        half = after(half, kept[1][4])
        rest = flip(half, CORE)
        other = jnp.where(core == 0, jnp.concatenate([half, rest]), jnp.concatenate([rest, half]))
        parts = project(kept[0][4], proj), project(mixed, other)
    else:
        parts = own_sums([project(k[4], proj) for k in kept])
        cots = blocks_of(cot)
    middle, nm = middle_norm(x, *parts, proj_bias, ln2)

    blocks, outs, gmids = [], [], []
    for nm_b, cot_b in zip(blocks_of(nm), cots):
        if blocks:
            nm_b = after(nm_b, gmids[-1])
        hid, gpre, out_b, gmid_b = mlp(nm_b, cot_b, fc1_weight, row(fc1_bias), fc2_weight)
        blocks.append((nm_b, cot_b, hid, gpre))
        outs.append(out_b)
        gmids.append(gmid_b)
    gmid_own, gmid_peer = own_sums(gmids)
    gb1, *g_mlp = mlp_weights(fast, me, blocks)
    outs = own_sums(outs)
    gmid_peer = after(gmid_peer, gb1)
    gmiddle, branch, sums2 = middle_back(gmid_own, gmid_peer, middle, cot, ln2[0])
    branches = blocks_of(branch)
    if fast:
        keep1, send1, keep2, send2 = g_mlp
        got1, got2 = after(flip(send1, CORE), branch), after(flip(send2, CORE), branch)
        side1, side2 = side_send(keep1, got1), side_send(keep2, got2)
        branches[0] = after(branches[0], side1, side2)
    backs, gparts = [], []
    for b, kept_b in enumerate(kept):
        if b == 1 and fast:
            side1 = after(flip(side1, SIDE), gparts[0])
            line1 = line_sends(keep1, got1, side1)
            branches[1] = after(branches[1], *line1, gparts[0])
        *back, gpart, gsum = attn_backward(windows, branches[b], xs[b], kept_b[:4], qkv, proj)
        backs.append((*back, gsum))
        gparts.append(gpart)
    if fast:
        side2 = after(flip(side2, SIDE), gparts[1])
        line2 = line_sends(keep2, got2, side2)
        line1 = [after(r, gparts[1]) for r in flip_line(line1)]
        piece1 = own_piece(keep1, got1, side1, line1)
        branches[0] = after(branches[0], piece1, *line2, outs[1])
    *g_attn, small = attn_weights(
        fast, me, sums2, gb1, [(k[5], k[4], br, *back) for k, br, back in zip(kept, branches, backs)])
    gnorms = own_sums(gparts)
    gpatch = input_back(*gnorms, x, ln1[0], gmiddle)
    output = (middle + outs[0].astype(F32) + outs[1].astype(F32) + row(fc2_bias)).astype(BF)

    if fast:
        line2 = [after(r, small) for r in flip_line(line2)]
        piece2 = own_piece(keep2, got2, side2, line2)
        keep, send = g_attn
        got = flip(after(send, piece2), CORE)
        side = flip(side_send(keep, got), SIDE)
        fc = jnp.concatenate([piece1, piece2, small], axis=0)
        fc_quad = jnp.stack([fc] + flip_line([fc] * 3))
        side = after(side, fc_quad, output)
        line = [after(r, gpatch) for r in flip_line(line_sends(keep, got, side))]
        piece = own_piece(keep, got, side, line)
        quad = jnp.stack([piece] + flip_line([piece] * 3))
        fc_pair = after(flip(fc_quad, SIDE), quad)
        g_fc1, g_fc2, small = finish_mlp(me, (fc_quad, fc_pair, after(flip(fc_quad, CORE), quad), after(flip(fc_pair, CORE), quad)))
        pair = flip(quad, SIDE)
        gw, gproj = finish(me, (quad, pair, flip(quad, CORE), after(flip(pair, CORE), small)),
                           shape_of(3, features, width), shape_of(width, features))
        totals = small[0:6] + across(small[0:6])
    else:
        g_fc1, g_fc2, gw, gproj = [g.astype(F32) for g in lax.psum((*g_mlp, *g_attn), "dp")]
        gw, gproj = gw[:, :, :width], gproj[:width]
        small = lax.psum(small, "dp").astype(F32)
        totals = lax.psum(small[0:6], "mp")
    padded = width + extra
    gqv = jnp.stack([small[6, :width], small[6, padded : padded + width]])
    gb1 = small[7:12].reshape(-1)[: gb1.size]
    gt = small[12:].reshape(12, 2 * LANES)[:heads, :REL].T

    unrow = lambda a: a.reshape(WIN, windows, features).transpose(1, 0, 2)
    return (
        unrow(output),
        unrow(gpatch),
        totals[0],
        totals[1],
        gw.transpose(1, 0, 2),
        gqv,
        gt,
        gproj,
        totals[4],
        totals[2],
        totals[3],
        g_fc1,
        gb1,
        g_fc2,
        totals[5],
    )


def solution(mesh):
    placed = (
        P(("dp", "mp"), None, None),
        P(("dp", "mp"), None),
        P(),
        P(),
        P(None, None, "mp"),
        P(None, "mp"),
        P(None, "mp"),
        P("mp", None),
        P(),
        P(),
        P(),
        P(None, "mp"),
        P("mp"),
        P("mp", None),
        P(),
        P(("dp", "mp"), None, None),
    )
    return jax.shard_map(
        functools.partial(shards, mesh.shape["dp"], mesh.shape["mp"]),
        mesh=mesh,
        in_specs=placed,
        out_specs=(
            P(("dp", "mp"), None, None),
            P(("dp", "mp"), None, None),
            P(),
            P(),
            P(None, None, "mp"),
            P(None, "mp"),
            P(None, "mp"),
            P("mp", None),
            P(),
            P(),
            P(),
            P(None, "mp"),
            P("mp"),
            P("mp", None),
            P(),
        ),
        check_vma=False,
    )
```

```python
import functools

import jax
import jax.numpy as jnp
from jax import lax
from jax.experimental import pallas as pl
from jax.experimental.pallas import tpu as pltpu
from jax.sharding import PartitionSpec as P

HEAD = 32
WSIDE = 7
WIN = 49
REL = 169
SLOT = 64
GROUP = 4
LANES = 128
EPS = 1e-05
SCALING = HEAD ** (-0.5)
BF = jnp.bfloat16
F32 = jnp.float32
HIGH = lax.Precision.HIGHEST
VMEM_LIMIT = 28 * 1024 * 1024
ALL_VMEM = 58 * 1024 * 1024
BLOCK = 96
CORE, SIDE, LINE = 1, 2, 4

ROW_COL = (((1,), (0,)), ((), ()))
LAST_LAST = (((1,), (1,)), ((), ()))
ROWS_ROWS = (((0,), (0,)), ((), ()))


def mm(a, b, dims=ROW_COL):
    return lax.dot_general(a, b, dims, preferred_element_type=F32)


def norm_parts(rows):
    mean = jnp.mean(rows, axis=-1, keepdims=True)
    centred = rows - mean
    variance = jnp.mean(centred * centred, axis=-1, keepdims=True)
    inv = lax.rsqrt(variance + EPS)
    return centred * inv, inv


def norm_back(xhat, inv, gain, upstream):
    z = upstream * gain
    mean_z = jnp.mean(z, axis=-1, keepdims=True)
    mean_zx = jnp.mean(z * xhat, axis=-1, keepdims=True)
    return (z - mean_z - xhat * mean_zx) * inv


def head_masks():
    lane = lax.broadcasted_iota(jnp.int32, (SLOT, LANES), 1)
    return [jnp.where((lane >> 5) == h, 1.0, 0.0).astype(BF) for h in range(GROUP)]


def block_ones():
    row = lax.broadcasted_iota(jnp.int32, (GROUP * SLOT, GROUP * SLOT), 0)
    col = lax.broadcasted_iota(jnp.int32, (GROUP * SLOT, GROUP * SLOT), 1)
    return jnp.where((row >> 6) == (col >> 6), 1.0, 0.0).astype(BF)


def spread(tile, masks):
    return jnp.concatenate([tile * m for m in masks], axis=0)


def collect(full, masks_f):
    total = full[0:SLOT] * masks_f[0]
    for h in range(1, GROUP):
        total = total + full[h * SLOT : (h + 1) * SLOT] * masks_f[h]
    return total


def fill(scratch, rows, windows):
    pitch = windows + 1
    for g in range(scratch.shape[0]):
        for place in range(WIN):
            scratch[g, place * pitch : place * pitch + windows, :] = rows[
                place * windows : (place + 1) * windows, g * LANES : (g + 1) * LANES]
        scratch[g, WIN * pitch :, :] = jnp.zeros((scratch.shape[1] - WIN * pitch, LANES), rows.dtype)


def empty(scratch, windows):
    pitch = windows + 1
    planes = [
        jnp.concatenate([scratch[g, place * pitch : place * pitch + windows, :] for place in range(WIN)], axis=0)
        for g in range(scratch.shape[0])
    ]
    return jnp.concatenate(planes, axis=1).astype(BF)


def row_max(tile, low_half):
    low = jnp.max(jnp.where(low_half, tile, -3e38), axis=-1, keepdims=True)
    high = jnp.max(jnp.where(low_half, -3e38, tile), axis=-1, keepdims=True)
    return jnp.where(low_half, low, high)


def ds(start, size):
    unit = 384 if size % 384 == 0 else 48
    return pl.ds(pl.multiple_of(start, unit), size)


def each_block(me, *by_core):
    for c_rel, target in enumerate(by_core):
        for y_rel in range(2):
            for z_rel in range(4):
                yield target, y_rel, z_rel, (me & 1) ^ c_rel, ((me >> 1) & 1) ^ y_rel, (me >> 2) ^ z_rel


def line(ref):
    return ref[...].reshape(1, -1)


def begin(sems, *pairs):
    copies = [pltpu.make_async_copy(a, b, sems.at[i]) for i, (a, b) in enumerate(pairs)]
    for copy in copies:
        copy.start()
    return copies


def finish_all(copies):
    for copy in copies:
        copy.wait()


def attn_forward_kernel(windows, x_in, gain_ref, shift_ref, w_in, bias_ref, pos_ref, valid_ref,
                        prob_ref, q_ref, k_ref, v_ref, mixed_ref, normed_t_ref,
                        mask_s, q_s, k_s, v_s, mixed_s, x_ref, w_ref, in_sems):
    copies = begin(in_sems, (x_in, x_ref), *[(w_in.at[p], w_ref.at[p]) for p in range(3)])
    mask_s[...] = jnp.zeros(mask_s.shape, F32)
    for h in range(GROUP):
        mask_s[:, h * SLOT : h * SLOT + WIN] = valid_ref[...].astype(F32)
    masks = head_masks()
    ones = block_ones()
    low_half = lax.broadcasted_iota(jnp.int32, (SLOT, LANES), 1) < SLOT
    copies[0].wait()
    x = x_ref[...].astype(F32)
    rows = x.shape[0]
    groups = q_s.shape[0]
    xhat, _ = norm_parts(x)
    normed = (xhat * line(gain_ref) + line(shift_ref)).astype(BF)
    normed_t_ref[...] = normed.T
    for part, scratch in enumerate((q_s, k_s, v_s)):
        copies[1 + part].wait()
        got = mm(normed, w_ref[part])
        if part != 1:
            got = got + bias_ref[part // 2 : part // 2 + 1, :]
        fill(scratch, got.astype(BF).astype(F32), windows)

    def window(w, carry):
        allowed = jnp.broadcast_to(mask_s[pl.ds(w, 1), :], (SLOT, GROUP * SLOT)) > 0.5
        for g in range(groups):
            cols = slice(g * LANES, (g + 1) * LANES)
            places = pl.ds(w, SLOT, stride=windows + 1)
            q = q_s[g, places, :].astype(BF)
            k = k_s[g, places, :].astype(BF)
            v = v_s[g, places, :].astype(BF)
            q_ref[w, :, cols] = q
            k_ref[w, :, cols] = k
            v_ref[w, :, cols] = v
            scores = mm(q, spread(k, masks), LAST_LAST) * SCALING + pos_ref[g]
            scores = jnp.where(allowed, scores, -1000000000.0)
            top = jnp.concatenate([row_max(scores[:, :LANES], low_half), row_max(scores[:, LANES:], low_half)], axis=1)
            e = jnp.exp(scores - top)
            total = mm(e.astype(BF), ones)
            prob = (e / total).astype(BF)
            prob_ref[w, g] = prob
            mixed_s[g, places, :] = mm(prob, spread(v, masks))
        return carry

    lax.fori_loop(0, windows, window, 0, unroll=2)
    mixed_ref[...] = empty(mixed_s, windows)


def middle_kernel(heads, me_ref, x_in, own_in, peer_in, bias_ref, gain_ref, shift_ref, *refs):
    if heads:
        half_in, rest_in, middle_ref, nm_ref, x_ref, own_ref, peer_ref, proj_ref, sems = refs
        lines = half_in.shape[0]
        core = me_ref[0] & 1
        place = lambda c: proj_ref.at[pl.ds(pl.multiple_of(c * lines, lines), lines), :]
        copies = begin(sems, (peer_in, peer_ref), (half_in, place(core)), (rest_in, place(1 - core)), (x_in, x_ref),
                       (own_in, own_ref))
        finish_all(copies[:3])
        peer = mm(peer_ref[...], proj_ref[...])
        finish_all(copies[3:])
    else:
        middle_ref, nm_ref, x_ref, own_ref, peer_ref, sems = refs
        finish_all(begin(sems, (x_in, x_ref), (own_in, own_ref), (peer_in, peer_ref)))
        peer = peer_ref[...].astype(F32)
    middle = x_ref[...].astype(F32) + (own_ref[...].astype(F32) + peer) + line(bias_ref)
    middle_ref[...] = middle
    xhat, _ = norm_parts(middle)
    nm_ref[...] = (xhat * line(gain_ref) + line(shift_ref)).astype(BF)


def mlp_kernel(nm_ref, cot_ref, fc1_ref, b1_ref, fc2_ref, hid_ref, gpre_ref, out_ref, gmid_ref):
    hidden_size = fc1_ref.shape[1]
    features = fc1_ref.shape[0]
    step = 256 if hidden_size % 256 == 0 else 128
    count = hidden_size // step

    nm = nm_ref[...]
    cot = cot_ref[...]

    def units(c, carry):
        cols = pl.ds(pl.multiple_of(c * step, step), step)
        pre = mm(nm, fc1_ref[:, cols]) + b1_ref[:, cols]
        phi = 0.5 * (1.0 + lax.erf(pre * (0.5 ** 0.5)))
        hid_ref[:, cols] = (pre * phi).astype(BF)
        slope = phi + pre * (jnp.exp(-0.5 * pre * pre) * 0.3989422804014327)
        gpre_ref[:, cols] = (mm(cot, fc2_ref[cols, :], LAST_LAST) * slope).astype(BF)
        return carry

    lax.fori_loop(0, count, units, 0)

    def tile(c, carry):
        cols = pl.ds(pl.multiple_of(c * 256, 256), 256)
        gmid_ref[:, cols] = mm(gpre_ref[...], fc1_ref[cols, :], LAST_LAST).astype(BF)
        out_ref[:, cols] = mm(hid_ref[...], fc2_ref[:, cols]).astype(BF)
        return carry

    lax.fori_loop(0, features // 256, tile, 0)

def mlp_weights_kernel(count, split, me_ref, *refs):
    inputs, refs = refs[: 4 * count], refs[4 * count :]
    n_out = 5 if split else 3
    gb1_ref, *outs = refs[:n_out]
    held = refs[n_out : n_out + 4 * count]
    nts = refs[n_out + 4 * count : n_out + 5 * count]
    g1_ref, g2_ref, in_sems, out_sems = refs[n_out + 5 * count :]
    order = [4 * b + k for k in (0, 2, 1, 3) for b in range(count)]
    copies = dict(zip(order, begin(in_sems, *[(inputs[i], held[i]) for i in order])))
    blocks = [held[4 * b : 4 * b + 4] for b in range(count)]
    hidden_size = g1_ref.shape[1]
    features = g1_ref.shape[0]
    step = 384 if hidden_size % 384 == 0 else 128
    wide = features if hidden_size % features == 0 else step
    finish_all([copies[4 * b] for b in range(count)])
    for block, nt in zip(blocks, nts):
        nt[...] = block[0][...].T
    finish_all([copies[4 * b + k] for k in (2, 1) for b in range(count)])

    def second(j, carry):
        cols = ds(j * step, step)
        g2_ref[cols, :] = sum(mm(hid_ref[:, cols], cot_ref[...], ROWS_ROWS) for _, cot_ref, hid_ref, _ in blocks).astype(BF)
        return carry

    def first(j, carry):
        cols = ds(j * wide, wide)
        g1_ref[:, cols] = sum(mm(nt[...], block[3][:, cols]) for nt, block in zip(nts, blocks)).astype(BF)
        return carry

    lax.fori_loop(0, hidden_size // step, second, 0)
    me = me_ref[0]
    sent = []

    def send(k, source, target):
        sent.append(pltpu.make_async_copy(source, target, out_sems.at[k]))
        sent[-1].start()

    if split:
        for i, (target, y_rel, z_rel, c, y, z) in enumerate(each_block(me, outs[2], outs[3])):
            send(i, g2_ref.at[ds(c * 768 + y * 384 + z * 96, 96), :], target.at[y_rel, z_rel])
    else:
        send(0, g2_ref, outs[1])
    finish_all([copies[4 * b + 3] for b in range(count)])
    gb1_ref[...] = sum(jnp.sum(block[3][...].astype(F32), axis=0, keepdims=True) for block in blocks)
    lax.fori_loop(0, hidden_size // wide, first, 0)
    if split:
        for i, (target, y_rel, z_rel, c, y, z) in enumerate(each_block(me, outs[0], outs[1])):
            send(16 + i, g1_ref.at[ds(y * 384 + z * 96, 96), ds(c * 768, 768)], target.at[y_rel, z_rel])
    else:
        send(1, g1_ref, outs[0])
    finish_all(sent)


def middle_back_kernel(own_ref, peer_ref, middle_ref, cot_ref, gain_ref, gmiddle_ref, branch_ref, sums_ref):
    upstream = cot_ref[...].astype(F32)
    xhat, inv = norm_parts(middle_ref[...])
    gmid = own_ref[...].astype(F32) + peer_ref[...].astype(F32)
    sums_ref[0:1, :] = jnp.sum(gmid * xhat, axis=0, keepdims=True)
    sums_ref[1:2, :] = jnp.sum(gmid, axis=0, keepdims=True)
    gmiddle = upstream + norm_back(xhat, inv, line(gain_ref), gmid)
    gmiddle_ref[...] = gmiddle
    branch_ref[...] = gmiddle.astype(BF)
    sums_ref[2:3, :] = jnp.sum(gmiddle, axis=0, keepdims=True)
    sums_ref[3:4, :] = jnp.sum(upstream, axis=0, keepdims=True)


def attn_backward_kernel(windows, branch_ref, x_ref, prob_ref, q_ref, k_ref, v_ref, w_ref, proj_ref,
                         grads_ref, gqv_ref, gpos_ref, part_ref, sums_ref, gm_s, gq_s, gk_s, gv_s):
    rows = branch_ref.shape[0]
    groups = gm_s.shape[0]
    gpos_ref[...] = jnp.zeros(gpos_ref.shape, F32)
    masks = head_masks()
    masks_f = [m.astype(F32) for m in masks]
    ones = block_ones()
    fill(gm_s, mm(branch_ref[...], proj_ref[...], LAST_LAST).astype(BF).astype(F32), windows)

    def window(w, carry):
        for g in range(groups):
            cols = slice(g * LANES, (g + 1) * LANES)
            places = pl.ds(w, SLOT, stride=windows + 1)
            gm = gm_s[g, places, :].astype(BF)
            q = q_ref[w, :, cols]
            k = k_ref[w, :, cols]
            v = v_ref[w, :, cols]
            prob = prob_ref[w, g]
            prob_f = prob.astype(F32)
            gprob = mm(gm, spread(v, masks), LAST_LAST)
            both = prob_f * gprob
            delta = mm(both.astype(BF), ones)
            gs = (both - prob_f * delta).astype(BF)
            gpos_ref[g] += gs.astype(F32)
            gq_s[g, places, :] = mm(gs, spread(k, masks)) * SCALING
            gk_s[g, places, :] = collect(mm(gs, q, ROWS_ROWS), masks_f) * SCALING
            gv_s[g, places, :] = collect(mm(prob, gm, ROWS_ROWS), masks_f)
        return carry

    lax.fori_loop(0, windows, window, 0, unroll=2)
    back = None
    for part, scratch in enumerate((gq_s, gk_s, gv_s)):
        grad = empty(scratch, windows)
        grads_ref[part] = grad
        if part != 1:
            width = grad.shape[1]
            lanes = slice(part // 2 * width, (part // 2 + 1) * width)
            gqv_ref[:, lanes] = jnp.sum(grad.astype(F32), axis=0, keepdims=True)
        term = mm(grad, w_ref[part], LAST_LAST)
        back = term if back is None else back + term
    part_ref[...] = back.astype(BF)
    xhat, _ = norm_parts(x_ref[...].astype(F32))
    sums_ref[0:1, :] = jnp.sum(back * xhat, axis=0, keepdims=True)
    sums_ref[1:2, :] = jnp.sum(back, axis=0, keepdims=True)


def place_offset(i):
    return i // WSIDE * (2 * WSIDE - 1) + i % WSIDE


def offset_picks():
    row = lax.broadcasted_iota(jnp.int32, (2 * LANES, 2 * SLOT), 0)
    col = lax.broadcasted_iota(jnp.int32, (2 * LANES, 2 * SLOT), 1)
    j = col & (SLOT - 1)
    line = (j * 37) >> 8
    offset = place_offset(WIN - 1) - line * (2 * WSIDE - 1) - (j - line * WSIDE)
    hit = ((row & (LANES - 1)) == offset) & ((row >> 7) == (col >> 6)) & (j < WIN)
    return jnp.where(hit, 1.0, 0.0).astype(BF)


def position_kernel(table_ref, pos_ref, table_s, rows_s):
    heads = table_ref.shape[0]
    table_s[...] = jnp.zeros(table_s.shape, F32)
    table_s[0:heads, 0:REL] = table_ref[...]
    table = table_s[...]
    lines = table.shape[0]
    rows_s[WIN * lines :, :] = jnp.zeros((rows_s.shape[0] - WIN * lines, LANES), F32)
    for i in range(WIN):
        turned = pltpu.roll(table, (2 * LANES - place_offset(i)) % (2 * LANES), 1)
        rows_s[i * lines : (i + 1) * lines, :] = turned[:, :LANES]
    picks = offset_picks()
    for pair in range(pos_ref.shape[0] * 2):
        pieces = [rows_s[pl.ds(2 * pair + k, SLOT, stride=lines), :] for k in range(2)]
        rest = jnp.concatenate(pieces, axis=1)
        total = jnp.zeros((SLOT, 2 * SLOT), F32)
        for _ in range(3):
            top = rest.astype(BF)
            total = total + mm(top, picks)
            rest = rest - top.astype(F32)
        pos_ref[pair // 2, :, pair % 2 * LANES : (pair % 2 + 1) * LANES] = total


def attn_weights_kernel(count, split, me_ref, sums2_ref, gb1_ref, *refs):
    blocks, refs = [refs[7 * b : 7 * b + 7] for b in range(count)], refs[7 * count :]
    *outs, small_ref = refs[:3]
    gw_ref, gproj_ref, rows_s, out_sems = refs[3:]
    gproj, gqv, gpos, sums = 0.0, 0.0, 0.0, 0.0
    for _, mixed_ref, branch_ref, _, gqv_ref, gpos_ref, sums_ref in blocks:
        gproj = gproj + mm(mixed_ref[...], branch_ref[...], ROWS_ROWS)
        gqv, gpos, sums = gqv + gqv_ref[...], gpos + gpos_ref[...], sums + sums_ref[...]
    width, features = gproj.shape
    gproj_ref[...] = gproj.astype(BF)
    hidden = gb1_ref.shape[1]
    lines = [sums[k : k + 1] for k in range(2)] + [sums2_ref[k : k + 1, :] for k in range(4)]
    lines.append(gqv)
    lines += [gb1_ref[:, k : min(k + features, hidden)] for k in range(0, hidden, features)]
    small = jnp.concatenate(
        [jnp.concatenate([line, jnp.zeros((1, features - line.shape[1]), F32)], axis=1) if line.shape[1] < features else line
         for line in lines] + [jnp.zeros((12 - len(lines), features), F32)], axis=0)
    picks = offset_picks()
    for pair in range(gpos.shape[0] * 2):
        rest = gpos[pair // 2][:, pair % 2 * LANES : (pair % 2 + 1) * LANES]
        total = jnp.zeros((SLOT, 2 * LANES), F32)
        for _ in range(2):
            top = rest.astype(BF)
            total = total + mm(top, picks, LAST_LAST)
            rest = rest - top.astype(F32)
        for k in range(2):
            rows_s[pl.ds(2 * pair + k, SLOT, stride=16), :] = total[:, k * LANES : (k + 1) * LANES]
    for h in range(gpos.shape[0] * 4, 16):
        rows_s[pl.ds(h, SLOT, stride=16), :] = jnp.zeros((SLOT, LANES), F32)
    table = jnp.zeros((16, 2 * LANES), F32)
    for i in range(WIN):
        row = jnp.concatenate([rows_s[i * 16 : (i + 1) * 16, :], jnp.zeros((16, LANES), F32)], axis=1)
        table = table + (pltpu.roll(row, place_offset(i), 1) if i else row)
    packed = [jnp.concatenate([table[3 * r + k : 3 * r + k + 1] for k in range(3)], axis=1) for r in range(4)]
    small_ref[...] = jnp.concatenate([small] + packed, axis=0).astype(BF)
    sent = []

    def send(k, source, target):
        sent.append(pltpu.make_async_copy(source, target, out_sems.at[k]))
        sent[-1].start()

    if split:
        for i, (target, y_rel, z_rel, c, y, z) in enumerate(each_block(me_ref[0], *outs)):
            send(i, gproj_ref.at[ds((c * 4 + y * 2 + (z >> 1)) * 48, 48), ds((z & 1) * 384, 384)],
                 target.at[y_rel, z_rel, 48:96, 384:768])
    else:
        send(0, gproj_ref, outs[1])
    for part in range(3):
        gw = 0.0
        for normed_t_ref, _, _, grads_ref, _, _, _ in blocks:
            gw = gw + mm(normed_t_ref[...], grads_ref[part])
        gw_ref[part] = gw.astype(BF)
        if split:
            for i, (target, y_rel, z_rel, c, y, z) in enumerate(each_block(me_ref[0], *outs)):
                send(16 * (part + 1) + i, gw_ref.at[part, ds(c * 384 + y * 192 + z * 48, 48), :],
                     target.at[y_rel, z_rel, part // 2 * 48 : part // 2 * 48 + 48, part % 2 * 384 : part % 2 * 384 + 384])
        else:
            send(1 + part, gw_ref.at[part], outs[0].at[part])
    finish_all(sent)


def input_back_kernel(own_ref, peer_ref, x_ref, gain_ref, gmiddle_ref, gpatch_ref):
    gnorm = own_ref[...].astype(F32) + peer_ref[...].astype(F32)
    xhat, inv = norm_parts(x_ref[...].astype(F32))
    gpatch_ref[...] = (gmiddle_ref[...] + norm_back(xhat, inv, line(gain_ref), gnorm)).astype(BF)


def finish_kernel(me_ref, *refs):
    sources, outs, held, wide, (in_sems, out_sems) = refs[:4], refs[4:6], refs[6:10], refs[10:12], refs[12:]
    copies = begin(in_sems, *zip(sources, held))
    sent = []

    def put(value, k, where):
        wide[k][where] = value.astype(F32)
        sent.append(pltpu.make_async_copy(wide[k].at[where], outs[k].at[where], out_sems.at[len(sent)]))
        sent[-1].start()

    for source, y_rel, z_rel, c, y, z in each_block(me_ref[0], (0, 1), (2, 3)):
        source = source[y_rel]
        if z_rel == 0:
            copies[source].wait()
        piece = held[source].at[z_rel]
        lines = ds(c * 384 + y * 192 + z * 48, 48)
        put(piece[0:48, 0:384], 0, (0, lines, slice(None)))
        put(piece[0:48, 384:768], 0, (1, lines, slice(None)))
        put(piece[48:96, 0:384], 0, (2, lines, slice(None)))
        put(piece[48:96, 384:768], 1, (ds((c * 4 + y * 2 + (z >> 1)) * 48, 48), ds((z & 1) * 384, 384)))
    finish_all(sent)


def finish_mlp_kernel(me_ref, *refs):
    sources, (g1_out, g2_out, small_ref), held, (g1_ref, g2_ref, small_s, in_sems, out_sems) = (
        refs[:4], refs[4:7], refs[7:11], refs[11:])
    copies = begin(in_sems, *zip(sources, held))
    sent = []

    def put(value, k, wide, out, where):
        wide[where] = value.astype(F32)
        sent.append(pltpu.make_async_copy(wide.at[where], out.at[where], out_sems.at[k, len(sent) // 2]))
        sent[-1].start()

    for source, y_rel, z_rel, c, y, z in each_block(me_ref[0], (0, 1), (2, 3)):
        source = source[y_rel]
        if z_rel == 0:
            copies[source].wait()
        piece = held[source].at[z_rel]
        put(piece[0:BLOCK, :], 0, g1_ref, g1_out, (ds(y * 384 + z * 96, 96), ds(c * 768, 768)))
        put(piece[BLOCK : 2 * BLOCK, :], 1, g2_ref, g2_out, (ds(c * 768 + y * 384 + z * 96, 96), slice(None)))
        small_s[z * 4 + y * 2 + c] = piece[2 * BLOCK :, :].astype(F32)
    total = small_s[0]
    for d in range(1, 16):
        total = total + small_s[d]
    small_ref[...] = total
    finish_all(sent)


def shape_of(*dims, dtype=F32):
    return jax.ShapeDtypeStruct(dims, dtype)


def call(kernel, outs, scratch, name, flops, smem, *args, far=(), far_outs=(), limit=VMEM_LIMIT):
    space = lambda is_far: pl.BlockSpec(memory_space=pltpu.HBM if is_far else pltpu.VMEM)
    in_specs = [pl.BlockSpec(memory_space=pltpu.SMEM)] * len(smem) + [space(i in far) for i in range(len(args))]
    return pl.pallas_call(
        kernel,
        out_shape=outs,
        in_specs=in_specs,
        out_specs=[space(i in far_outs) for i in range(len(outs))],
        scratch_shapes=scratch,
        compiler_params=pltpu.CompilerParams(vmem_limit_bytes=limit),
        cost_estimate=pl.CostEstimate(flops=flops, bytes_accessed=flops // 256, transcendentals=0),
        name=name,
    )(*smem, *args)


def like(*arrays):
    return [pltpu.VMEM(a.shape, a.dtype) for a in arrays]


def dma(*counts):
    return [pltpu.SemaphoreType.DMA(c if isinstance(c, tuple) else (c,)) for c in counts]


SMALL = 1000000


def position(table):
    heads = table.shape[0]
    groups = -(-heads // GROUP)
    return call(position_kernel, [shape_of(groups, SLOT, GROUP * SLOT)],
                [pltpu.VMEM((16, 2 * LANES), F32), pltpu.VMEM((16 * SLOT, LANES), F32)], "position", SMALL, (), table)[0]


def attn_forward(windows, x, ln1, qkv, qv_bias, pos, mask):
    rows, features = x.shape
    width = qkv.shape[2]
    groups = width // LANES
    tile = shape_of(windows, SLOT, width, dtype=BF)
    outs = [shape_of(windows, groups, SLOT, GROUP * SLOT, dtype=BF), tile, tile, tile, shape_of(rows, width, dtype=BF),
            shape_of(features, rows, dtype=BF)]
    scratch = [pltpu.VMEM((windows, GROUP * SLOT), F32)] + [pltpu.VMEM((groups, SLOT * (windows + 1), LANES), F32)] * 4
    scratch += like(x, qkv) + dma(4)
    return call(functools.partial(attn_forward_kernel, windows), outs, scratch, "attn_forward", SMALL, (),
                x, *ln1, qkv, qv_bias, pos, mask, far=(0, 3), limit=ALL_VMEM)


def middle_norm(me, x, own, peer, bias, ln2, halves):
    rows, features = x.shape
    scratch = like(x, own, peer)
    if halves:
        scratch += [pltpu.VMEM((2 * halves[0].shape[0], features), BF)]
    return call(functools.partial(middle_kernel, bool(halves)), [shape_of(rows, features), shape_of(rows, features, dtype=BF)],
                scratch + dma(5), "middle", SMALL, (me,), x, own, peer, bias, *ln2, *halves, far=(0, 1, 2, 6, 7),
                limit=ALL_VMEM)


def mlp(nm, cot, fc1, fc1_bias, fc2):
    rows, features = nm.shape
    hidden = fc2.shape[0]
    outs = [shape_of(rows, hidden, dtype=BF)] * 2 + [shape_of(rows, features, dtype=BF)] * 2
    return call(mlp_kernel, outs, [], "mlp", SMALL, (), nm, cot, fc1, fc1_bias, fc2)


def mlp_weights(split, me, blocks):
    rows, features = blocks[0][0].shape
    hidden = blocks[0][2].shape[1]
    grads = [shape_of(features, hidden, dtype=BF), shape_of(hidden, features, dtype=BF)]
    outs = [shape_of(1, hidden)] + ([shape_of(2, 4, BLOCK, features, dtype=BF)] * 4 if split else grads)
    flat = [a for b in blocks for a in b]
    scratch = like(*flat) + [pltpu.VMEM((features, rows), BF)] * len(blocks) + like(*grads) + dma(len(flat), 32)
    return call(functools.partial(mlp_weights_kernel, len(blocks), split), outs, scratch, "mlp_weights", SMALL,
                (me,), *flat, far=range(len(flat)), far_outs=range(1, len(outs)), limit=ALL_VMEM)


def middle_back(own, peer, middle, cot, gain):
    rows, features = middle.shape
    return call(
        middle_back_kernel, [shape_of(rows, features), shape_of(rows, features, dtype=BF), shape_of(4, features)], [],
        "middle_back", 20000 * SMALL, (), own, peer, middle, cot, gain)


def attn_backward(windows, branch, x, kept, qkv, proj):
    rows, features = branch.shape
    width = proj.shape[0]
    groups = width // LANES
    outs = [shape_of(3, rows, width, dtype=BF), shape_of(1, 2 * width), shape_of(groups, SLOT, GROUP * SLOT),
            shape_of(rows, features, dtype=BF), shape_of(2, features)]
    scratch = [pltpu.VMEM((groups, SLOT * (windows + 1), LANES), F32)] * 4
    return call(functools.partial(attn_backward_kernel, windows), outs, scratch, "attn_backward", SMALL, (),
                branch, x, *kept, qkv, proj)


def attn_weights(split, me, sums2, gb1, blocks):
    features = blocks[0][0].shape[0]
    width = blocks[0][1].shape[1]
    grads = [shape_of(3, features, width, dtype=BF), shape_of(width, features, dtype=BF)]
    outs = ([shape_of(2, 4, BLOCK, features, dtype=BF)] * 2 if split else grads) + [shape_of(16, features, dtype=BF)]
    scratch = like(*grads) + [pltpu.VMEM((16 * SLOT, LANES), F32)]
    flat = [a for b in blocks for a in b]
    return call(functools.partial(attn_weights_kernel, len(blocks), split), outs, scratch + dma(64),
                "attn_weights", SMALL, (me,), sums2, gb1, *flat, far_outs=(0, 1))


def input_back(own, peer, x, gain, gmiddle):
    rows, features = x.shape
    return call(input_back_kernel, [shape_of(rows, features, dtype=BF)], [], "input_back", SMALL, (),
                own, peer, x, gain, gmiddle)[0]


def finish(me, sources, *outs):
    scratch = like(*sources, *outs) + dma(4, 16 * 4)
    return call(finish_kernel, list(outs), scratch, "finish", SMALL, (me,), *sources, far=range(4), far_outs=range(len(outs)))


def finish_mlp(me, sources):
    features = sources[0].shape[2]
    outs = [shape_of(features, 2 * features), shape_of(2 * features, features), shape_of(16, features)]
    scratch = like(*sources, *outs[:2]) + [pltpu.VMEM((16, 16, features), F32)] + dma(4, (2, 16))
    return call(finish_mlp_kernel, outs, scratch, "finish_mlp", SMALL, (me,), *sources, far=range(4), far_outs=(0, 1))


def across(v):
    return lax.ppermute(v, "mp", [(0, 1), (1, 0)])


def flip(v, bits):
    return lax.ppermute(v, "dp", [(i, i ^ bits) for i in range(16)])


def after(v, *others):
    return lax.optimization_barrier((v, *others))[0]


def total_of(terms):
    total = terms[0].astype(F32)
    for t in terms[1:]:
        total = total + t.astype(F32)
    return total.astype(BF)


def side_send(keep, got):
    return total_of([keep[1], got[1]])


def line_sends(keep, got, side):
    return [total_of([keep[0, k], got[0, k], side[k]]) for k in (1, 2, 3)]


def own_piece(keep, got, side, line):
    return total_of([keep[0, 0], got[0, 0], side[0], *line])


def flip_line(pieces):
    return [flip(p, LINE * k) for k, p in zip((1, 2, 3), pieces)]


def shards(
    dp_size,
    mp_size,
    patches,
    token_valid,
    ln1_gain,
    ln1_shift,
    qkv_weight,
    qv_bias,
    bias_table,
    proj_weight,
    proj_bias,
    ln2_gain,
    ln2_shift,
    fc1_weight,
    fc1_bias,
    fc2_weight,
    fc2_bias,
    cotangent,
):
    windows, _, features = patches.shape
    rows = windows * WIN
    width = proj_weight.shape[0]
    heads = width // HEAD
    fast = mp_size == 2 and dp_size == 16 and features == 768
    x = patches.transpose(1, 0, 2).reshape(rows, features)
    cot = cotangent.transpose(1, 0, 2).reshape(rows, features)
    row = lambda a: a.reshape(1, -1)
    extra = -width % LANES
    qkv = jnp.pad(qkv_weight.transpose(1, 0, 2), ((0, 0), (0, 0), (0, extra)))
    proj = jnp.pad(proj_weight, ((0, extra), (0, 0)))
    pos = position(bias_table.T)
    bias = jnp.pad(qv_bias, ((0, 0), (0, extra)))
    valid = token_valid.astype(F32)
    ln1, ln2 = (ln1_gain, ln1_shift), (ln2_gain, ln2_shift)

    def blocks_of(v):
        return [v, across(v)] if fast else list(lax.all_gather(v, "mp"))

    def own_sums(parts):
        if fast:
            return parts[0], across(parts[1])
        own = lax.psum_scatter(jnp.concatenate(parts), "mp", scatter_dimension=0, tiled=True)
        return own, jnp.zeros_like(own)

    index = lax.axis_index("dp").astype(jnp.int32)
    me = index.reshape(1)
    valids = blocks_of(valid)
    kept, xs = [], []
    for x_b, valid_b in zip(blocks_of(x), valids):
        if kept:
            x_b = after(x_b, kept[0][4])
            if fast:
                core = index & 1
                half = across(lax.dynamic_slice_in_dim(proj, core * (width // 2), width // 2, 0))
        xs.append(x_b)
        kept.append(attn_forward(windows, x_b, ln1, qkv, bias, pos, valid_b))
    project = lambda mixed, weight: jnp.dot(mixed, weight, preferred_element_type=F32).astype(BF)
    if fast:
        cots = [cot, across(after(cot, kept[0][4], valids[1], half))]
        mixed = across(after(kept[1][4], cots[1]))
        half = after(half, kept[1][4])
        rest = flip(half, CORE)
        parts, halves = (project(kept[0][4], proj), mixed), (half, rest)
    else:
        parts, halves = own_sums([project(k[4], proj) for k in kept]), ()
        cots = blocks_of(cot)
    middle, nm = middle_norm(me, x, *parts, proj_bias, ln2, halves)

    blocks, outs, gmids = [], [], []
    for nm_b, cot_b in zip(blocks_of(nm), cots):
        if blocks:
            nm_b = after(nm_b, gmids[-1])
        hid, gpre, out_b, gmid_b = mlp(nm_b, cot_b, fc1_weight, row(fc1_bias), fc2_weight)
        blocks.append((nm_b, cot_b, hid, gpre))
        outs.append(out_b)
        gmids.append(gmid_b)
    gmid_own, gmid_peer = own_sums(gmids)
    gb1, *g_mlp = mlp_weights(fast, me, blocks)
    outs = own_sums(outs)
    gmid_peer = after(gmid_peer, gb1)
    gmiddle, branch, sums2 = middle_back(gmid_own, gmid_peer, middle, cot, ln2[0])
    branches = blocks_of(branch)
    if fast:
        keep1, send1, keep2, send2 = g_mlp
        got1, got2 = after(flip(send1, CORE), branch), after(flip(send2, CORE), branch)
        side1, side2 = side_send(keep1, got1), side_send(keep2, got2)
        branches[0] = after(branches[0], side1, side2)
    backs, gparts = [], []
    for b, kept_b in enumerate(kept):
        if b == 1 and fast:
            side1 = after(flip(side1, SIDE), gparts[0])
            line1 = line_sends(keep1, got1, side1)
            branches[1] = after(branches[1], *line1, gparts[0])
        *back, gpart, gsum = attn_backward(windows, branches[b], xs[b], kept_b[:4], qkv, proj)
        backs.append((*back, gsum))
        gparts.append(gpart)
    if fast:
        side2 = after(flip(side2, SIDE), gparts[1])
        line2 = line_sends(keep2, got2, side2)
        line1 = [after(r, gparts[1]) for r in flip_line(line1)]
        piece1 = own_piece(keep1, got1, side1, line1)
        branches[0] = after(branches[0], piece1, *line2, outs[1])
    *g_attn, small = attn_weights(
        fast, me, sums2, gb1, [(k[5], k[4], br, *back) for k, br, back in zip(kept, branches, backs)])
    gnorms = own_sums(gparts)
    gpatch = input_back(*gnorms, x, ln1[0], gmiddle)
    output = (middle + outs[0].astype(F32) + outs[1].astype(F32) + row(fc2_bias)).astype(BF)

    if fast:
        line2 = [after(r, small) for r in flip_line(line2)]
        piece2 = own_piece(keep2, got2, side2, line2)
        keep, send = g_attn
        got = flip(after(send, piece2), CORE)
        side = flip(side_send(keep, got), SIDE)
        fc = jnp.concatenate([piece1, piece2, small], axis=0)
        fc_quad = jnp.stack([fc] + flip_line([fc] * 3))
        side = after(side, fc_quad, output)
        line = [after(r, gpatch) for r in flip_line(line_sends(keep, got, side))]
        piece = own_piece(keep, got, side, line)
        quad = jnp.stack([piece] + flip_line([piece] * 3))
        fc_pair = after(flip(fc_quad, SIDE), quad)
        g_fc1, g_fc2, small = finish_mlp(me, (fc_quad, fc_pair, after(flip(fc_quad, CORE), quad), after(flip(fc_pair, CORE), quad)))
        pair = after(flip(quad, SIDE), small)
        gw, gproj = finish(me, (quad, pair, flip(quad, CORE), flip(pair, CORE)),
                           shape_of(3, features, width), shape_of(width, features))
        totals = small[0:6] + across(small[0:6])
    else:
        g_fc1, g_fc2, gw, gproj = [g.astype(F32) for g in lax.psum((*g_mlp, *g_attn), "dp")]
        gw, gproj = gw[:, :, :width], gproj[:width]
        small = lax.psum(small, "dp").astype(F32)
        totals = lax.psum(small[0:6], "mp")
    padded = width + extra
    gqv = jnp.stack([small[6, :width], small[6, padded : padded + width]])
    gb1 = small[7:12].reshape(-1)[: gb1.size]
    gt = small[12:].reshape(12, 2 * LANES)[:heads, :REL].T

    unrow = lambda a: a.reshape(WIN, windows, features).transpose(1, 0, 2)
    return (
        unrow(output),
        unrow(gpatch),
        totals[0],
        totals[1],
        gw.transpose(1, 0, 2),
        gqv,
        gt,
        gproj,
        totals[4],
        totals[2],
        totals[3],
        g_fc1,
        gb1,
        g_fc2,
        totals[5],
    )


def solution(mesh):
    placed = (
        P(("dp", "mp"), None, None),
        P(("dp", "mp"), None),
        P(),
        P(),
        P(None, None, "mp"),
        P(None, "mp"),
        P(None, "mp"),
        P("mp", None),
        P(),
        P(),
        P(),
        P(None, "mp"),
        P("mp"),
        P("mp", None),
        P(),
        P(("dp", "mp"), None, None),
    )
    return jax.shard_map(
        functools.partial(shards, mesh.shape["dp"], mesh.shape["mp"]),
        mesh=mesh,
        in_specs=placed,
        out_specs=(
            P(("dp", "mp"), None, None),
            P(("dp", "mp"), None, None),
            P(),
            P(),
            P(None, None, "mp"),
            P(None, "mp"),
            P(None, "mp"),
            P("mp", None),
            P(),
            P(),
            P(),
            P(None, "mp"),
            P("mp"),
            P("mp", None),
            P(),
        ),
        check_vma=False,
    )
```

```python
import functools

import jax
import jax.numpy as jnp
from jax import lax
from jax.experimental import pallas as pl
from jax.experimental.pallas import tpu as pltpu
from jax.sharding import PartitionSpec as P

HEAD = 32
WSIDE = 7
WIN = 49
REL = 169
SLOT = 64
GROUP = 4
LANES = 128
EPS = 1e-05
SCALING = HEAD ** (-0.5)
BF = jnp.bfloat16
F32 = jnp.float32
HIGH = lax.Precision.HIGHEST
VMEM_LIMIT = 28 * 1024 * 1024
ALL_VMEM = 58 * 1024 * 1024
BLOCK = 96
CORE, SIDE, LINE = 1, 2, 4

ROW_COL = (((1,), (0,)), ((), ()))
LAST_LAST = (((1,), (1,)), ((), ()))
ROWS_ROWS = (((0,), (0,)), ((), ()))


def mm(a, b, dims=ROW_COL):
    return lax.dot_general(a, b, dims, preferred_element_type=F32)


def norm_parts(rows):
    mean = jnp.mean(rows, axis=-1, keepdims=True)
    centred = rows - mean
    variance = jnp.mean(centred * centred, axis=-1, keepdims=True)
    inv = lax.rsqrt(variance + EPS)
    return centred * inv, inv


def norm_back(xhat, inv, gain, upstream):
    z = upstream * gain
    mean_z = jnp.mean(z, axis=-1, keepdims=True)
    mean_zx = jnp.mean(z * xhat, axis=-1, keepdims=True)
    return (z - mean_z - xhat * mean_zx) * inv


def head_masks():
    lane = lax.broadcasted_iota(jnp.int32, (SLOT, LANES), 1)
    return [jnp.where((lane >> 5) == h, 1.0, 0.0).astype(BF) for h in range(GROUP)]


def block_ones():
    row = lax.broadcasted_iota(jnp.int32, (GROUP * SLOT, GROUP * SLOT), 0)
    col = lax.broadcasted_iota(jnp.int32, (GROUP * SLOT, GROUP * SLOT), 1)
    return jnp.where((row >> 6) == (col >> 6), 1.0, 0.0).astype(BF)


def spread(tile, masks):
    return jnp.concatenate([tile * m for m in masks], axis=0)


def collect(full, masks_f):
    total = full[0:SLOT] * masks_f[0]
    for h in range(1, GROUP):
        total = total + full[h * SLOT : (h + 1) * SLOT] * masks_f[h]
    return total


def fill(scratch, rows, windows):
    pitch = windows + 1
    for g in range(scratch.shape[0]):
        for place in range(WIN):
            scratch[g, place * pitch : place * pitch + windows, :] = rows[
                place * windows : (place + 1) * windows, g * LANES : (g + 1) * LANES]
        scratch[g, WIN * pitch :, :] = jnp.zeros((scratch.shape[1] - WIN * pitch, LANES), rows.dtype)


def empty(scratch, windows):
    pitch = windows + 1
    planes = [
        jnp.concatenate([scratch[g, place * pitch : place * pitch + windows, :] for place in range(WIN)], axis=0)
        for g in range(scratch.shape[0])
    ]
    return jnp.concatenate(planes, axis=1).astype(BF)


def row_max(tile, low_half):
    low = jnp.max(jnp.where(low_half, tile, -3e38), axis=-1, keepdims=True)
    high = jnp.max(jnp.where(low_half, -3e38, tile), axis=-1, keepdims=True)
    return jnp.where(low_half, low, high)


def row_sum(tile, low_half):
    low = jnp.sum(jnp.where(low_half, tile, 0.0), axis=-1, keepdims=True)
    high = jnp.sum(jnp.where(low_half, 0.0, tile), axis=-1, keepdims=True)
    return jnp.where(low_half, low, high)


def ds(start, size):
    unit = 384 if size % 384 == 0 else 48
    return pl.ds(pl.multiple_of(start, unit), size)


def each_block(me, *by_core):
    for c_rel, target in enumerate(by_core):
        for y_rel in range(2):
            for z_rel in range(4):
                yield target, y_rel, z_rel, (me & 1) ^ c_rel, ((me >> 1) & 1) ^ y_rel, (me >> 2) ^ z_rel


def line(ref):
    return ref[...].reshape(1, -1)


def begin(sems, *pairs):
    copies = [pltpu.make_async_copy(a, b, sems.at[i]) for i, (a, b) in enumerate(pairs)]
    for copy in copies:
        copy.start()
    return copies


def finish_all(copies):
    for copy in copies:
        copy.wait()


def attn_forward_kernel(windows, x_in, gain_ref, shift_ref, w_in, bias_ref, pos_ref, valid_ref,
                        prob_ref, q_ref, k_ref, v_ref, mixed_ref, normed_t_ref,
                        mask_s, q_s, k_s, v_s, mixed_s, x_ref, w_ref, in_sems):
    copies = begin(in_sems, (x_in, x_ref), *[(w_in.at[p], w_ref.at[p]) for p in range(3)])
    mask_s[...] = jnp.zeros(mask_s.shape, F32)
    for h in range(GROUP):
        mask_s[:, h * SLOT : h * SLOT + WIN] = valid_ref[...].astype(F32)
    masks = head_masks()
    ones = block_ones()
    low_half = lax.broadcasted_iota(jnp.int32, (SLOT, LANES), 1) < SLOT
    copies[0].wait()
    x = x_ref[...].astype(F32)
    rows = x.shape[0]
    groups = q_s.shape[0]
    xhat, _ = norm_parts(x)
    normed = (xhat * line(gain_ref) + line(shift_ref)).astype(BF)
    normed_t_ref[...] = normed.T
    for part, scratch in enumerate((q_s, k_s, v_s)):
        copies[1 + part].wait()
        got = mm(normed, w_ref[part])
        if part != 1:
            got = got + bias_ref[part // 2 : part // 2 + 1, :]
        fill(scratch, got.astype(BF).astype(F32), windows)

    def window(w, carry):
        allowed = jnp.broadcast_to(mask_s[pl.ds(w, 1), :], (SLOT, GROUP * SLOT)) > 0.5
        for g in range(groups):
            cols = slice(g * LANES, (g + 1) * LANES)
            places = pl.ds(w, SLOT, stride=windows + 1)
            q = q_s[g, places, :].astype(BF)
            k = k_s[g, places, :].astype(BF)
            v = v_s[g, places, :].astype(BF)
            q_ref[w, :, cols] = q
            k_ref[w, :, cols] = k
            v_ref[w, :, cols] = v
            scores = mm(q, spread(k, masks), LAST_LAST) * SCALING + pos_ref[g]
            scores = jnp.where(allowed, scores, -1000000000.0)
            top = jnp.concatenate([row_max(scores[:, :LANES], low_half), row_max(scores[:, LANES:], low_half)], axis=1)
            e = jnp.exp(scores - top)
            total = mm(e.astype(BF), ones)
            inv = pl.reciprocal(total, approx=True)
            prob = (e * (inv * (2.0 - total * inv))).astype(BF)
            prob_ref[w, g] = prob
            mixed_s[g, places, :] = mm(prob, spread(v, masks))
        return carry

    lax.fori_loop(0, windows, window, 0, unroll=2)
    mixed_ref[...] = empty(mixed_s, windows)


def middle_kernel(heads, me_ref, x_in, own_in, peer_in, bias_ref, gain_ref, shift_ref, *refs):
    if heads:
        half_in, rest_in, middle_ref, nm_ref, x_ref, own_ref, peer_ref, proj_ref, sems = refs
        lines = half_in.shape[0]
        core = me_ref[0] & 1
        place = lambda c: proj_ref.at[pl.ds(pl.multiple_of(c * lines, lines), lines), :]
        copies = begin(sems, (peer_in, peer_ref), (half_in, place(core)), (rest_in, place(1 - core)), (x_in, x_ref),
                       (own_in, own_ref))
        finish_all(copies[:3])
        peer = mm(peer_ref[...], proj_ref[...])
        finish_all(copies[3:])
    else:
        middle_ref, nm_ref, x_ref, own_ref, peer_ref, sems = refs
        finish_all(begin(sems, (x_in, x_ref), (own_in, own_ref), (peer_in, peer_ref)))
        peer = peer_ref[...].astype(F32)
    middle = x_ref[...].astype(F32) + (own_ref[...].astype(F32) + peer) + line(bias_ref)
    middle_ref[...] = middle
    xhat, _ = norm_parts(middle)
    nm_ref[...] = (xhat * line(gain_ref) + line(shift_ref)).astype(BF)


def mlp_kernel(nm_ref, cot_ref, fc1_ref, b1_ref, fc2_ref, hid_ref, gpre_ref, out_ref, gmid_ref):
    hidden_size = fc1_ref.shape[1]
    features = fc1_ref.shape[0]
    step = 256 if hidden_size % 256 == 0 else 128
    count = hidden_size // step

    nm = nm_ref[...]
    cot = cot_ref[...]

    def units(c, carry):
        cols = pl.ds(pl.multiple_of(c * step, step), step)
        pre = mm(nm, fc1_ref[:, cols]) + b1_ref[:, cols]
        phi = 0.5 * (1.0 + lax.erf(pre * (0.5 ** 0.5)))
        hid_ref[:, cols] = (pre * phi).astype(BF)
        slope = phi + pre * (jnp.exp(-0.5 * pre * pre) * 0.3989422804014327)
        gpre_ref[:, cols] = (mm(cot, fc2_ref[cols, :], LAST_LAST) * slope).astype(BF)
        return carry

    lax.fori_loop(0, count, units, 0)

    def tile(c, carry):
        cols = pl.ds(pl.multiple_of(c * 256, 256), 256)
        gmid_ref[:, cols] = mm(gpre_ref[...], fc1_ref[cols, :], LAST_LAST).astype(BF)
        out_ref[:, cols] = mm(hid_ref[...], fc2_ref[:, cols]).astype(BF)
        return carry

    lax.fori_loop(0, features // 256, tile, 0)

def mlp_weights_kernel(count, split, me_ref, *refs):
    inputs, refs = refs[: 4 * count], refs[4 * count :]
    n_out = 5 if split else 3
    gb1_ref, *outs = refs[:n_out]
    held = refs[n_out : n_out + 4 * count]
    nts = refs[n_out + 4 * count : n_out + 5 * count]
    g1_ref, g2_ref, in_sems, unit_sems, out_sems = refs[n_out + 5 * count :]
    blocks = [held[4 * b : 4 * b + 4] for b in range(count)]
    hidden_size = g1_ref.shape[1]
    features = g1_ref.shape[0]
    step = 384 if hidden_size % 384 == 0 else 128
    wide = features if hidden_size % features == 0 else step

    def units_in(j):
        cols = ds(j * step, step)
        return [pltpu.make_async_copy(inputs[4 * b + 2].at[:, cols], held[4 * b + 2].at[:, cols], unit_sems.at[b, j])
                for b in range(count)]

    order = [4 * b + k for k in (0, 1) for b in range(count)]
    copies = dict(zip(order, begin(in_sems, *[(inputs[i], held[i]) for i in order])))
    for j in range(hidden_size // step):
        for copy in units_in(j):
            copy.start()
    last = [pltpu.make_async_copy(inputs[4 * b + 3], held[4 * b + 3], in_sems.at[2 * count + b]) for b in range(count)]
    for copy in last:
        copy.start()
    finish_all([copies[4 * b] for b in range(count)])
    for block, nt in zip(blocks, nts):
        nt[...] = block[0][...].T
    finish_all([copies[4 * b + 1] for b in range(count)])

    def second(j, carry):
        finish_all(units_in(j))
        cols = ds(j * step, step)
        g2_ref[cols, :] = sum(mm(hid_ref[:, cols], cot_ref[...], ROWS_ROWS) for _, cot_ref, hid_ref, _ in blocks).astype(BF)
        return carry

    def first(j, carry):
        cols = ds(j * wide, wide)
        g1_ref[:, cols] = sum(mm(nt[...], block[3][:, cols]) for nt, block in zip(nts, blocks)).astype(BF)
        return carry

    lax.fori_loop(0, hidden_size // step, second, 0)
    me = me_ref[0]
    sent = []

    def send(k, source, target):
        sent.append(pltpu.make_async_copy(source, target, out_sems.at[k]))
        sent[-1].start()

    if split:
        for i, (target, y_rel, z_rel, c, y, z) in enumerate(each_block(me, outs[2], outs[3])):
            send(i, g2_ref.at[ds(c * 768 + y * 384 + z * 96, 96), :], target.at[y_rel, z_rel])
    else:
        send(0, g2_ref, outs[1])
    finish_all(last)
    gb1_ref[...] = sum(jnp.sum(block[3][...].astype(F32), axis=0, keepdims=True) for block in blocks)
    lax.fori_loop(0, hidden_size // wide, first, 0)
    if split:
        for i, (target, y_rel, z_rel, c, y, z) in enumerate(each_block(me, outs[0], outs[1])):
            send(16 + i, g1_ref.at[ds(y * 384 + z * 96, 96), ds(c * 768, 768)], target.at[y_rel, z_rel])
    else:
        send(1, g1_ref, outs[0])
    finish_all(sent)


def middle_back_kernel(own_ref, peer_ref, middle_ref, cot_ref, gain_ref, gmiddle_ref, branch_ref, sums_ref):
    upstream = cot_ref[...].astype(F32)
    xhat, inv = norm_parts(middle_ref[...])
    gmid = own_ref[...].astype(F32) + peer_ref[...].astype(F32)
    sums_ref[0:1, :] = jnp.sum(gmid * xhat, axis=0, keepdims=True)
    sums_ref[1:2, :] = jnp.sum(gmid, axis=0, keepdims=True)
    gmiddle = upstream + norm_back(xhat, inv, line(gain_ref), gmid)
    gmiddle_ref[...] = gmiddle
    branch_ref[...] = gmiddle.astype(BF)
    sums_ref[2:3, :] = jnp.sum(gmiddle, axis=0, keepdims=True)
    sums_ref[3:4, :] = jnp.sum(upstream, axis=0, keepdims=True)


def attn_backward_kernel(windows, branch_ref, x_ref, prob_ref, q_ref, k_ref, v_ref, w_ref, proj_ref,
                         grads_ref, gqv_ref, gpos_ref, part_ref, sums_ref, gm_s, gq_s, gk_s, gv_s):
    rows = branch_ref.shape[0]
    groups = gm_s.shape[0]
    gpos_ref[...] = jnp.zeros(gpos_ref.shape, F32)
    masks = head_masks()
    masks_f = [m.astype(F32) for m in masks]
    low_half = lax.broadcasted_iota(jnp.int32, (SLOT, LANES), 1) < SLOT
    fill(gm_s, mm(branch_ref[...], proj_ref[...], LAST_LAST).astype(BF).astype(F32), windows)

    def window(w, carry):
        for g in range(groups):
            cols = slice(g * LANES, (g + 1) * LANES)
            places = pl.ds(w, SLOT, stride=windows + 1)
            gm = gm_s[g, places, :].astype(BF)
            q = q_ref[w, :, cols]
            k = k_ref[w, :, cols]
            v = v_ref[w, :, cols]
            prob = prob_ref[w, g]
            prob_f = prob.astype(F32)
            gprob = mm(gm, spread(v, masks), LAST_LAST)
            both = prob_f * gprob
            delta = jnp.concatenate([row_sum(both[:, :LANES], low_half), row_sum(both[:, LANES:], low_half)], axis=1)
            gs = (both - prob_f * delta).astype(BF)
            gpos_ref[g] += gs.astype(F32)
            gq_s[g, places, :] = mm(gs, spread(k, masks)) * SCALING
            gk_s[g, places, :] = collect(mm(gs, q, ROWS_ROWS), masks_f) * SCALING
            gv_s[g, places, :] = collect(mm(prob, gm, ROWS_ROWS), masks_f)
        return carry

    lax.fori_loop(0, windows, window, 0, unroll=2)
    back = None
    for part, scratch in enumerate((gq_s, gk_s, gv_s)):
        grad = empty(scratch, windows)
        grads_ref[part] = grad
        if part != 1:
            width = grad.shape[1]
            lanes = slice(part // 2 * width, (part // 2 + 1) * width)
            gqv_ref[:, lanes] = jnp.sum(grad.astype(F32), axis=0, keepdims=True)
        term = mm(grad, w_ref[part], LAST_LAST)
        back = term if back is None else back + term
    part_ref[...] = back.astype(BF)
    xhat, _ = norm_parts(x_ref[...].astype(F32))
    sums_ref[0:1, :] = jnp.sum(back * xhat, axis=0, keepdims=True)
    sums_ref[1:2, :] = jnp.sum(back, axis=0, keepdims=True)


def place_offset(i):
    return i // WSIDE * (2 * WSIDE - 1) + i % WSIDE


def offset_picks():
    row = lax.broadcasted_iota(jnp.int32, (2 * LANES, 2 * SLOT), 0)
    col = lax.broadcasted_iota(jnp.int32, (2 * LANES, 2 * SLOT), 1)
    j = col & (SLOT - 1)
    line = (j * 37) >> 8
    offset = place_offset(WIN - 1) - line * (2 * WSIDE - 1) - (j - line * WSIDE)
    hit = ((row & (LANES - 1)) == offset) & ((row >> 7) == (col >> 6)) & (j < WIN)
    return jnp.where(hit, 1.0, 0.0).astype(BF)


def position_kernel(table_ref, pos_ref, table_s, rows_s):
    heads = table_ref.shape[0]
    table_s[...] = jnp.zeros(table_s.shape, F32)
    table_s[0:heads, 0:REL] = table_ref[...]
    table = table_s[...]
    lines = table.shape[0]
    rows_s[WIN * lines :, :] = jnp.zeros((rows_s.shape[0] - WIN * lines, LANES), F32)
    for i in range(WIN):
        turned = pltpu.roll(table, (2 * LANES - place_offset(i)) % (2 * LANES), 1)
        rows_s[i * lines : (i + 1) * lines, :] = turned[:, :LANES]
    picks = offset_picks()
    for pair in range(pos_ref.shape[0] * 2):
        pieces = [rows_s[pl.ds(2 * pair + k, SLOT, stride=lines), :] for k in range(2)]
        rest = jnp.concatenate(pieces, axis=1)
        total = jnp.zeros((SLOT, 2 * SLOT), F32)
        for _ in range(3):
            top = rest.astype(BF)
            total = total + mm(top, picks)
            rest = rest - top.astype(F32)
        pos_ref[pair // 2, :, pair % 2 * LANES : (pair % 2 + 1) * LANES] = total


def attn_weights_kernel(count, split, me_ref, sums2_ref, gb1_ref, *refs):
    blocks, refs = [refs[7 * b : 7 * b + 7] for b in range(count)], refs[7 * count :]
    *outs, small_ref = refs[:3]
    gw_ref, gproj_ref, rows_s, out_sems = refs[3:]
    gproj, gqv, gpos, sums = 0.0, 0.0, 0.0, 0.0
    for _, mixed_ref, branch_ref, _, gqv_ref, gpos_ref, sums_ref in blocks:
        gproj = gproj + mm(mixed_ref[...], branch_ref[...], ROWS_ROWS)
        gqv, gpos, sums = gqv + gqv_ref[...], gpos + gpos_ref[...], sums + sums_ref[...]
    width, features = gproj.shape
    gproj_ref[...] = gproj.astype(BF)
    hidden = gb1_ref.shape[1]
    lines = [sums[k : k + 1] for k in range(2)] + [sums2_ref[k : k + 1, :] for k in range(4)]
    lines.append(gqv)
    lines += [gb1_ref[:, k : min(k + features, hidden)] for k in range(0, hidden, features)]
    small = jnp.concatenate(
        [jnp.concatenate([line, jnp.zeros((1, features - line.shape[1]), F32)], axis=1) if line.shape[1] < features else line
         for line in lines] + [jnp.zeros((12 - len(lines), features), F32)], axis=0)
    picks = offset_picks()
    for pair in range(gpos.shape[0] * 2):
        rest = gpos[pair // 2][:, pair % 2 * LANES : (pair % 2 + 1) * LANES]
        total = jnp.zeros((SLOT, 2 * LANES), F32)
        for _ in range(2):
            top = rest.astype(BF)
            total = total + mm(top, picks, LAST_LAST)
            rest = rest - top.astype(F32)
        for k in range(2):
            rows_s[pl.ds(2 * pair + k, SLOT, stride=16), :] = total[:, k * LANES : (k + 1) * LANES]
    for h in range(gpos.shape[0] * 4, 16):
        rows_s[pl.ds(h, SLOT, stride=16), :] = jnp.zeros((SLOT, LANES), F32)
    table = jnp.zeros((16, 2 * LANES), F32)
    for i in range(WIN):
        row = jnp.concatenate([rows_s[i * 16 : (i + 1) * 16, :], jnp.zeros((16, LANES), F32)], axis=1)
        table = table + (pltpu.roll(row, place_offset(i), 1) if i else row)
    packed = [jnp.concatenate([table[3 * r + k : 3 * r + k + 1] for k in range(3)], axis=1) for r in range(4)]
    small_ref[...] = jnp.concatenate([small] + packed, axis=0).astype(BF)
    sent = []

    def send(k, source, target):
        sent.append(pltpu.make_async_copy(source, target, out_sems.at[k]))
        sent[-1].start()

    if split:
        for i, (target, y_rel, z_rel, c, y, z) in enumerate(each_block(me_ref[0], *outs)):
            send(i, gproj_ref.at[ds((c * 4 + y * 2 + (z >> 1)) * 48, 48), ds((z & 1) * 384, 384)],
                 target.at[y_rel, z_rel, 48:96, 384:768])
    else:
        send(0, gproj_ref, outs[1])
    for part in range(3):
        gw = 0.0
        for normed_t_ref, _, _, grads_ref, _, _, _ in blocks:
            gw = gw + mm(normed_t_ref[...], grads_ref[part])
        gw_ref[part] = gw.astype(BF)
        if split:
            for i, (target, y_rel, z_rel, c, y, z) in enumerate(each_block(me_ref[0], *outs)):
                send(16 * (part + 1) + i, gw_ref.at[part, ds(c * 384 + y * 192 + z * 48, 48), :],
                     target.at[y_rel, z_rel, part // 2 * 48 : part // 2 * 48 + 48, part % 2 * 384 : part % 2 * 384 + 384])
        else:
            send(1 + part, gw_ref.at[part], outs[0].at[part])
    finish_all(sent)


def input_back_kernel(own_ref, peer_ref, x_ref, gain_ref, gmiddle_ref, gpatch_ref):
    gnorm = own_ref[...].astype(F32) + peer_ref[...].astype(F32)
    xhat, inv = norm_parts(x_ref[...].astype(F32))
    gpatch_ref[...] = (gmiddle_ref[...] + norm_back(xhat, inv, line(gain_ref), gnorm)).astype(BF)


def finish_kernel(me_ref, *refs):
    sources, outs, held, wide, (in_sems, out_sems) = refs[:4], refs[4:6], refs[6:10], refs[10:12], refs[12:]
    copies = begin(in_sems, *zip(sources, held))
    sent = []

    def put(value, k, where):
        wide[k][where] = value.astype(F32)
        sent.append(pltpu.make_async_copy(wide[k].at[where], outs[k].at[where], out_sems.at[len(sent)]))
        sent[-1].start()

    for source, y_rel, z_rel, c, y, z in each_block(me_ref[0], (0, 1), (2, 3)):
        source = source[y_rel]
        if z_rel == 0:
            copies[source].wait()
        piece = held[source].at[z_rel]
        lines = ds(c * 384 + y * 192 + z * 48, 48)
        put(piece[0:48, 0:384], 0, (0, lines, slice(None)))
        put(piece[0:48, 384:768], 0, (1, lines, slice(None)))
        put(piece[48:96, 0:384], 0, (2, lines, slice(None)))
        put(piece[48:96, 384:768], 1, (ds((c * 4 + y * 2 + (z >> 1)) * 48, 48), ds((z & 1) * 384, 384)))
    finish_all(sent)


def finish_mlp_kernel(me_ref, *refs):
    sources, (g1_out, g2_out, small_ref), held, (g1_ref, g2_ref, small_s, in_sems, out_sems) = (
        refs[:4], refs[4:7], refs[7:11], refs[11:])
    copies = begin(in_sems, *zip(sources, held))
    sent = []

    def put(value, k, wide, out, where):
        wide[where] = value.astype(F32)
        sent.append(pltpu.make_async_copy(wide.at[where], out.at[where], out_sems.at[k, len(sent) // 2]))
        sent[-1].start()

    for source, y_rel, z_rel, c, y, z in each_block(me_ref[0], (0, 1), (2, 3)):
        source = source[y_rel]
        if z_rel == 0:
            copies[source].wait()
        piece = held[source].at[z_rel]
        put(piece[0:BLOCK, :], 0, g1_ref, g1_out, (ds(y * 384 + z * 96, 96), ds(c * 768, 768)))
        put(piece[BLOCK : 2 * BLOCK, :], 1, g2_ref, g2_out, (ds(c * 768 + y * 384 + z * 96, 96), slice(None)))
        small_s[z * 4 + y * 2 + c] = piece[2 * BLOCK :, :].astype(F32)
    total = small_s[0]
    for d in range(1, 16):
        total = total + small_s[d]
    small_ref[...] = total
    finish_all(sent)


def shape_of(*dims, dtype=F32):
    return jax.ShapeDtypeStruct(dims, dtype)


def call(kernel, outs, scratch, name, flops, smem, *args, far=(), far_outs=(), limit=VMEM_LIMIT):
    space = lambda is_far: pl.BlockSpec(memory_space=pltpu.HBM if is_far else pltpu.VMEM)
    in_specs = [pl.BlockSpec(memory_space=pltpu.SMEM)] * len(smem) + [space(i in far) for i in range(len(args))]
    return pl.pallas_call(
        kernel,
        out_shape=outs,
        in_specs=in_specs,
        out_specs=[space(i in far_outs) for i in range(len(outs))],
        scratch_shapes=scratch,
        compiler_params=pltpu.CompilerParams(vmem_limit_bytes=limit),
        cost_estimate=pl.CostEstimate(flops=flops, bytes_accessed=flops // 256, transcendentals=0),
        name=name,
    )(*smem, *args)


def like(*arrays):
    return [pltpu.VMEM(a.shape, a.dtype) for a in arrays]


def dma(*counts):
    return [pltpu.SemaphoreType.DMA(c if isinstance(c, tuple) else (c,)) for c in counts]


SMALL = 1000000


def position(table):
    heads = table.shape[0]
    groups = -(-heads // GROUP)
    return call(position_kernel, [shape_of(groups, SLOT, GROUP * SLOT)],
                [pltpu.VMEM((16, 2 * LANES), F32), pltpu.VMEM((16 * SLOT, LANES), F32)], "position", SMALL, (), table)[0]


def attn_forward(windows, x, ln1, qkv, qv_bias, pos, mask):
    rows, features = x.shape
    width = qkv.shape[2]
    groups = width // LANES
    tile = shape_of(windows, SLOT, width, dtype=BF)
    outs = [shape_of(windows, groups, SLOT, GROUP * SLOT, dtype=BF), tile, tile, tile, shape_of(rows, width, dtype=BF),
            shape_of(features, rows, dtype=BF)]
    scratch = [pltpu.VMEM((windows, GROUP * SLOT), F32)] + [pltpu.VMEM((groups, SLOT * (windows + 1), LANES), F32)] * 4
    scratch += like(x, qkv) + dma(4)
    return call(functools.partial(attn_forward_kernel, windows), outs, scratch, "attn_forward", SMALL, (),
                x, *ln1, qkv, qv_bias, pos, mask, far=(0, 3), limit=ALL_VMEM)


def middle_norm(me, x, own, peer, bias, ln2, halves):
    rows, features = x.shape
    scratch = like(x, own, peer)
    if halves:
        scratch += [pltpu.VMEM((2 * halves[0].shape[0], features), BF)]
    return call(functools.partial(middle_kernel, bool(halves)), [shape_of(rows, features), shape_of(rows, features, dtype=BF)],
                scratch + dma(5), "middle", SMALL, (me,), x, own, peer, bias, *ln2, *halves, far=(0, 1, 2, 6, 7),
                limit=ALL_VMEM)


def mlp(nm, cot, fc1, fc1_bias, fc2):
    rows, features = nm.shape
    hidden = fc2.shape[0]
    outs = [shape_of(rows, hidden, dtype=BF)] * 2 + [shape_of(rows, features, dtype=BF)] * 2
    return call(mlp_kernel, outs, [], "mlp", SMALL, (), nm, cot, fc1, fc1_bias, fc2)


def mlp_weights(split, me, blocks):
    rows, features = blocks[0][0].shape
    hidden = blocks[0][2].shape[1]
    grads = [shape_of(features, hidden, dtype=BF), shape_of(hidden, features, dtype=BF)]
    outs = [shape_of(1, hidden)] + ([shape_of(2, 4, BLOCK, features, dtype=BF)] * 4 if split else grads)
    flat = [a for b in blocks for a in b]
    scratch = like(*flat) + [pltpu.VMEM((features, rows), BF)] * len(blocks) + like(*grads) + dma(3 * len(blocks), (len(blocks), hidden // 128), 32)
    return call(functools.partial(mlp_weights_kernel, len(blocks), split), outs, scratch, "mlp_weights", SMALL,
                (me,), *flat, far=range(len(flat)), far_outs=range(1, len(outs)), limit=ALL_VMEM)


def middle_back(own, peer, middle, cot, gain):
    rows, features = middle.shape
    return call(
        middle_back_kernel, [shape_of(rows, features), shape_of(rows, features, dtype=BF), shape_of(4, features)], [],
        "middle_back", 20000 * SMALL, (), own, peer, middle, cot, gain)


def attn_backward(windows, branch, x, kept, qkv, proj):
    rows, features = branch.shape
    width = proj.shape[0]
    groups = width // LANES
    outs = [shape_of(3, rows, width, dtype=BF), shape_of(1, 2 * width), shape_of(groups, SLOT, GROUP * SLOT),
            shape_of(rows, features, dtype=BF), shape_of(2, features)]
    scratch = [pltpu.VMEM((groups, SLOT * (windows + 1), LANES), F32)] * 4
    return call(functools.partial(attn_backward_kernel, windows), outs, scratch, "attn_backward", SMALL, (),
                branch, x, *kept, qkv, proj)


def attn_weights(split, me, sums2, gb1, blocks):
    features = blocks[0][0].shape[0]
    width = blocks[0][1].shape[1]
    grads = [shape_of(3, features, width, dtype=BF), shape_of(width, features, dtype=BF)]
    outs = ([shape_of(2, 4, BLOCK, features, dtype=BF)] * 2 if split else grads) + [shape_of(16, features, dtype=BF)]
    scratch = like(*grads) + [pltpu.VMEM((16 * SLOT, LANES), F32)]
    flat = [a for b in blocks for a in b]
    return call(functools.partial(attn_weights_kernel, len(blocks), split), outs, scratch + dma(64),
                "attn_weights", SMALL, (me,), sums2, gb1, *flat, far_outs=(0, 1))


def input_back(own, peer, x, gain, gmiddle):
    rows, features = x.shape
    return call(input_back_kernel, [shape_of(rows, features, dtype=BF)], [], "input_back", SMALL, (),
                own, peer, x, gain, gmiddle)[0]


def finish(me, sources, *outs):
    scratch = like(*sources, *outs) + dma(4, 16 * 4)
    return call(finish_kernel, list(outs), scratch, "finish", SMALL, (me,), *sources, far=range(4), far_outs=range(len(outs)))


def finish_mlp(me, sources):
    features = sources[0].shape[2]
    outs = [shape_of(features, 2 * features), shape_of(2 * features, features), shape_of(16, features)]
    scratch = like(*sources, *outs[:2]) + [pltpu.VMEM((16, 16, features), F32)] + dma(4, (2, 16))
    return call(finish_mlp_kernel, outs, scratch, "finish_mlp", SMALL, (me,), *sources, far=range(4), far_outs=(0, 1))


def across(v):
    return lax.ppermute(v, "mp", [(0, 1), (1, 0)])


def flip(v, bits):
    return lax.ppermute(v, "dp", [(i, i ^ bits) for i in range(16)])


def after(v, *others):
    return lax.optimization_barrier((v, *others))[0]


def total_of(terms):
    total = terms[0].astype(F32)
    for t in terms[1:]:
        total = total + t.astype(F32)
    return total.astype(BF)


def side_send(keep, got):
    return total_of([keep[1], got[1]])


def line_sends(keep, got, side):
    return [total_of([keep[0, k], got[0, k], side[k]]) for k in (1, 2, 3)]


def own_piece(keep, got, side, line):
    return total_of([keep[0, 0], got[0, 0], side[0], *line])


def flip_line(pieces):
    return [flip(p, LINE * k) for k, p in zip((1, 2, 3), pieces)]


def shards(
    dp_size,
    mp_size,
    patches,
    token_valid,
    ln1_gain,
    ln1_shift,
    qkv_weight,
    qv_bias,
    bias_table,
    proj_weight,
    proj_bias,
    ln2_gain,
    ln2_shift,
    fc1_weight,
    fc1_bias,
    fc2_weight,
    fc2_bias,
    cotangent,
):
    windows, _, features = patches.shape
    rows = windows * WIN
    width = proj_weight.shape[0]
    heads = width // HEAD
    fast = mp_size == 2 and dp_size == 16 and features == 768
    x = patches.transpose(1, 0, 2).reshape(rows, features)
    cot = cotangent.transpose(1, 0, 2).reshape(rows, features)
    row = lambda a: a.reshape(1, -1)
    extra = -width % LANES
    qkv = jnp.pad(qkv_weight.transpose(1, 0, 2), ((0, 0), (0, 0), (0, extra)))
    proj = jnp.pad(proj_weight, ((0, extra), (0, 0)))
    pos = position(bias_table.T)
    bias = jnp.pad(qv_bias, ((0, 0), (0, extra)))
    valid = token_valid.astype(F32)
    ln1, ln2 = (ln1_gain, ln1_shift), (ln2_gain, ln2_shift)

    def blocks_of(v):
        return [v, across(v)] if fast else list(lax.all_gather(v, "mp"))

    def own_sums(parts):
        if fast:
            return parts[0], across(parts[1])
        own = lax.psum_scatter(jnp.concatenate(parts), "mp", scatter_dimension=0, tiled=True)
        return own, jnp.zeros_like(own)

    index = lax.axis_index("dp").astype(jnp.int32)
    me = index.reshape(1)
    valids = blocks_of(valid)
    kept, xs = [], []
    for x_b, valid_b in zip(blocks_of(x), valids):
        if kept:
            x_b = after(x_b, kept[0][4])
        xs.append(x_b)
        kept.append(attn_forward(windows, x_b, ln1, qkv, bias, pos, valid_b))
    project = lambda mixed, weight: jnp.dot(mixed, weight, preferred_element_type=F32).astype(BF)
    if fast:
        core = index & 1
        half = across(lax.dynamic_slice_in_dim(after(proj, valids[1]), core * (width // 2), width // 2, 0))
        cots = [cot, across(after(cot, valids[1]))]
        mixed = across(after(kept[1][4], cots[1], half))
        half = after(half, kept[1][4])
        rest = flip(half, CORE)
        parts, halves = (project(kept[0][4], proj), mixed), (half, rest)
    else:
        parts, halves = own_sums([project(k[4], proj) for k in kept]), ()
        cots = blocks_of(cot)
    middle, nm = middle_norm(me, x, *parts, proj_bias, ln2, halves)

    blocks, outs, gmids = [], [], []
    for nm_b, cot_b in zip(blocks_of(nm), cots):
        if blocks:
            nm_b = after(nm_b, gmids[-1])
        hid, gpre, out_b, gmid_b = mlp(nm_b, cot_b, fc1_weight, row(fc1_bias), fc2_weight)
        blocks.append((nm_b, cot_b, hid, gpre))
        outs.append(out_b)
        gmids.append(gmid_b)
    gmid_own, gmid_peer = own_sums(gmids)
    gb1, *g_mlp = mlp_weights(fast, me, blocks)
    outs = own_sums(outs)
    gmid_peer = after(gmid_peer, gb1)
    gmiddle, branch, sums2 = middle_back(gmid_own, gmid_peer, middle, cot, ln2[0])
    branches = blocks_of(branch)
    if fast:
        keep1, send1, keep2, send2 = g_mlp
        got1, got2 = after(flip(send1, CORE), branch), after(flip(send2, CORE), branch)
        side1, side2 = side_send(keep1, got1), side_send(keep2, got2)
        branches[0] = after(branches[0], side1, side2)
    backs, gparts = [], []
    for b, kept_b in enumerate(kept):
        if b == 1 and fast:
            side1 = after(flip(side1, SIDE), gparts[0])
            line1 = line_sends(keep1, got1, side1)
            branches[1] = after(branches[1], *line1, gparts[0])
        *back, gpart, gsum = attn_backward(windows, branches[b], xs[b], kept_b[:4], qkv, proj)
        backs.append((*back, gsum))
        gparts.append(gpart)
    if fast:
        side2 = after(flip(side2, SIDE), gparts[1])
        line2 = line_sends(keep2, got2, side2)
        line1 = [after(r, gparts[1]) for r in flip_line(line1)]
        piece1 = own_piece(keep1, got1, side1, line1)
        branches[0] = after(branches[0], piece1, *line2, outs[1])
    *g_attn, small = attn_weights(
        fast, me, sums2, gb1, [(k[5], k[4], br, *back) for k, br, back in zip(kept, branches, backs)])
    gnorms = own_sums(gparts)
    gpatch = input_back(*gnorms, x, ln1[0], gmiddle)
    output = (middle + outs[0].astype(F32) + outs[1].astype(F32) + row(fc2_bias)).astype(BF)

    if fast:
        line2 = [after(r, small) for r in flip_line(line2)]
        piece2 = own_piece(keep2, got2, side2, line2)
        keep, send = g_attn
        got = flip(after(send, piece2), CORE)
        side = flip(side_send(keep, got), SIDE)
        fc = jnp.concatenate([piece1, piece2, small], axis=0)
        fc_quad = jnp.stack([fc] + [after(r, output, gpatch) for r in flip_line([fc] * 3)])
        side = after(side, fc_quad, output, gpatch)
        line = flip_line(line_sends(keep, got, side))
        piece = own_piece(keep, got, side, line)
        quad = jnp.stack([piece] + flip_line([piece] * 3))
        fc_pair = after(flip(fc_quad, SIDE), quad)
        g_fc1, g_fc2, small = finish_mlp(me, (fc_quad, fc_pair, after(flip(fc_quad, CORE), quad), after(flip(fc_pair, CORE), quad)))
        totals = small[0:6] + across(small[0:6])
        pair = after(flip(quad, SIDE), totals)
        gw, gproj = finish(me, (quad, pair, flip(quad, CORE), flip(pair, CORE)),
                           shape_of(3, features, width), shape_of(width, features))
    else:
        g_fc1, g_fc2, gw, gproj = [g.astype(F32) for g in lax.psum((*g_mlp, *g_attn), "dp")]
        gw, gproj = gw[:, :, :width], gproj[:width]
        small = lax.psum(small, "dp").astype(F32)
        totals = lax.psum(small[0:6], "mp")
    padded = width + extra
    gqv = jnp.stack([small[6, :width], small[6, padded : padded + width]])
    gb1 = small[7:12].reshape(-1)[: gb1.size]
    gt = small[12:].reshape(12, 2 * LANES)[:heads, :REL].T

    unrow = lambda a: a.reshape(WIN, windows, features).transpose(1, 0, 2)
    return (
        unrow(output),
        unrow(gpatch),
        totals[0],
        totals[1],
        gw.transpose(1, 0, 2),
        gqv,
        gt,
        gproj,
        totals[4],
        totals[2],
        totals[3],
        g_fc1,
        gb1,
        g_fc2,
        totals[5],
    )


def solution(mesh):
    placed = (
        P(("dp", "mp"), None, None),
        P(("dp", "mp"), None),
        P(),
        P(),
        P(None, None, "mp"),
        P(None, "mp"),
        P(None, "mp"),
        P("mp", None),
        P(),
        P(),
        P(),
        P(None, "mp"),
        P("mp"),
        P("mp", None),
        P(),
        P(("dp", "mp"), None, None),
    )
    return jax.shard_map(
        functools.partial(shards, mesh.shape["dp"], mesh.shape["mp"]),
        mesh=mesh,
        in_specs=placed,
        out_specs=(
            P(("dp", "mp"), None, None),
            P(("dp", "mp"), None, None),
            P(),
            P(),
            P(None, None, "mp"),
            P(None, "mp"),
            P(None, "mp"),
            P("mp", None),
            P(),
            P(),
            P(),
            P(None, "mp"),
            P("mp"),
            P("mp", None),
            P(),
        ),
        check_vma=False,
    )
```

```python
import functools

import jax
import jax.numpy as jnp
from jax import lax
from jax.experimental import pallas as pl
from jax.experimental.pallas import tpu as pltpu
from jax.sharding import PartitionSpec as P

HEAD = 32
WSIDE = 7
WIN = 49
REL = 169
SLOT = 64
GROUP = 4
LANES = 128
EPS = 1e-05
SCALING = HEAD ** (-0.5)
BF = jnp.bfloat16
F32 = jnp.float32
HIGH = lax.Precision.HIGHEST
VMEM_LIMIT = 28 * 1024 * 1024
ALL_VMEM = 58 * 1024 * 1024
BLOCK = 96
CORE, SIDE, LINE = 1, 2, 4

ROW_COL = (((1,), (0,)), ((), ()))
LAST_LAST = (((1,), (1,)), ((), ()))
ROWS_ROWS = (((0,), (0,)), ((), ()))


def mm(a, b, dims=ROW_COL):
    return lax.dot_general(a, b, dims, preferred_element_type=F32)


def norm_parts(rows):
    mean = jnp.mean(rows, axis=-1, keepdims=True)
    centred = rows - mean
    variance = jnp.mean(centred * centred, axis=-1, keepdims=True)
    inv = lax.rsqrt(variance + EPS)
    return centred * inv, inv


def norm_back(xhat, inv, gain, upstream):
    z = upstream * gain
    mean_z = jnp.mean(z, axis=-1, keepdims=True)
    mean_zx = jnp.mean(z * xhat, axis=-1, keepdims=True)
    return (z - mean_z - xhat * mean_zx) * inv


def head_masks():
    lane = lax.broadcasted_iota(jnp.int32, (SLOT, LANES), 1)
    return [jnp.where((lane >> 5) == h, 1.0, 0.0).astype(BF) for h in range(GROUP)]


def block_ones():
    row = lax.broadcasted_iota(jnp.int32, (GROUP * SLOT, GROUP * SLOT), 0)
    col = lax.broadcasted_iota(jnp.int32, (GROUP * SLOT, GROUP * SLOT), 1)
    return jnp.where((row >> 6) == (col >> 6), 1.0, 0.0).astype(BF)


def spread(tile, masks):
    return jnp.concatenate([tile * m for m in masks], axis=0)


def collect(full, masks_f):
    total = full[0:SLOT] * masks_f[0]
    for h in range(1, GROUP):
        total = total + full[h * SLOT : (h + 1) * SLOT] * masks_f[h]
    return total


def fill(scratch, rows, windows):
    pitch = windows + 1
    for g in range(scratch.shape[0]):
        for place in range(WIN):
            scratch[g, place * pitch : place * pitch + windows, :] = rows[
                place * windows : (place + 1) * windows, g * LANES : (g + 1) * LANES]
        scratch[g, WIN * pitch :, :] = jnp.zeros((scratch.shape[1] - WIN * pitch, LANES), rows.dtype)


def empty(scratch, windows):
    pitch = windows + 1
    planes = [
        jnp.concatenate([scratch[g, place * pitch : place * pitch + windows, :] for place in range(WIN)], axis=0)
        for g in range(scratch.shape[0])
    ]
    return jnp.concatenate(planes, axis=1).astype(BF)


def row_max(tile, low_half):
    low = jnp.max(jnp.where(low_half, tile, -3e38), axis=-1, keepdims=True)
    high = jnp.max(jnp.where(low_half, -3e38, tile), axis=-1, keepdims=True)
    return jnp.where(low_half, low, high)


def row_sum(tile, low_half):
    low = jnp.sum(jnp.where(low_half, tile, 0.0), axis=-1, keepdims=True)
    high = jnp.sum(jnp.where(low_half, 0.0, tile), axis=-1, keepdims=True)
    return jnp.where(low_half, low, high)


def ds(start, size):
    unit = 384 if size % 384 == 0 else 48
    return pl.ds(pl.multiple_of(start, unit), size)


def each_block(me, *by_core):
    for c_rel, target in enumerate(by_core):
        for y_rel in range(2):
            for z_rel in range(4):
                yield target, y_rel, z_rel, (me & 1) ^ c_rel, ((me >> 1) & 1) ^ y_rel, (me >> 2) ^ z_rel


def line(ref):
    return ref[...].reshape(1, -1)


def begin(sems, *pairs):
    copies = [pltpu.make_async_copy(a, b, sems.at[i]) for i, (a, b) in enumerate(pairs)]
    for copy in copies:
        copy.start()
    return copies


def finish_all(copies):
    for copy in copies:
        copy.wait()


def attn_forward_kernel(windows, x_in, gain_ref, shift_ref, w_in, bias_ref, pos_ref, valid_ref,
                        prob_ref, q_ref, k_ref, v_ref, mixed_ref, normed_t_ref,
                        mask_s, q_s, k_s, v_s, mixed_s, x_ref, w_ref, in_sems):
    copies = begin(in_sems, (x_in, x_ref), *[(w_in.at[p], w_ref.at[p]) for p in range(3)])
    mask_s[...] = jnp.zeros(mask_s.shape, F32)
    for h in range(GROUP):
        mask_s[:, h * SLOT : h * SLOT + WIN] = valid_ref[...].astype(F32)
    masks = head_masks()
    ones = block_ones()
    low_half = lax.broadcasted_iota(jnp.int32, (SLOT, LANES), 1) < SLOT
    copies[0].wait()
    x = x_ref[...].astype(F32)
    rows = x.shape[0]
    groups = q_s.shape[0]
    xhat, _ = norm_parts(x)
    normed = (xhat * line(gain_ref) + line(shift_ref)).astype(BF)
    normed_t_ref[...] = normed.T
    for part, scratch in enumerate((q_s, k_s, v_s)):
        copies[1 + part].wait()
        got = mm(normed, w_ref[part])
        if part != 1:
            got = got + bias_ref[part // 2 : part // 2 + 1, :]
        fill(scratch, got.astype(BF).astype(F32), windows)

    def window(w, carry):
        allowed = jnp.broadcast_to(mask_s[pl.ds(w, 1), :], (SLOT, GROUP * SLOT)) > 0.5
        for g in range(groups):
            cols = slice(g * LANES, (g + 1) * LANES)
            places = pl.ds(w, SLOT, stride=windows + 1)
            q = q_s[g, places, :].astype(BF)
            k = k_s[g, places, :].astype(BF)
            v = v_s[g, places, :].astype(BF)
            q_ref[w, :, cols] = q
            k_ref[w, :, cols] = k
            v_ref[w, :, cols] = v
            scores = mm(q, spread(k, masks), LAST_LAST) * SCALING + pos_ref[g]
            scores = jnp.where(allowed, scores, -1000000000.0)
            top = jnp.concatenate([row_max(scores[:, :LANES], low_half), row_max(scores[:, LANES:], low_half)], axis=1)
            e = jnp.exp(scores - top)
            total = mm(e.astype(BF), ones)
            inv = pl.reciprocal(total, approx=True)
            prob = (e * (inv * (2.0 - total * inv))).astype(BF)
            prob_ref[w, g] = prob
            mixed_s[g, places, :] = mm(prob, spread(v, masks))
        return carry

    lax.fori_loop(0, windows, window, 0, unroll=2)
    mixed_ref[...] = empty(mixed_s, windows)


def middle_kernel(heads, me_ref, x_in, own_in, peer_in, bias_ref, gain_ref, shift_ref, *refs):
    if heads:
        half_in, rest_in, middle_ref, nm_ref, x_ref, own_ref, peer_ref, proj_ref, sems = refs
        lines = half_in.shape[0]
        core = me_ref[0] & 1
        place = lambda c: proj_ref.at[pl.ds(pl.multiple_of(c * lines, lines), lines), :]
        copies = begin(sems, (peer_in, peer_ref), (half_in, place(core)), (rest_in, place(1 - core)), (x_in, x_ref),
                       (own_in, own_ref))
        finish_all(copies[:3])
        peer = mm(peer_ref[...], proj_ref[...])
        finish_all(copies[3:])
    else:
        middle_ref, nm_ref, x_ref, own_ref, peer_ref, sems = refs
        finish_all(begin(sems, (x_in, x_ref), (own_in, own_ref), (peer_in, peer_ref)))
        peer = peer_ref[...].astype(F32)
    middle = x_ref[...].astype(F32) + (own_ref[...].astype(F32) + peer) + line(bias_ref)
    middle_ref[...] = middle
    xhat, _ = norm_parts(middle)
    nm_ref[...] = (xhat * line(gain_ref) + line(shift_ref)).astype(BF)


def mlp_kernel(nm_ref, cot_ref, fc1_ref, b1_ref, fc2_ref, hid_ref, gpre_ref, out_ref, gmid_ref):
    hidden_size = fc1_ref.shape[1]
    features = fc1_ref.shape[0]
    step = 256 if hidden_size % 256 == 0 else 128
    count = hidden_size // step

    nm = nm_ref[...]
    cot = cot_ref[...]

    def units(c, carry):
        cols = pl.ds(pl.multiple_of(c * step, step), step)
        pre = mm(nm, fc1_ref[:, cols]) + b1_ref[:, cols]
        phi = 0.5 * (1.0 + lax.erf(pre * (0.5 ** 0.5)))
        hid_ref[:, cols] = (pre * phi).astype(BF)
        slope = phi + pre * (jnp.exp(-0.5 * pre * pre) * 0.3989422804014327)
        gpre_ref[:, cols] = (mm(cot, fc2_ref[cols, :], LAST_LAST) * slope).astype(BF)
        return carry

    lax.fori_loop(0, count, units, 0)

    def tile(c, carry):
        cols = pl.ds(pl.multiple_of(c * 256, 256), 256)
        gmid_ref[:, cols] = mm(gpre_ref[...], fc1_ref[cols, :], LAST_LAST).astype(BF)
        out_ref[:, cols] = mm(hid_ref[...], fc2_ref[:, cols]).astype(BF)
        return carry

    lax.fori_loop(0, features // 256, tile, 0)

def mlp_weights_kernel(count, split, me_ref, *refs):
    inputs, refs = refs[: 4 * count], refs[4 * count :]
    n_out = 5 if split else 3
    gb1_ref, *outs = refs[:n_out]
    held = refs[n_out : n_out + 4 * count]
    nts = refs[n_out + 4 * count : n_out + 5 * count]
    g1_ref, g2_ref, in_sems, unit_sems, out_sems = refs[n_out + 5 * count :]
    blocks = [held[4 * b : 4 * b + 4] for b in range(count)]
    hidden_size = g1_ref.shape[1]
    features = g1_ref.shape[0]
    step = 384 if hidden_size % 384 == 0 else 128
    wide = features if hidden_size % features == 0 else step

    def units_in(j):
        cols = ds(j * step, step)
        return [pltpu.make_async_copy(inputs[4 * b + 2].at[:, cols], held[4 * b + 2].at[:, cols], unit_sems.at[b, j])
                for b in range(count)]

    order = [4 * b + k for k in (0, 1) for b in range(count)]
    copies = dict(zip(order, begin(in_sems, *[(inputs[i], held[i]) for i in order])))
    for j in range(hidden_size // step):
        for copy in units_in(j):
            copy.start()
    last = [pltpu.make_async_copy(inputs[4 * b + 3], held[4 * b + 3], in_sems.at[2 * count + b]) for b in range(count)]
    for copy in last:
        copy.start()
    finish_all([copies[4 * b] for b in range(count)])
    for block, nt in zip(blocks, nts):
        nt[...] = block[0][...].T
    finish_all([copies[4 * b + 1] for b in range(count)])

    def second(j, carry):
        finish_all(units_in(j))
        cols = ds(j * step, step)
        g2_ref[cols, :] = sum(mm(hid_ref[:, cols], cot_ref[...], ROWS_ROWS) for _, cot_ref, hid_ref, _ in blocks).astype(BF)
        return carry

    def first(j, carry):
        cols = ds(j * wide, wide)
        g1_ref[:, cols] = sum(mm(nt[...], block[3][:, cols]) for nt, block in zip(nts, blocks)).astype(BF)
        return carry

    lax.fori_loop(0, hidden_size // step, second, 0)
    me = me_ref[0]
    sent = []

    def send(k, source, target):
        sent.append(pltpu.make_async_copy(source, target, out_sems.at[k]))
        sent[-1].start()

    if split:
        for i, (target, y_rel, z_rel, c, y, z) in enumerate(each_block(me, outs[2], outs[3])):
            send(i, g2_ref.at[ds(c * 768 + y * 384 + z * 96, 96), :], target.at[y_rel, z_rel])
    else:
        send(0, g2_ref, outs[1])
    finish_all(last)
    gb1_ref[...] = sum(jnp.sum(block[3][...].astype(F32), axis=0, keepdims=True) for block in blocks)
    lax.fori_loop(0, hidden_size // wide, first, 0)
    if split:
        for i, (target, y_rel, z_rel, c, y, z) in enumerate(each_block(me, outs[0], outs[1])):
            send(16 + i, g1_ref.at[ds(y * 384 + z * 96, 96), ds(c * 768, 768)], target.at[y_rel, z_rel])
    else:
        send(1, g1_ref, outs[0])
    finish_all(sent)


def middle_back_kernel(own_ref, peer_ref, middle_ref, cot_ref, gain_ref, gmiddle_ref, branch_ref, sums_ref):
    upstream = cot_ref[...].astype(F32)
    xhat, inv = norm_parts(middle_ref[...])
    gmid = own_ref[...].astype(F32) + peer_ref[...].astype(F32)
    sums_ref[0:1, :] = jnp.sum(gmid * xhat, axis=0, keepdims=True)
    sums_ref[1:2, :] = jnp.sum(gmid, axis=0, keepdims=True)
    gmiddle = upstream + norm_back(xhat, inv, line(gain_ref), gmid)
    gmiddle_ref[...] = gmiddle
    branch_ref[...] = gmiddle.astype(BF)
    sums_ref[2:3, :] = jnp.sum(gmiddle, axis=0, keepdims=True)
    sums_ref[3:4, :] = jnp.sum(upstream, axis=0, keepdims=True)


def attn_backward_kernel(windows, branch_ref, x_ref, prob_ref, q_ref, k_ref, v_ref, w_ref, proj_ref,
                         grads_ref, gqv_ref, gpos_ref, part_ref, sums_ref, gm_s, gq_s, gk_s, gv_s):
    rows = branch_ref.shape[0]
    groups = gm_s.shape[0]
    gpos_ref[...] = jnp.zeros(gpos_ref.shape, F32)
    masks = head_masks()
    masks_f = [m.astype(F32) for m in masks]
    low_half = lax.broadcasted_iota(jnp.int32, (SLOT, LANES), 1) < SLOT
    fill(gm_s, mm(branch_ref[...], proj_ref[...], LAST_LAST).astype(BF).astype(F32), windows)

    def window(w, carry):
        for g in range(groups):
            cols = slice(g * LANES, (g + 1) * LANES)
            places = pl.ds(w, SLOT, stride=windows + 1)
            gm = gm_s[g, places, :].astype(BF)
            q = q_ref[w, :, cols]
            k = k_ref[w, :, cols]
            v = v_ref[w, :, cols]
            prob = prob_ref[w, g]
            prob_f = prob.astype(F32)
            gprob = mm(gm, spread(v, masks), LAST_LAST)
            both = prob_f * gprob
            delta = jnp.concatenate([row_sum(both[:, :LANES], low_half), row_sum(both[:, LANES:], low_half)], axis=1)
            gs = (both - prob_f * delta).astype(BF)
            gpos_ref[g] += gs.astype(F32)
            gq_s[g, places, :] = mm(gs, spread(k, masks)) * SCALING
            gk_s[g, places, :] = collect(mm(gs, q, ROWS_ROWS), masks_f) * SCALING
            gv_s[g, places, :] = collect(mm(prob, gm, ROWS_ROWS), masks_f)
        return carry

    lax.fori_loop(0, windows, window, 0, unroll=2)
    back = None
    for part, scratch in enumerate((gq_s, gk_s, gv_s)):
        grad = empty(scratch, windows)
        grads_ref[part] = grad
        if part != 1:
            width = grad.shape[1]
            lanes = slice(part // 2 * width, (part // 2 + 1) * width)
            gqv_ref[:, lanes] = jnp.sum(grad.astype(F32), axis=0, keepdims=True)
        term = mm(grad, w_ref[part], LAST_LAST)
        back = term if back is None else back + term
    part_ref[...] = back.astype(BF)
    xhat, _ = norm_parts(x_ref[...].astype(F32))
    sums_ref[0:1, :] = jnp.sum(back * xhat, axis=0, keepdims=True)
    sums_ref[1:2, :] = jnp.sum(back, axis=0, keepdims=True)


def place_offset(i):
    return i // WSIDE * (2 * WSIDE - 1) + i % WSIDE


def offset_picks():
    row = lax.broadcasted_iota(jnp.int32, (2 * LANES, 2 * SLOT), 0)
    col = lax.broadcasted_iota(jnp.int32, (2 * LANES, 2 * SLOT), 1)
    j = col & (SLOT - 1)
    line = (j * 37) >> 8
    offset = place_offset(WIN - 1) - line * (2 * WSIDE - 1) - (j - line * WSIDE)
    hit = ((row & (LANES - 1)) == offset) & ((row >> 7) == (col >> 6)) & (j < WIN)
    return jnp.where(hit, 1.0, 0.0).astype(BF)


def position_kernel(table_ref, pos_ref, table_s, rows_s):
    heads = table_ref.shape[0]
    table_s[...] = jnp.zeros(table_s.shape, F32)
    table_s[0:heads, 0:REL] = table_ref[...]
    table = table_s[...]
    lines = table.shape[0]
    rows_s[WIN * lines :, :] = jnp.zeros((rows_s.shape[0] - WIN * lines, LANES), F32)
    for i in range(WIN):
        turned = pltpu.roll(table, (2 * LANES - place_offset(i)) % (2 * LANES), 1)
        rows_s[i * lines : (i + 1) * lines, :] = turned[:, :LANES]
    picks = offset_picks()
    for pair in range(pos_ref.shape[0] * 2):
        pieces = [rows_s[pl.ds(2 * pair + k, SLOT, stride=lines), :] for k in range(2)]
        rest = jnp.concatenate(pieces, axis=1)
        total = jnp.zeros((SLOT, 2 * SLOT), F32)
        for _ in range(3):
            top = rest.astype(BF)
            total = total + mm(top, picks)
            rest = rest - top.astype(F32)
        pos_ref[pair // 2, :, pair % 2 * LANES : (pair % 2 + 1) * LANES] = total


def attn_weights_kernel(count, split, me_ref, sums2_ref, gb1_ref, *refs):
    blocks, refs = [refs[7 * b : 7 * b + 7] for b in range(count)], refs[7 * count :]
    *outs, small_ref = refs[:3]
    gw_ref, gproj_ref, rows_s, out_sems = refs[3:]
    gproj, gqv, gpos, sums = 0.0, 0.0, 0.0, 0.0
    for _, mixed_ref, branch_ref, _, gqv_ref, gpos_ref, sums_ref in blocks:
        gproj = gproj + mm(mixed_ref[...], branch_ref[...], ROWS_ROWS)
        gqv, gpos, sums = gqv + gqv_ref[...], gpos + gpos_ref[...], sums + sums_ref[...]
    width, features = gproj.shape
    gproj_ref[...] = gproj.astype(BF)
    hidden = gb1_ref.shape[1]
    lines = [sums[k : k + 1] for k in range(2)] + [sums2_ref[k : k + 1, :] for k in range(4)]
    lines.append(gqv)
    lines += [gb1_ref[:, k : min(k + features, hidden)] for k in range(0, hidden, features)]
    small = jnp.concatenate(
        [jnp.concatenate([line, jnp.zeros((1, features - line.shape[1]), F32)], axis=1) if line.shape[1] < features else line
         for line in lines] + [jnp.zeros((12 - len(lines), features), F32)], axis=0)
    picks = offset_picks()
    for pair in range(gpos.shape[0] * 2):
        rest = gpos[pair // 2][:, pair % 2 * LANES : (pair % 2 + 1) * LANES]
        total = jnp.zeros((SLOT, 2 * LANES), F32)
        for _ in range(2):
            top = rest.astype(BF)
            total = total + mm(top, picks, LAST_LAST)
            rest = rest - top.astype(F32)
        for k in range(2):
            rows_s[pl.ds(2 * pair + k, SLOT, stride=16), :] = total[:, k * LANES : (k + 1) * LANES]
    for h in range(gpos.shape[0] * 4, 16):
        rows_s[pl.ds(h, SLOT, stride=16), :] = jnp.zeros((SLOT, LANES), F32)
    table = jnp.zeros((16, 2 * LANES), F32)
    for i in range(WIN):
        row = jnp.concatenate([rows_s[i * 16 : (i + 1) * 16, :], jnp.zeros((16, LANES), F32)], axis=1)
        table = table + (pltpu.roll(row, place_offset(i), 1) if i else row)
    packed = [jnp.concatenate([table[3 * r + k : 3 * r + k + 1] for k in range(3)], axis=1) for r in range(4)]
    small_ref[...] = jnp.concatenate([small] + packed, axis=0).astype(BF)
    sent = []

    def send(k, source, target):
        sent.append(pltpu.make_async_copy(source, target, out_sems.at[k]))
        sent[-1].start()

    if split:
        for i, (target, y_rel, z_rel, c, y, z) in enumerate(each_block(me_ref[0], *outs)):
            send(i, gproj_ref.at[ds((c * 4 + y * 2 + (z >> 1)) * 48, 48), ds((z & 1) * 384, 384)],
                 target.at[y_rel, z_rel, 48:96, 384:768])
    else:
        send(0, gproj_ref, outs[1])
    for part in range(3):
        gw = 0.0
        for normed_t_ref, _, _, grads_ref, _, _, _ in blocks:
            gw = gw + mm(normed_t_ref[...], grads_ref[part])
        gw_ref[part] = gw.astype(BF)
        if split:
            for i, (target, y_rel, z_rel, c, y, z) in enumerate(each_block(me_ref[0], *outs)):
                send(16 * (part + 1) + i, gw_ref.at[part, ds(c * 384 + y * 192 + z * 48, 48), :],
                     target.at[y_rel, z_rel, part // 2 * 48 : part // 2 * 48 + 48, part % 2 * 384 : part % 2 * 384 + 384])
        else:
            send(1 + part, gw_ref.at[part], outs[0].at[part])
    finish_all(sent)


def input_back_kernel(own_ref, peer_ref, x_ref, gain_ref, gmiddle_ref, gpatch_ref):
    gnorm = own_ref[...].astype(F32) + peer_ref[...].astype(F32)
    xhat, inv = norm_parts(x_ref[...].astype(F32))
    gpatch_ref[...] = (gmiddle_ref[...] + norm_back(xhat, inv, line(gain_ref), gnorm)).astype(BF)


def finish_kernel(me_ref, *refs):
    sources, outs, held, wide, (in_sems, out_sems) = refs[:4], refs[4:6], refs[6:10], refs[10:12], refs[12:]
    copies = begin(in_sems, *zip(sources, held))
    sent = []

    def put(value, k, where):
        wide[k][where] = value.astype(F32)
        sent.append(pltpu.make_async_copy(wide[k].at[where], outs[k].at[where], out_sems.at[len(sent)]))
        sent[-1].start()

    for source, y_rel, z_rel, c, y, z in each_block(me_ref[0], (0, 1), (2, 3)):
        source = source[y_rel]
        if z_rel == 0:
            copies[source].wait()
        piece = held[source].at[z_rel]
        lines = ds(c * 384 + y * 192 + z * 48, 48)
        put(piece[0:48, 0:384], 0, (0, lines, slice(None)))
        put(piece[0:48, 384:768], 0, (1, lines, slice(None)))
        put(piece[48:96, 0:384], 0, (2, lines, slice(None)))
        put(piece[48:96, 384:768], 1, (ds((c * 4 + y * 2 + (z >> 1)) * 48, 48), ds((z & 1) * 384, 384)))
    finish_all(sent)


def finish_mlp_kernel(me_ref, *refs):
    sources, (g1_out, g2_out, small_ref), held, (g1_ref, g2_ref, small_s, in_sems, out_sems) = (
        refs[:4], refs[4:7], refs[7:11], refs[11:])
    copies = begin(in_sems, *zip(sources, held))
    sent = []

    def put(value, k, wide, out, where):
        wide[where] = value.astype(F32)
        sent.append(pltpu.make_async_copy(wide.at[where], out.at[where], out_sems.at[k, len(sent) // 2]))
        sent[-1].start()

    for source, y_rel, z_rel, c, y, z in each_block(me_ref[0], (0, 1), (2, 3)):
        source = source[y_rel]
        if z_rel == 0:
            copies[source].wait()
        piece = held[source].at[z_rel]
        put(piece[0:BLOCK, :], 0, g1_ref, g1_out, (ds(y * 384 + z * 96, 96), ds(c * 768, 768)))
        put(piece[BLOCK : 2 * BLOCK, :], 1, g2_ref, g2_out, (ds(c * 768 + y * 384 + z * 96, 96), slice(None)))
        small_s[z * 4 + y * 2 + c] = piece[2 * BLOCK :, :].astype(F32)
    total = small_s[0]
    for d in range(1, 16):
        total = total + small_s[d]
    small_ref[...] = total
    finish_all(sent)


def shape_of(*dims, dtype=F32):
    return jax.ShapeDtypeStruct(dims, dtype)


def call(kernel, outs, scratch, name, flops, smem, *args, far=(), far_outs=(), limit=VMEM_LIMIT):
    space = lambda is_far: pl.BlockSpec(memory_space=pltpu.HBM if is_far else pltpu.VMEM)
    in_specs = [pl.BlockSpec(memory_space=pltpu.SMEM)] * len(smem) + [space(i in far) for i in range(len(args))]
    return pl.pallas_call(
        kernel,
        out_shape=outs,
        in_specs=in_specs,
        out_specs=[space(i in far_outs) for i in range(len(outs))],
        scratch_shapes=scratch,
        compiler_params=pltpu.CompilerParams(vmem_limit_bytes=limit),
        cost_estimate=pl.CostEstimate(flops=flops, bytes_accessed=flops // 256, transcendentals=0),
        name=name,
    )(*smem, *args)


def like(*arrays):
    return [pltpu.VMEM(a.shape, a.dtype) for a in arrays]


def dma(*counts):
    return [pltpu.SemaphoreType.DMA(c if isinstance(c, tuple) else (c,)) for c in counts]


SMALL = 1000000


def position(table):
    heads = table.shape[0]
    groups = -(-heads // GROUP)
    return call(position_kernel, [shape_of(groups, SLOT, GROUP * SLOT)],
                [pltpu.VMEM((16, 2 * LANES), F32), pltpu.VMEM((16 * SLOT, LANES), F32)], "position", SMALL, (), table)[0]


def attn_forward(windows, x, ln1, qkv, qv_bias, pos, mask):
    rows, features = x.shape
    width = qkv.shape[2]
    groups = width // LANES
    tile = shape_of(windows, SLOT, width, dtype=BF)
    outs = [shape_of(windows, groups, SLOT, GROUP * SLOT, dtype=BF), tile, tile, tile, shape_of(rows, width, dtype=BF),
            shape_of(features, rows, dtype=BF)]
    scratch = [pltpu.VMEM((windows, GROUP * SLOT), F32)] + [pltpu.VMEM((groups, SLOT * (windows + 1), LANES), F32)] * 4
    scratch += like(x, qkv) + dma(4)
    return call(functools.partial(attn_forward_kernel, windows), outs, scratch, "attn_forward", SMALL, (),
                x, *ln1, qkv, qv_bias, pos, mask, far=(0, 3), limit=ALL_VMEM)


def middle_norm(me, x, own, peer, bias, ln2, halves):
    rows, features = x.shape
    scratch = like(x, own, peer)
    if halves:
        scratch += [pltpu.VMEM((2 * halves[0].shape[0], features), BF)]
    return call(functools.partial(middle_kernel, bool(halves)), [shape_of(rows, features), shape_of(rows, features, dtype=BF)],
                scratch + dma(5), "middle", SMALL, (me,), x, own, peer, bias, *ln2, *halves, far=(0, 1, 2, 6, 7),
                limit=ALL_VMEM)


def mlp(nm, cot, fc1, fc1_bias, fc2):
    rows, features = nm.shape
    hidden = fc2.shape[0]
    outs = [shape_of(rows, hidden, dtype=BF)] * 2 + [shape_of(rows, features, dtype=BF)] * 2
    return call(mlp_kernel, outs, [], "mlp", SMALL, (), nm, cot, fc1, fc1_bias, fc2)


def mlp_weights(split, me, blocks):
    rows, features = blocks[0][0].shape
    hidden = blocks[0][2].shape[1]
    grads = [shape_of(features, hidden, dtype=BF), shape_of(hidden, features, dtype=BF)]
    outs = [shape_of(1, hidden)] + ([shape_of(2, 4, BLOCK, features, dtype=BF)] * 4 if split else grads)
    flat = [a for b in blocks for a in b]
    scratch = like(*flat) + [pltpu.VMEM((features, rows), BF)] * len(blocks) + like(*grads) + dma(3 * len(blocks), (len(blocks), hidden // 128), 32)
    return call(functools.partial(mlp_weights_kernel, len(blocks), split), outs, scratch, "mlp_weights", SMALL,
                (me,), *flat, far=range(len(flat)), far_outs=range(1, len(outs)), limit=ALL_VMEM)


def middle_back(own, peer, middle, cot, gain):
    rows, features = middle.shape
    return call(
        middle_back_kernel, [shape_of(rows, features), shape_of(rows, features, dtype=BF), shape_of(4, features)], [],
        "middle_back", 20000 * SMALL, (), own, peer, middle, cot, gain)


def attn_backward(windows, branch, x, kept, qkv, proj):
    rows, features = branch.shape
    width = proj.shape[0]
    groups = width // LANES
    outs = [shape_of(3, rows, width, dtype=BF), shape_of(1, 2 * width), shape_of(groups, SLOT, GROUP * SLOT),
            shape_of(rows, features, dtype=BF), shape_of(2, features)]
    scratch = [pltpu.VMEM((groups, SLOT * (windows + 1), LANES), F32)] * 4
    return call(functools.partial(attn_backward_kernel, windows), outs, scratch, "attn_backward", SMALL, (),
                branch, x, *kept, qkv, proj)


def attn_weights(split, me, sums2, gb1, blocks):
    features = blocks[0][0].shape[0]
    width = blocks[0][1].shape[1]
    grads = [shape_of(3, features, width, dtype=BF), shape_of(width, features, dtype=BF)]
    outs = ([shape_of(2, 4, BLOCK, features, dtype=BF)] * 2 if split else grads) + [shape_of(16, features, dtype=BF)]
    scratch = like(*grads) + [pltpu.VMEM((16 * SLOT, LANES), F32)]
    flat = [a for b in blocks for a in b]
    return call(functools.partial(attn_weights_kernel, len(blocks), split), outs, scratch + dma(64),
                "attn_weights", SMALL, (me,), sums2, gb1, *flat, far_outs=(0, 1))


def input_back(own, peer, x, gain, gmiddle):
    rows, features = x.shape
    return call(input_back_kernel, [shape_of(rows, features, dtype=BF)], [], "input_back", SMALL, (),
                own, peer, x, gain, gmiddle)[0]


def finish(me, sources, *outs):
    scratch = like(*sources, *outs) + dma(4, 16 * 4)
    return call(finish_kernel, list(outs), scratch, "finish", SMALL, (me,), *sources, far=range(4), far_outs=range(len(outs)))


def finish_mlp(me, sources):
    features = sources[0].shape[2]
    outs = [shape_of(features, 2 * features), shape_of(2 * features, features), shape_of(16, features)]
    scratch = like(*sources, *outs[:2]) + [pltpu.VMEM((16, 16, features), F32)] + dma(4, (2, 16))
    return call(finish_mlp_kernel, outs, scratch, "finish_mlp", SMALL, (me,), *sources, far=range(4), far_outs=(0, 1))


def across(v):
    return lax.ppermute(v, "mp", [(0, 1), (1, 0)])


def flip(v, bits):
    return lax.ppermute(v, "dp", [(i, i ^ bits) for i in range(16)])


def after(v, *others):
    return lax.optimization_barrier((v, *others))[0]


def total_of(terms):
    total = terms[0].astype(F32)
    for t in terms[1:]:
        total = total + t.astype(F32)
    return total.astype(BF)


def side_send(keep, got):
    return total_of([keep[1], got[1]])


def line_sends(keep, got, side):
    return [total_of([keep[0, k], got[0, k], side[k]]) for k in (1, 2, 3)]


def own_piece(keep, got, side, line):
    return total_of([keep[0, 0], got[0, 0], side[0], *line])


def flip_line(pieces):
    return [flip(p, LINE * k) for k, p in zip((1, 2, 3), pieces)]


def sum_line(sends):
    near, far, both = sends
    return [flip(near, LINE), flip(total_of([far, flip(both, LINE)]), 2 * LINE)]


def gather_line(piece):
    far = flip(piece, 2 * LINE)
    return [flip(piece, LINE), far, flip(far, LINE)]


def shards(
    dp_size,
    mp_size,
    patches,
    token_valid,
    ln1_gain,
    ln1_shift,
    qkv_weight,
    qv_bias,
    bias_table,
    proj_weight,
    proj_bias,
    ln2_gain,
    ln2_shift,
    fc1_weight,
    fc1_bias,
    fc2_weight,
    fc2_bias,
    cotangent,
):
    windows, _, features = patches.shape
    rows = windows * WIN
    width = proj_weight.shape[0]
    heads = width // HEAD
    fast = mp_size == 2 and dp_size == 16 and features == 768
    x = patches.transpose(1, 0, 2).reshape(rows, features)
    cot = cotangent.transpose(1, 0, 2).reshape(rows, features)
    row = lambda a: a.reshape(1, -1)
    extra = -width % LANES
    qkv = jnp.pad(qkv_weight.transpose(1, 0, 2), ((0, 0), (0, 0), (0, extra)))
    proj = jnp.pad(proj_weight, ((0, extra), (0, 0)))
    pos = position(bias_table.T)
    bias = jnp.pad(qv_bias, ((0, 0), (0, extra)))
    valid = token_valid.astype(F32)
    ln1, ln2 = (ln1_gain, ln1_shift), (ln2_gain, ln2_shift)

    def blocks_of(v):
        return [v, across(v)] if fast else list(lax.all_gather(v, "mp"))

    def own_sums(parts):
        if fast:
            return parts[0], across(parts[1])
        own = lax.psum_scatter(jnp.concatenate(parts), "mp", scatter_dimension=0, tiled=True)
        return own, jnp.zeros_like(own)

    index = lax.axis_index("dp").astype(jnp.int32)
    me = index.reshape(1)
    valids = blocks_of(valid)
    kept, xs = [], []
    for x_b, valid_b in zip(blocks_of(x), valids):
        if kept:
            x_b = after(x_b, kept[0][4])
        xs.append(x_b)
        kept.append(attn_forward(windows, x_b, ln1, qkv, bias, pos, valid_b))
    project = lambda mixed, weight: jnp.dot(mixed, weight, preferred_element_type=F32).astype(BF)
    if fast:
        core = index & 1
        half = across(lax.dynamic_slice_in_dim(after(proj, valids[1]), core * (width // 2), width // 2, 0))
        cots = [cot, across(after(cot, valids[1]))]
        mixed = across(after(kept[1][4], cots[1], half))
        half = after(half, kept[1][4])
        rest = flip(half, CORE)
        parts, halves = (project(kept[0][4], proj), mixed), (half, rest)
    else:
        parts, halves = own_sums([project(k[4], proj) for k in kept]), ()
        cots = blocks_of(cot)
    middle, nm = middle_norm(me, x, *parts, proj_bias, ln2, halves)

    blocks, outs, gmids = [], [], []
    for nm_b, cot_b in zip(blocks_of(nm), cots):
        if blocks:
            nm_b = after(nm_b, gmids[-1])
        hid, gpre, out_b, gmid_b = mlp(nm_b, cot_b, fc1_weight, row(fc1_bias), fc2_weight)
        blocks.append((nm_b, cot_b, hid, gpre))
        outs.append(out_b)
        gmids.append(gmid_b)
    gmid_own, gmid_peer = own_sums(gmids)
    gb1, *g_mlp = mlp_weights(fast, me, blocks)
    outs = own_sums(outs)
    gmid_peer = after(gmid_peer, gb1)
    gmiddle, branch, sums2 = middle_back(gmid_own, gmid_peer, middle, cot, ln2[0])
    branches = blocks_of(branch)
    if fast:
        keep1, send1, keep2, send2 = g_mlp
        got1, got2 = after(flip(send1, CORE), branch), after(flip(send2, CORE), branch)
        side1, side2 = side_send(keep1, got1), side_send(keep2, got2)
        branches[0] = after(branches[0], side1, side2)
    backs, gparts = [], []
    for b, kept_b in enumerate(kept):
        if b == 1 and fast:
            side1 = after(flip(side1, SIDE), gparts[0])
            line1 = line_sends(keep1, got1, side1)
            branches[1] = after(branches[1], *line1, gparts[0])
        *back, gpart, gsum = attn_backward(windows, branches[b], xs[b], kept_b[:4], qkv, proj)
        backs.append((*back, gsum))
        gparts.append(gpart)
    if fast:
        side2 = after(flip(side2, SIDE), gparts[1])
        line2 = line_sends(keep2, got2, side2)
        line1 = [after(r, gparts[1]) for r in flip_line(line1)]
        piece1 = own_piece(keep1, got1, side1, line1)
        branches[0] = after(branches[0], piece1, *line2, outs[1])
    *g_attn, small = attn_weights(
        fast, me, sums2, gb1, [(k[5], k[4], br, *back) for k, br, back in zip(kept, branches, backs)])
    gnorms = own_sums(gparts)
    gpatch = input_back(*gnorms, x, ln1[0], gmiddle)
    output = (middle + outs[0].astype(F32) + outs[1].astype(F32) + row(fc2_bias)).astype(BF)

    if fast:
        line2 = [after(r, small) for r in flip_line(line2)]
        piece2 = own_piece(keep2, got2, side2, line2)
        keep, send = g_attn
        got = flip(after(send, piece2), CORE)
        side = flip(side_send(keep, got), SIDE)
        fc = jnp.concatenate([piece1, piece2, small], axis=0)
        fc_quad = jnp.stack([fc] + [after(r, output, gpatch) for r in gather_line(fc)])
        side = after(side, fc_quad, output, gpatch)
        line = sum_line(line_sends(keep, got, side))
        piece = own_piece(keep, got, side, line)
        quad = jnp.stack([piece] + gather_line(piece))
        fc_pair = after(flip(fc_quad, SIDE), quad)
        g_fc1, g_fc2, small = finish_mlp(me, (fc_quad, fc_pair, after(flip(fc_quad, CORE), quad), after(flip(fc_pair, CORE), quad)))
        totals = small[0:6] + across(small[0:6])
        pair = after(flip(quad, SIDE), totals)
        gw, gproj = finish(me, (quad, pair, flip(quad, CORE), flip(pair, CORE)),
                           shape_of(3, features, width), shape_of(width, features))
    else:
        g_fc1, g_fc2, gw, gproj = [g.astype(F32) for g in lax.psum((*g_mlp, *g_attn), "dp")]
        gw, gproj = gw[:, :, :width], gproj[:width]
        small = lax.psum(small, "dp").astype(F32)
        totals = lax.psum(small[0:6], "mp")
    padded = width + extra
    gqv = jnp.stack([small[6, :width], small[6, padded : padded + width]])
    gb1 = small[7:12].reshape(-1)[: gb1.size]
    gt = small[12:].reshape(12, 2 * LANES)[:heads, :REL].T

    unrow = lambda a: a.reshape(WIN, windows, features).transpose(1, 0, 2)
    return (
        unrow(output),
        unrow(gpatch),
        totals[0],
        totals[1],
        gw.transpose(1, 0, 2),
        gqv,
        gt,
        gproj,
        totals[4],
        totals[2],
        totals[3],
        g_fc1,
        gb1,
        g_fc2,
        totals[5],
    )


def solution(mesh):
    placed = (
        P(("dp", "mp"), None, None),
        P(("dp", "mp"), None),
        P(),
        P(),
        P(None, None, "mp"),
        P(None, "mp"),
        P(None, "mp"),
        P("mp", None),
        P(),
        P(),
        P(),
        P(None, "mp"),
        P("mp"),
        P("mp", None),
        P(),
        P(("dp", "mp"), None, None),
    )
    return jax.shard_map(
        functools.partial(shards, mesh.shape["dp"], mesh.shape["mp"]),
        mesh=mesh,
        in_specs=placed,
        out_specs=(
            P(("dp", "mp"), None, None),
            P(("dp", "mp"), None, None),
            P(),
            P(),
            P(None, None, "mp"),
            P(None, "mp"),
            P(None, "mp"),
            P("mp", None),
            P(),
            P(),
            P(),
            P(None, "mp"),
            P("mp"),
            P("mp", None),
            P(),
        ),
        check_vma=False,
    )
```

```python
import functools

import jax
import jax.numpy as jnp
from jax import lax
from jax.experimental import pallas as pl
from jax.experimental.pallas import tpu as pltpu
from jax.sharding import PartitionSpec as P

HEAD = 32
WSIDE = 7
WIN = 49
REL = 169
SLOT = 64
GROUP = 4
LANES = 128
EPS = 1e-05
SCALING = HEAD ** (-0.5)
BF = jnp.bfloat16
F32 = jnp.float32
HIGH = lax.Precision.HIGHEST
VMEM_LIMIT = 28 * 1024 * 1024
ALL_VMEM = 58 * 1024 * 1024
BLOCK = 96
CORE, SIDE, LINE = 1, 2, 4

ROW_COL = (((1,), (0,)), ((), ()))
LAST_LAST = (((1,), (1,)), ((), ()))
ROWS_ROWS = (((0,), (0,)), ((), ()))


def mm(a, b, dims=ROW_COL):
    return lax.dot_general(a, b, dims, preferred_element_type=F32)


def norm_parts(rows):
    mean = jnp.mean(rows, axis=-1, keepdims=True)
    centred = rows - mean
    variance = jnp.mean(centred * centred, axis=-1, keepdims=True)
    inv = lax.rsqrt(variance + EPS)
    return centred * inv, inv


def norm_back(xhat, inv, gain, upstream):
    z = upstream * gain
    mean_z = jnp.mean(z, axis=-1, keepdims=True)
    mean_zx = jnp.mean(z * xhat, axis=-1, keepdims=True)
    return (z - mean_z - xhat * mean_zx) * inv


def head_masks():
    lane = lax.broadcasted_iota(jnp.int32, (SLOT, LANES), 1)
    return [jnp.where((lane >> 5) == h, 1.0, 0.0).astype(BF) for h in range(GROUP)]


def block_ones():
    row = lax.broadcasted_iota(jnp.int32, (GROUP * SLOT, GROUP * SLOT), 0)
    col = lax.broadcasted_iota(jnp.int32, (GROUP * SLOT, GROUP * SLOT), 1)
    return jnp.where((row >> 6) == (col >> 6), 1.0, 0.0).astype(BF)


def spread(tile, masks):
    return jnp.concatenate([tile * m for m in masks], axis=0)


def collect(full, masks_f):
    total = full[0:SLOT] * masks_f[0]
    for h in range(1, GROUP):
        total = total + full[h * SLOT : (h + 1) * SLOT] * masks_f[h]
    return total


def fill(scratch, rows, windows):
    pitch = windows + 1
    for g in range(scratch.shape[0]):
        for place in range(WIN):
            scratch[g, place * pitch : place * pitch + windows, :] = rows[
                place * windows : (place + 1) * windows, g * LANES : (g + 1) * LANES]
        scratch[g, WIN * pitch :, :] = jnp.zeros((scratch.shape[1] - WIN * pitch, LANES), rows.dtype)


def empty(scratch, windows):
    pitch = windows + 1
    planes = [
        jnp.concatenate([scratch[g, place * pitch : place * pitch + windows, :] for place in range(WIN)], axis=0)
        for g in range(scratch.shape[0])
    ]
    return jnp.concatenate(planes, axis=1).astype(BF)


def row_max(tile, low_half):
    low = jnp.max(jnp.where(low_half, tile, -3e38), axis=-1, keepdims=True)
    high = jnp.max(jnp.where(low_half, -3e38, tile), axis=-1, keepdims=True)
    return jnp.where(low_half, low, high)


def row_sum(tile, low_half):
    low = jnp.sum(jnp.where(low_half, tile, 0.0), axis=-1, keepdims=True)
    high = jnp.sum(jnp.where(low_half, 0.0, tile), axis=-1, keepdims=True)
    return jnp.where(low_half, low, high)


def ds(start, size):
    unit = 384 if size % 384 == 0 else 48
    return pl.ds(pl.multiple_of(start, unit), size)


def each_block(me, *by_core):
    for c_rel, target in enumerate(by_core):
        for y_rel in range(2):
            for z_rel in range(4):
                yield target, y_rel, z_rel, (me & 1) ^ c_rel, ((me >> 1) & 1) ^ y_rel, (me >> 2) ^ z_rel


def line(ref):
    return ref[...].reshape(1, -1)


def begin(sems, *pairs):
    copies = [pltpu.make_async_copy(a, b, sems.at[i]) for i, (a, b) in enumerate(pairs)]
    for copy in copies:
        copy.start()
    return copies


def finish_all(copies):
    for copy in copies:
        copy.wait()


def attn_forward_kernel(windows, x_in, gain_ref, shift_ref, w_in, bias_ref, pos_ref, valid_ref,
                        prob_ref, q_ref, k_ref, v_ref, mixed_ref, normed_t_ref,
                        mask_s, q_s, k_s, v_s, mixed_s, x_ref, w_ref, in_sems):
    copies = begin(in_sems, (x_in, x_ref), *[(w_in.at[p], w_ref.at[p]) for p in range(3)])
    mask_s[...] = jnp.zeros(mask_s.shape, F32)
    for h in range(GROUP):
        mask_s[:, h * SLOT : h * SLOT + WIN] = valid_ref[...].astype(F32)
    masks = head_masks()
    ones = block_ones()
    low_half = lax.broadcasted_iota(jnp.int32, (SLOT, LANES), 1) < SLOT
    copies[0].wait()
    x = x_ref[...].astype(F32)
    rows = x.shape[0]
    groups = q_s.shape[0]
    xhat, _ = norm_parts(x)
    normed = (xhat * line(gain_ref) + line(shift_ref)).astype(BF)
    normed_t_ref[...] = normed.T
    for part, scratch in enumerate((q_s, k_s, v_s)):
        copies[1 + part].wait()
        got = mm(normed, w_ref[part])
        if part != 1:
            got = got + bias_ref[part // 2 : part // 2 + 1, :]
        fill(scratch, got.astype(BF).astype(F32), windows)

    def window(w, carry):
        allowed = jnp.broadcast_to(mask_s[pl.ds(w, 1), :], (SLOT, GROUP * SLOT)) > 0.5
        for g in range(groups):
            cols = slice(g * LANES, (g + 1) * LANES)
            places = pl.ds(w, SLOT, stride=windows + 1)
            q = q_s[g, places, :].astype(BF)
            k = k_s[g, places, :].astype(BF)
            v = v_s[g, places, :].astype(BF)
            q_ref[w, :, cols] = q
            k_ref[w, :, cols] = k
            v_ref[w, :, cols] = v
            scores = mm(q, spread(k, masks), LAST_LAST) * SCALING + pos_ref[g]
            scores = jnp.where(allowed, scores, -1000000000.0)
            top = jnp.concatenate([row_max(scores[:, :LANES], low_half), row_max(scores[:, LANES:], low_half)], axis=1)
            e = jnp.exp(scores - top)
            total = mm(e.astype(BF), ones)
            inv = pl.reciprocal(total, approx=True)
            prob = (e * (inv * (2.0 - total * inv))).astype(BF)
            prob_ref[w, g] = prob
            mixed_s[g, places, :] = mm(prob, spread(v, masks))
        return carry

    lax.fori_loop(0, windows, window, 0, unroll=2)
    mixed_ref[...] = empty(mixed_s, windows)


def middle_kernel(heads, me_ref, x_in, own_in, peer_in, bias_ref, gain_ref, shift_ref, *refs):
    if heads:
        half_in, rest_in, middle_ref, nm_ref, x_ref, own_ref, peer_ref, proj_ref, sems = refs
        lines = half_in.shape[0]
        core = me_ref[0] & 1
        place = lambda c: proj_ref.at[pl.ds(pl.multiple_of(c * lines, lines), lines), :]
        copies = begin(sems, (peer_in, peer_ref), (half_in, place(core)), (rest_in, place(1 - core)), (x_in, x_ref),
                       (own_in, own_ref))
        finish_all(copies[:3])
        peer = mm(peer_ref[...], proj_ref[...])
        finish_all(copies[3:])
    else:
        middle_ref, nm_ref, x_ref, own_ref, peer_ref, sems = refs
        finish_all(begin(sems, (x_in, x_ref), (own_in, own_ref), (peer_in, peer_ref)))
        peer = peer_ref[...].astype(F32)
    middle = x_ref[...].astype(F32) + (own_ref[...].astype(F32) + peer) + line(bias_ref)
    middle_ref[...] = middle
    xhat, _ = norm_parts(middle)
    nm_ref[...] = (xhat * line(gain_ref) + line(shift_ref)).astype(BF)


def mlp_kernel(nm_ref, cot_ref, fc1_ref, b1_ref, fc2_ref, hid_ref, gpre_ref, out_ref, gmid_ref):
    hidden_size = fc1_ref.shape[1]
    features = fc1_ref.shape[0]
    step = 256 if hidden_size % 256 == 0 else 128
    count = hidden_size // step

    nm = nm_ref[...]
    cot = cot_ref[...]

    def units(c, carry):
        cols = pl.ds(pl.multiple_of(c * step, step), step)
        pre = mm(nm, fc1_ref[:, cols]) + b1_ref[:, cols]
        phi = 0.5 * (1.0 + lax.erf(pre * (0.5 ** 0.5)))
        hid_ref[:, cols] = (pre * phi).astype(BF)
        slope = phi + pre * (jnp.exp(-0.5 * pre * pre) * 0.3989422804014327)
        gpre_ref[:, cols] = (mm(cot, fc2_ref[cols, :], LAST_LAST) * slope).astype(BF)
        return carry

    lax.fori_loop(0, count, units, 0)

    def tile(c, carry):
        cols = pl.ds(pl.multiple_of(c * 256, 256), 256)
        gmid_ref[:, cols] = mm(gpre_ref[...], fc1_ref[cols, :], LAST_LAST).astype(BF)
        out_ref[:, cols] = mm(hid_ref[...], fc2_ref[:, cols]).astype(BF)
        return carry

    lax.fori_loop(0, features // 256, tile, 0)

def fc2_weights_kernel(count, split, me_ref, *refs):
    inputs, refs = refs[: 2 * count], refs[2 * count :]
    n_out = 2 if split else 1
    outs, held, (g_ref, in_sems, unit_sems, out_sems) = refs[:n_out], refs[n_out : n_out + 2 * count], refs[n_out + 2 * count :]
    hidden_size = g_ref.shape[0]
    step = 384 if hidden_size % 384 == 0 else 128

    def units_in(j):
        cols = ds(j * step, step)
        return [pltpu.make_async_copy(inputs[2 * b + 1].at[:, cols], held[2 * b + 1].at[:, cols], unit_sems.at[b, j])
                for b in range(count)]

    copies = begin(in_sems, *[(inputs[2 * b], held[2 * b]) for b in range(count)])
    for j in range(hidden_size // step):
        for copy in units_in(j):
            copy.start()
    finish_all(copies)

    def units(j, carry):
        finish_all(units_in(j))
        cols = ds(j * step, step)
        g_ref[cols, :] = sum(
            mm(held[2 * b + 1][:, cols], held[2 * b][...], ROWS_ROWS) for b in range(count)).astype(BF)
        return carry

    lax.fori_loop(0, hidden_size // step, units, 0)
    if split:
        finish_all(begin(out_sems, *[
            (g_ref.at[ds(c * 768 + y * 384 + z * 96, 96), :], target.at[y_rel, z_rel])
            for target, y_rel, z_rel, c, y, z in each_block(me_ref[0], *outs)]))
    else:
        finish_all(begin(out_sems, (g_ref, outs[0])))


def fc1_weights_kernel(count, split, me_ref, *refs):
    inputs, refs = refs[: 2 * count], refs[2 * count :]
    n_out = 3 if split else 2
    (gb1_ref, *outs), held = refs[:n_out], refs[n_out : n_out + 2 * count]
    nts = refs[n_out + 2 * count : n_out + 3 * count]
    g_ref, in_sems, out_sems = refs[n_out + 3 * count :]
    features, hidden_size = g_ref.shape
    wide = features if hidden_size % features == 0 else 128
    copies = begin(in_sems, *[(inputs[2 * b + k], held[2 * b + k]) for k in range(2) for b in range(count)])
    finish_all(copies[:count])
    for b in range(count):
        nts[b][...] = held[2 * b][...].T
    finish_all(copies[count:])
    gb1_ref[...] = sum(jnp.sum(held[2 * b + 1][...].astype(F32), axis=0, keepdims=True) for b in range(count))
    sent = []
    if split:
        moves = [(c_rel, pltpu.make_async_copy(
            g_ref.at[ds(y * 384 + z * 96, 96), ds(c * 768, 768)], target.at[y_rel, z_rel], out_sems.at[i]))
            for i, ((c_rel, target), y_rel, z_rel, c, y, z) in enumerate(each_block(me_ref[0], *enumerate(outs)))]

    def units(j, carry):
        cols = ds(j * wide, wide)
        g_ref[:, cols] = sum(mm(nts[b][...], held[2 * b + 1][:, cols]) for b in range(count)).astype(BF)
        return carry

    if split:
        core = me_ref[0] & 1
        for c_rel in (1, 0):
            units(core ^ c_rel, 0)
            for which, move in moves:
                if which == c_rel:
                    move.start()
        finish_all([move for _, move in moves])
    else:
        lax.fori_loop(0, hidden_size // wide, units, 0)
        finish_all(begin(out_sems, (g_ref, outs[0])))


def middle_back_kernel(own_ref, peer_ref, middle_ref, cot_ref, gain_ref, gmiddle_ref, branch_ref, sums_ref):
    upstream = cot_ref[...].astype(F32)
    xhat, inv = norm_parts(middle_ref[...])
    gmid = own_ref[...].astype(F32) + peer_ref[...].astype(F32)
    sums_ref[0:1, :] = jnp.sum(gmid * xhat, axis=0, keepdims=True)
    sums_ref[1:2, :] = jnp.sum(gmid, axis=0, keepdims=True)
    gmiddle = upstream + norm_back(xhat, inv, line(gain_ref), gmid)
    gmiddle_ref[...] = gmiddle
    branch_ref[...] = gmiddle.astype(BF)
    sums_ref[2:3, :] = jnp.sum(gmiddle, axis=0, keepdims=True)
    sums_ref[3:4, :] = jnp.sum(upstream, axis=0, keepdims=True)


def attn_backward_kernel(windows, branch_ref, x_ref, prob_ref, q_ref, k_ref, v_ref, w_ref, proj_ref,
                         grads_ref, gqv_ref, gpos_ref, part_ref, sums_ref, gm_s, gq_s, gk_s, gv_s):
    rows = branch_ref.shape[0]
    groups = gm_s.shape[0]
    gpos_ref[...] = jnp.zeros(gpos_ref.shape, F32)
    masks = head_masks()
    masks_f = [m.astype(F32) for m in masks]
    low_half = lax.broadcasted_iota(jnp.int32, (SLOT, LANES), 1) < SLOT
    fill(gm_s, mm(branch_ref[...], proj_ref[...], LAST_LAST).astype(BF).astype(F32), windows)

    def window(w, carry):
        for g in range(groups):
            cols = slice(g * LANES, (g + 1) * LANES)
            places = pl.ds(w, SLOT, stride=windows + 1)
            gm = gm_s[g, places, :].astype(BF)
            q = q_ref[w, :, cols]
            k = k_ref[w, :, cols]
            v = v_ref[w, :, cols]
            prob = prob_ref[w, g]
            prob_f = prob.astype(F32)
            gprob = mm(gm, spread(v, masks), LAST_LAST)
            both = prob_f * gprob
            delta = jnp.concatenate([row_sum(both[:, :LANES], low_half), row_sum(both[:, LANES:], low_half)], axis=1)
            gs = (both - prob_f * delta).astype(BF)
            gpos_ref[g] += gs.astype(F32)
            gq_s[g, places, :] = mm(gs, spread(k, masks)) * SCALING
            gk_s[g, places, :] = collect(mm(gs, q, ROWS_ROWS), masks_f) * SCALING
            gv_s[g, places, :] = collect(mm(prob, gm, ROWS_ROWS), masks_f)
        return carry

    lax.fori_loop(0, windows, window, 0, unroll=2)
    back = None
    for part, scratch in enumerate((gq_s, gk_s, gv_s)):
        grad = empty(scratch, windows)
        grads_ref[part] = grad
        if part != 1:
            width = grad.shape[1]
            lanes = slice(part // 2 * width, (part // 2 + 1) * width)
            gqv_ref[:, lanes] = jnp.sum(grad.astype(F32), axis=0, keepdims=True)
        term = mm(grad, w_ref[part], LAST_LAST)
        back = term if back is None else back + term
    part_ref[...] = back.astype(BF)
    xhat, _ = norm_parts(x_ref[...].astype(F32))
    sums_ref[0:1, :] = jnp.sum(back * xhat, axis=0, keepdims=True)
    sums_ref[1:2, :] = jnp.sum(back, axis=0, keepdims=True)


def place_offset(i):
    return i // WSIDE * (2 * WSIDE - 1) + i % WSIDE


def offset_picks():
    row = lax.broadcasted_iota(jnp.int32, (2 * LANES, 2 * SLOT), 0)
    col = lax.broadcasted_iota(jnp.int32, (2 * LANES, 2 * SLOT), 1)
    j = col & (SLOT - 1)
    line = (j * 37) >> 8
    offset = place_offset(WIN - 1) - line * (2 * WSIDE - 1) - (j - line * WSIDE)
    hit = ((row & (LANES - 1)) == offset) & ((row >> 7) == (col >> 6)) & (j < WIN)
    return jnp.where(hit, 1.0, 0.0).astype(BF)


def position_kernel(table_ref, pos_ref, table_s, rows_s):
    heads = table_ref.shape[0]
    table_s[...] = jnp.zeros(table_s.shape, F32)
    table_s[0:heads, 0:REL] = table_ref[...]
    table = table_s[...]
    lines = table.shape[0]
    rows_s[WIN * lines :, :] = jnp.zeros((rows_s.shape[0] - WIN * lines, LANES), F32)
    for i in range(WIN):
        turned = pltpu.roll(table, (2 * LANES - place_offset(i)) % (2 * LANES), 1)
        rows_s[i * lines : (i + 1) * lines, :] = turned[:, :LANES]
    picks = offset_picks()
    for pair in range(pos_ref.shape[0] * 2):
        pieces = [rows_s[pl.ds(2 * pair + k, SLOT, stride=lines), :] for k in range(2)]
        rest = jnp.concatenate(pieces, axis=1)
        total = jnp.zeros((SLOT, 2 * SLOT), F32)
        for _ in range(3):
            top = rest.astype(BF)
            total = total + mm(top, picks)
            rest = rest - top.astype(F32)
        pos_ref[pair // 2, :, pair % 2 * LANES : (pair % 2 + 1) * LANES] = total


def attn_weights_kernel(count, split, me_ref, sums2_ref, gb1_ref, *refs):
    blocks, refs = [refs[7 * b : 7 * b + 7] for b in range(count)], refs[7 * count :]
    *outs, small_ref = refs[:3]
    gw_ref, gproj_ref, rows_s, out_sems = refs[3:]
    gproj, gqv, gpos, sums = 0.0, 0.0, 0.0, 0.0
    for _, mixed_ref, branch_ref, _, gqv_ref, gpos_ref, sums_ref in blocks:
        gproj = gproj + mm(mixed_ref[...], branch_ref[...], ROWS_ROWS)
        gqv, gpos, sums = gqv + gqv_ref[...], gpos + gpos_ref[...], sums + sums_ref[...]
    width, features = gproj.shape
    gproj_ref[...] = gproj.astype(BF)
    hidden = gb1_ref.shape[1]
    lines = [sums[k : k + 1] for k in range(2)] + [sums2_ref[k : k + 1, :] for k in range(4)]
    lines.append(gqv)
    lines += [gb1_ref[:, k : min(k + features, hidden)] for k in range(0, hidden, features)]
    small = jnp.concatenate(
        [jnp.concatenate([line, jnp.zeros((1, features - line.shape[1]), F32)], axis=1) if line.shape[1] < features else line
         for line in lines] + [jnp.zeros((12 - len(lines), features), F32)], axis=0)
    picks = offset_picks()
    for pair in range(gpos.shape[0] * 2):
        rest = gpos[pair // 2][:, pair % 2 * LANES : (pair % 2 + 1) * LANES]
        total = jnp.zeros((SLOT, 2 * LANES), F32)
        for _ in range(2):
            top = rest.astype(BF)
            total = total + mm(top, picks, LAST_LAST)
            rest = rest - top.astype(F32)
        for k in range(2):
            rows_s[pl.ds(2 * pair + k, SLOT, stride=16), :] = total[:, k * LANES : (k + 1) * LANES]
    for h in range(gpos.shape[0] * 4, 16):
        rows_s[pl.ds(h, SLOT, stride=16), :] = jnp.zeros((SLOT, LANES), F32)
    table = jnp.zeros((16, 2 * LANES), F32)
    for i in range(WIN):
        row = jnp.concatenate([rows_s[i * 16 : (i + 1) * 16, :], jnp.zeros((16, LANES), F32)], axis=1)
        table = table + (pltpu.roll(row, place_offset(i), 1) if i else row)
    packed = [jnp.concatenate([table[3 * r + k : 3 * r + k + 1] for k in range(3)], axis=1) for r in range(4)]
    small_ref[...] = jnp.concatenate([small] + packed, axis=0).astype(BF)
    sent = []

    def send(k, source, target):
        sent.append(pltpu.make_async_copy(source, target, out_sems.at[k]))
        sent[-1].start()

    if split:
        for i, (target, y_rel, z_rel, c, y, z) in enumerate(each_block(me_ref[0], *outs)):
            send(i, gproj_ref.at[ds((c * 4 + y * 2 + (z >> 1)) * 48, 48), ds((z & 1) * 384, 384)],
                 target.at[y_rel, z_rel, 48:96, 384:768])
    else:
        send(0, gproj_ref, outs[1])
    for part in range(3):
        gw = 0.0
        for normed_t_ref, _, _, grads_ref, _, _, _ in blocks:
            gw = gw + mm(normed_t_ref[...], grads_ref[part])
        gw_ref[part] = gw.astype(BF)
        if split:
            for i, (target, y_rel, z_rel, c, y, z) in enumerate(each_block(me_ref[0], *outs)):
                send(16 * (part + 1) + i, gw_ref.at[part, ds(c * 384 + y * 192 + z * 48, 48), :],
                     target.at[y_rel, z_rel, part // 2 * 48 : part // 2 * 48 + 48, part % 2 * 384 : part % 2 * 384 + 384])
        else:
            send(1 + part, gw_ref.at[part], outs[0].at[part])
    finish_all(sent)


def input_back_kernel(own_ref, peer_ref, x_ref, gain_ref, gmiddle_ref, gpatch_ref):
    gnorm = own_ref[...].astype(F32) + peer_ref[...].astype(F32)
    xhat, inv = norm_parts(x_ref[...].astype(F32))
    gpatch_ref[...] = (gmiddle_ref[...] + norm_back(xhat, inv, line(gain_ref), gnorm)).astype(BF)


def finish_kernel(y_rels, me_ref, *refs):
    sources, refs = refs[:2], refs[2:]
    if y_rels[0] == 1:
        refs = refs[2:]
    outs, held, wide, (in_sems, out_sems) = refs[:2], refs[2:4], refs[4:6], refs[6:]
    copies = begin(in_sems, *zip(sources, held))
    sent = []

    def put(value, k, where):
        wide[k][where] = value.astype(F32)
        sent.append(pltpu.make_async_copy(wide[k].at[where], outs[k].at[where], out_sems.at[len(sent)]))
        sent[-1].start()

    for source, y_rel, z_rel, c, y, z in each_block(me_ref[0], 0, 1):
        if y_rel not in y_rels:
            continue
        if z_rel == 0:
            copies[source].wait()
        piece = held[source].at[z_rel]
        lines = ds(c * 384 + y * 192 + z * 48, 48)
        put(piece[0:48, 0:384], 0, (0, lines, slice(None)))
        put(piece[0:48, 384:768], 0, (1, lines, slice(None)))
        put(piece[48:96, 0:384], 0, (2, lines, slice(None)))
        put(piece[48:96, 384:768], 1, (ds((c * 4 + y * 2 + (z >> 1)) * 48, 48), ds((z & 1) * 384, 384)))
    finish_all(sent)


def finish_mlp_kernel(me_ref, *refs):
    sources, (g1_out, g2_out, small_ref), held, (g1_ref, g2_ref, small_s, in_sems, out_sems) = (
        refs[:4], refs[4:7], refs[7:11], refs[11:])
    copies = begin(in_sems, *zip(sources, held))
    sent = []

    def put(value, k, wide, out, where):
        wide[where] = value.astype(F32)
        sent.append(pltpu.make_async_copy(wide.at[where], out.at[where], out_sems.at[k, len(sent) // 2]))
        sent[-1].start()

    for source, y_rel, z_rel, c, y, z in each_block(me_ref[0], (0, 1), (2, 3)):
        source = source[y_rel]
        if z_rel == 0:
            copies[source].wait()
        piece = held[source].at[z_rel]
        put(piece[0:BLOCK, :], 0, g1_ref, g1_out, (ds(y * 384 + z * 96, 96), ds(c * 768, 768)))
        put(piece[BLOCK : 2 * BLOCK, :], 1, g2_ref, g2_out, (ds(c * 768 + y * 384 + z * 96, 96), slice(None)))
        small_s[z * 4 + y * 2 + c] = piece[2 * BLOCK :, :].astype(F32)
    total = small_s[0]
    for d in range(1, 16):
        total = total + small_s[d]
    small_ref[...] = total
    finish_all(sent)


def shape_of(*dims, dtype=F32):
    return jax.ShapeDtypeStruct(dims, dtype)


def call(kernel, outs, scratch, name, flops, smem, *args, far=(), far_outs=(), limit=VMEM_LIMIT, aliases=None):
    space = lambda is_far: pl.BlockSpec(memory_space=pltpu.HBM if is_far else pltpu.VMEM)
    in_specs = [pl.BlockSpec(memory_space=pltpu.SMEM)] * len(smem) + [space(i in far) for i in range(len(args))]
    return pl.pallas_call(
        kernel,
        out_shape=outs,
        in_specs=in_specs,
        out_specs=[space(i in far_outs) for i in range(len(outs))],
        scratch_shapes=scratch,
        compiler_params=pltpu.CompilerParams(vmem_limit_bytes=limit),
        cost_estimate=pl.CostEstimate(flops=flops, bytes_accessed=flops // 256, transcendentals=0),
        input_output_aliases=aliases or {},
        name=name,
    )(*smem, *args)


def like(*arrays):
    return [pltpu.VMEM(a.shape, a.dtype) for a in arrays]


def dma(*counts):
    return [pltpu.SemaphoreType.DMA(c if isinstance(c, tuple) else (c,)) for c in counts]


SMALL = 1000000


def position(table):
    heads = table.shape[0]
    groups = -(-heads // GROUP)
    return call(position_kernel, [shape_of(groups, SLOT, GROUP * SLOT)],
                [pltpu.VMEM((16, 2 * LANES), F32), pltpu.VMEM((16 * SLOT, LANES), F32)], "position", SMALL, (), table)[0]


def attn_forward(windows, x, ln1, qkv, qv_bias, pos, mask):
    rows, features = x.shape
    width = qkv.shape[2]
    groups = width // LANES
    tile = shape_of(windows, SLOT, width, dtype=BF)
    outs = [shape_of(windows, groups, SLOT, GROUP * SLOT, dtype=BF), tile, tile, tile, shape_of(rows, width, dtype=BF),
            shape_of(features, rows, dtype=BF)]
    scratch = [pltpu.VMEM((windows, GROUP * SLOT), F32)] + [pltpu.VMEM((groups, SLOT * (windows + 1), LANES), F32)] * 4
    scratch += like(x, qkv) + dma(4)
    return call(functools.partial(attn_forward_kernel, windows), outs, scratch, "attn_forward", SMALL, (),
                x, *ln1, qkv, qv_bias, pos, mask, far=(0, 3), limit=ALL_VMEM)


def middle_norm(me, x, own, peer, bias, ln2, halves):
    rows, features = x.shape
    scratch = like(x, own, peer)
    if halves:
        scratch += [pltpu.VMEM((2 * halves[0].shape[0], features), BF)]
    return call(functools.partial(middle_kernel, bool(halves)), [shape_of(rows, features), shape_of(rows, features, dtype=BF)],
                scratch + dma(5), "middle", SMALL, (me,), x, own, peer, bias, *ln2, *halves, far=(0, 1, 2, 6, 7),
                limit=ALL_VMEM)


def mlp(nm, cot, fc1, fc1_bias, fc2):
    rows, features = nm.shape
    hidden = fc2.shape[0]
    outs = [shape_of(rows, hidden, dtype=BF)] * 2 + [shape_of(rows, features, dtype=BF)] * 2
    return call(mlp_kernel, outs, [], "mlp", SMALL, (), nm, cot, fc1, fc1_bias, fc2)


def fc2_weights(split, me, blocks):
    rows, features = blocks[0][0].shape
    hidden = blocks[0][1].shape[1]
    grad = shape_of(hidden, features, dtype=BF)
    outs = [shape_of(2, 4, BLOCK, features, dtype=BF)] * 2 if split else [grad]
    flat = [a for b in blocks for a in b]
    scratch = like(*flat, grad) + dma(len(blocks), (len(blocks), hidden // 128), 16)
    return call(functools.partial(fc2_weights_kernel, len(blocks), split), outs, scratch, "fc2_weights", SMALL,
                (me,), *flat, far=range(len(flat)), far_outs=range(len(outs)), limit=ALL_VMEM)


def fc1_weights(split, me, blocks):
    rows, features = blocks[0][0].shape
    hidden = blocks[0][1].shape[1]
    grad = shape_of(features, hidden, dtype=BF)
    outs = [shape_of(1, hidden)] + ([shape_of(2, 4, BLOCK, features, dtype=BF)] * 2 if split else [grad])
    flat = [a for b in blocks for a in b]
    scratch = like(*flat) + [pltpu.VMEM((features, rows), BF)] * len(blocks) + like(grad) + dma(len(flat), 16)
    return call(functools.partial(fc1_weights_kernel, len(blocks), split), outs, scratch, "fc1_weights", SMALL,
                (me,), *flat, far=range(len(flat)), far_outs=range(1, len(outs)), limit=ALL_VMEM)


def middle_back(own, peer, middle, cot, gain):
    rows, features = middle.shape
    return call(
        middle_back_kernel, [shape_of(rows, features), shape_of(rows, features, dtype=BF), shape_of(4, features)], [],
        "middle_back", 10000 * SMALL, (), own, peer, middle, cot, gain)


def attn_backward(windows, cost, branch, x, kept, qkv, proj):
    rows, features = branch.shape
    width = proj.shape[0]
    groups = width // LANES
    outs = [shape_of(3, rows, width, dtype=BF), shape_of(1, 2 * width), shape_of(groups, SLOT, GROUP * SLOT),
            shape_of(rows, features, dtype=BF), shape_of(2, features)]
    scratch = [pltpu.VMEM((groups, SLOT * (windows + 1), LANES), F32)] * 4
    return call(functools.partial(attn_backward_kernel, windows), outs, scratch, "attn_backward", cost, (),
                branch, x, *kept, qkv, proj)


def attn_weights(split, me, sums2, gb1, blocks):
    features = blocks[0][0].shape[0]
    width = blocks[0][1].shape[1]
    grads = [shape_of(3, features, width, dtype=BF), shape_of(width, features, dtype=BF)]
    outs = ([shape_of(2, 4, BLOCK, features, dtype=BF)] * 2 if split else grads) + [shape_of(16, features, dtype=BF)]
    scratch = like(*grads) + [pltpu.VMEM((16 * SLOT, LANES), F32)]
    flat = [a for b in blocks for a in b]
    return call(functools.partial(attn_weights_kernel, len(blocks), split), outs, scratch + dma(64),
                "attn_weights", SMALL, (me,), sums2, gb1, *flat, far_outs=(0, 1))


def input_back(own, peer, x, gain, gmiddle):
    rows, features = x.shape
    return call(input_back_kernel, [shape_of(rows, features, dtype=BF)], [], "input_back", SMALL, (),
                own, peer, x, gain, gmiddle)[0]


def finish(me, y_rel, sources, outs, before=()):
    scratch = like(*sources, *outs) + dma(2, 8 * 4)
    return call(functools.partial(finish_kernel, (y_rel,)), list(outs), scratch, "finish", SMALL, (me,), *sources, *before,
                far=range(2 + len(before)), far_outs=range(len(outs)), aliases={3: 0, 4: 1} if before else {})


def finish_mlp(me, sources):
    features = sources[0].shape[2]
    outs = [shape_of(features, 2 * features), shape_of(2 * features, features), shape_of(16, features)]
    scratch = like(*sources, *outs[:2]) + [pltpu.VMEM((16, 16, features), F32)] + dma(4, (2, 16))
    return call(finish_mlp_kernel, outs, scratch, "finish_mlp", SMALL, (me,), *sources, far=range(4), far_outs=(0, 1))


def across(v):
    return lax.ppermute(v, "mp", [(0, 1), (1, 0)])


def flip(v, bits):
    return lax.ppermute(v, "dp", [(i, i ^ bits) for i in range(16)])


def after(v, *others):
    return lax.optimization_barrier((v, *others))[0]


def total_of(terms):
    total = terms[0].astype(F32)
    for t in terms[1:]:
        total = total + t.astype(F32)
    return total.astype(BF)


def side_send(keep, got):
    return total_of([keep[1], got[1]])


def line_sends(keep, got, side):
    return [total_of([keep[0, k], got[0, k], side[k]]) for k in (1, 2, 3)]


def own_piece(keep, got, side, line):
    return total_of([keep[0, 0], got[0, 0], side[0], *line])


def flip_line(pieces):
    return [flip(p, LINE * k) for k, p in zip((1, 2, 3), pieces)]


def sum_line(sends):
    near, far, both = sends
    return [flip(near, LINE), flip(total_of([far, flip(both, LINE)]), 2 * LINE)]


def gather_line(piece):
    far = flip(piece, 2 * LINE)
    return [flip(piece, LINE), far, flip(far, LINE)]


def shards(
    dp_size,
    mp_size,
    patches,
    token_valid,
    ln1_gain,
    ln1_shift,
    qkv_weight,
    qv_bias,
    bias_table,
    proj_weight,
    proj_bias,
    ln2_gain,
    ln2_shift,
    fc1_weight,
    fc1_bias,
    fc2_weight,
    fc2_bias,
    cotangent,
):
    windows, _, features = patches.shape
    rows = windows * WIN
    width = proj_weight.shape[0]
    heads = width // HEAD
    fast = mp_size == 2 and dp_size == 16 and features == 768
    x = patches.transpose(1, 0, 2).reshape(rows, features)
    cot = cotangent.transpose(1, 0, 2).reshape(rows, features)
    row = lambda a: a.reshape(1, -1)
    extra = -width % LANES
    qkv = jnp.pad(qkv_weight.transpose(1, 0, 2), ((0, 0), (0, 0), (0, extra)))
    proj = jnp.pad(proj_weight, ((0, extra), (0, 0)))
    pos = position(bias_table.T)
    bias = jnp.pad(qv_bias, ((0, 0), (0, extra)))
    valid = token_valid.astype(F32)
    ln1, ln2 = (ln1_gain, ln1_shift), (ln2_gain, ln2_shift)

    def blocks_of(v):
        return [v, across(v)] if fast else list(lax.all_gather(v, "mp"))

    def own_sums(parts):
        if fast:
            return parts[0], across(parts[1])
        own = lax.psum_scatter(jnp.concatenate(parts), "mp", scatter_dimension=0, tiled=True)
        return own, jnp.zeros_like(own)

    index = lax.axis_index("dp").astype(jnp.int32)
    me = index.reshape(1)
    valids = blocks_of(valid)
    kept, xs = [], []
    for x_b, valid_b in zip(blocks_of(x), valids):
        if kept:
            x_b = after(x_b, kept[0][4])
        xs.append(x_b)
        kept.append(attn_forward(windows, x_b, ln1, qkv, bias, pos, valid_b))
    project = lambda mixed, weight: jnp.dot(mixed, weight, preferred_element_type=F32).astype(BF)
    if fast:
        core = index & 1
        half = across(lax.dynamic_slice_in_dim(after(proj, valids[1]), core * (width // 2), width // 2, 0))
        cots = [cot, across(after(cot, valids[1]))]
        mixed = across(after(kept[1][4], cots[1], half))
        half = after(half, kept[1][4])
        rest = flip(half, CORE)
        parts, halves = (project(kept[0][4], proj), mixed), (half, rest)
    else:
        parts, halves = own_sums([project(k[4], proj) for k in kept]), ()
        cots = blocks_of(cot)
    middle, nm = middle_norm(me, x, *parts, proj_bias, ln2, halves)

    blocks, outs, gmids = [], [], []
    for nm_b, cot_b in zip(blocks_of(nm), cots):
        if blocks:
            nm_b = after(nm_b, gmids[-1])
        hid, gpre, out_b, gmid_b = mlp(nm_b, cot_b, fc1_weight, row(fc1_bias), fc2_weight)
        blocks.append((nm_b, cot_b, hid, gpre))
        outs.append(out_b)
        gmids.append(gmid_b)
    gmid_own, gmid_peer = own_sums(gmids)
    g_fc2 = fc2_weights(fast, me, [(cot_b, hid) for _, cot_b, hid, _ in blocks])
    gb1, *g_fc1 = fc1_weights(fast, me, [(after(nm_b, g_fc2[0]), gpre) for nm_b, _, _, gpre in blocks])
    outs = own_sums(outs)
    gmid_peer = after(gmid_peer, gb1)
    gmiddle, branch, sums2 = middle_back(gmid_own, gmid_peer, middle, cot, ln2[0])
    branches = blocks_of(branch)
    if fast:
        (keep2, send2), (keep1, send1) = g_fc1, g_fc2
        got1 = after(flip(send1, CORE), branch)
        side1 = side_send(keep1, got1)
        branches[0] = after(branches[0], side1)
    backs, gparts = [], []
    for b, kept_b in enumerate(kept):
        if b == 1 and fast:
            got2 = after(flip(send2, CORE), gparts[0])
            side2 = side_send(keep2, got2)
            side1 = after(flip(side1, SIDE), gparts[0])
            line1 = line_sends(keep1, got1, side1)
            branches[1] = after(branches[1], *line1, side2, gparts[0])
        *back, gpart, gsum = attn_backward(windows, SMALL if b else 20000 * SMALL, branches[b], xs[b], kept_b[:4], qkv, proj)
        backs.append((*back, gsum))
        gparts.append(gpart)
    if fast:
        side2 = after(flip(side2, SIDE), gparts[1])
        line2 = line_sends(keep2, got2, side2)
        line1 = [after(r, gparts[1]) for r in flip_line(line1)]
        piece1 = own_piece(keep1, got1, side1, line1)
        branches[0] = after(branches[0], piece1, *line2, outs[1])
    *g_attn, small = attn_weights(
        fast, me, sums2, gb1, [(k[5], k[4], br, *back) for k, br, back in zip(kept, branches, backs)])
    gnorms = own_sums(gparts)
    gpatch = input_back(*gnorms, x, ln1[0], gmiddle)
    output = (middle + outs[0].astype(F32) + outs[1].astype(F32) + row(fc2_bias)).astype(BF)

    if fast:
        line2 = [after(r, small) for r in flip_line(line2)]
        piece2 = own_piece(keep2, got2, side2, line2)
        keep, send = g_attn
        got = flip(after(send, piece2), CORE)
        side = flip(side_send(keep, got), SIDE)
        fc = jnp.concatenate([piece2, piece1, small], axis=0)
        fc_quad = jnp.stack([fc] + [after(r, output, gpatch) for r in gather_line(fc)])
        side = after(side, fc_quad, output, gpatch)
        line = sum_line(line_sends(keep, got, side))
        piece = own_piece(keep, got, side, line)
        quad = jnp.stack([piece] + gather_line(piece))
        fc_pair = after(flip(fc_quad, SIDE), quad)
        g_fc1, g_fc2, small = finish_mlp(me, (fc_quad, fc_pair, after(flip(fc_quad, CORE), quad), after(flip(fc_pair, CORE), quad)))
        totals = small[0:6] + across(small[0:6])
        pair = after(flip(quad, SIDE), totals)
        shapes = shape_of(3, features, width), shape_of(width, features)
        half_done = finish(me, 0, (quad, flip(quad, CORE)), shapes)
        pair = after(pair, half_done[0])
        gw, gproj = finish(me, 1, (pair, flip(pair, CORE)), shapes, half_done)
    else:
        g_fc1, g_fc2, gw, gproj = [g.astype(F32) for g in lax.psum((*g_fc1, *g_fc2, *g_attn), "dp")]
        gw, gproj = gw[:, :, :width], gproj[:width]
        small = lax.psum(small, "dp").astype(F32)
        totals = lax.psum(small[0:6], "mp")
    padded = width + extra
    gqv = jnp.stack([small[6, :width], small[6, padded : padded + width]])
    gb1 = small[7:12].reshape(-1)[: gb1.size]
    gt = small[12:].reshape(12, 2 * LANES)[:heads, :REL].T

    unrow = lambda a: a.reshape(WIN, windows, features).transpose(1, 0, 2)
    return (
        unrow(output),
        unrow(gpatch),
        totals[0],
        totals[1],
        gw.transpose(1, 0, 2),
        gqv,
        gt,
        gproj,
        totals[4],
        totals[2],
        totals[3],
        g_fc1,
        gb1,
        g_fc2,
        totals[5],
    )


def solution(mesh):
    placed = (
        P(("dp", "mp"), None, None),
        P(("dp", "mp"), None),
        P(),
        P(),
        P(None, None, "mp"),
        P(None, "mp"),
        P(None, "mp"),
        P("mp", None),
        P(),
        P(),
        P(),
        P(None, "mp"),
        P("mp"),
        P("mp", None),
        P(),
        P(("dp", "mp"), None, None),
    )
    return jax.shard_map(
        functools.partial(shards, mesh.shape["dp"], mesh.shape["mp"]),
        mesh=mesh,
        in_specs=placed,
        out_specs=(
            P(("dp", "mp"), None, None),
            P(("dp", "mp"), None, None),
            P(),
            P(),
            P(None, None, "mp"),
            P(None, "mp"),
            P(None, "mp"),
            P("mp", None),
            P(),
            P(),
            P(),
            P(None, "mp"),
            P("mp"),
            P("mp", None),
            P(),
        ),
        check_vma=False,
    )
```

```python
import functools

import jax
import jax.numpy as jnp
from jax import lax
from jax.experimental import pallas as pl
from jax.experimental.pallas import tpu as pltpu
from jax.sharding import PartitionSpec as P

HEAD = 32
WSIDE = 7
WIN = 49
REL = 169
SLOT = 64
GROUP = 4
LANES = 128
EPS = 1e-05
SCALING = HEAD ** (-0.5)
BF = jnp.bfloat16
F32 = jnp.float32
HIGH = lax.Precision.HIGHEST
VMEM_LIMIT = 28 * 1024 * 1024
ALL_VMEM = 58 * 1024 * 1024
BLOCK = 96
CORE, SIDE, LINE = 1, 2, 4

ROW_COL = (((1,), (0,)), ((), ()))
LAST_LAST = (((1,), (1,)), ((), ()))
ROWS_ROWS = (((0,), (0,)), ((), ()))


def mm(a, b, dims=ROW_COL):
    return lax.dot_general(a, b, dims, preferred_element_type=F32)


def norm_parts(rows):
    mean = jnp.mean(rows, axis=-1, keepdims=True)
    centred = rows - mean
    variance = jnp.mean(centred * centred, axis=-1, keepdims=True)
    inv = lax.rsqrt(variance + EPS)
    return centred * inv, inv


def norm_back(xhat, inv, gain, upstream):
    z = upstream * gain
    mean_z = jnp.mean(z, axis=-1, keepdims=True)
    mean_zx = jnp.mean(z * xhat, axis=-1, keepdims=True)
    return (z - mean_z - xhat * mean_zx) * inv


def head_masks():
    lane = lax.broadcasted_iota(jnp.int32, (SLOT, LANES), 1)
    return [jnp.where((lane >> 5) == h, 1.0, 0.0).astype(BF) for h in range(GROUP)]


def block_ones():
    row = lax.broadcasted_iota(jnp.int32, (GROUP * SLOT, GROUP * SLOT), 0)
    col = lax.broadcasted_iota(jnp.int32, (GROUP * SLOT, GROUP * SLOT), 1)
    return jnp.where((row >> 6) == (col >> 6), 1.0, 0.0).astype(BF)


def spread(tile, masks):
    return jnp.concatenate([tile * m for m in masks], axis=0)


def collect(full, masks_f):
    total = full[0:SLOT] * masks_f[0]
    for h in range(1, GROUP):
        total = total + full[h * SLOT : (h + 1) * SLOT] * masks_f[h]
    return total


def fill(scratch, rows, windows):
    pitch = windows + 1
    for g in range(scratch.shape[0]):
        for place in range(WIN):
            scratch[g, place * pitch : place * pitch + windows, :] = rows[
                place * windows : (place + 1) * windows, g * LANES : (g + 1) * LANES]
        scratch[g, WIN * pitch :, :] = jnp.zeros((scratch.shape[1] - WIN * pitch, LANES), rows.dtype)


def empty(scratch, windows):
    pitch = windows + 1
    planes = [
        jnp.concatenate([scratch[g, place * pitch : place * pitch + windows, :] for place in range(WIN)], axis=0)
        for g in range(scratch.shape[0])
    ]
    return jnp.concatenate(planes, axis=1).astype(BF)


def row_max(tile, low_half):
    low = jnp.max(jnp.where(low_half, tile, -3e38), axis=-1, keepdims=True)
    high = jnp.max(jnp.where(low_half, -3e38, tile), axis=-1, keepdims=True)
    return jnp.where(low_half, low, high)


def row_sum(tile, low_half):
    low = jnp.sum(jnp.where(low_half, tile, 0.0), axis=-1, keepdims=True)
    high = jnp.sum(jnp.where(low_half, 0.0, tile), axis=-1, keepdims=True)
    return jnp.where(low_half, low, high)


def ds(start, size):
    unit = 384 if size % 384 == 0 else 48
    return pl.ds(pl.multiple_of(start, unit), size)


def each_block(me, *by_core):
    for c_rel, target in enumerate(by_core):
        for y_rel in range(2):
            for z_rel in range(4):
                yield target, y_rel, z_rel, (me & 1) ^ c_rel, ((me >> 1) & 1) ^ y_rel, (me >> 2) ^ z_rel


def line(ref):
    return ref[...].reshape(1, -1)


def begin(sems, *pairs):
    copies = [pltpu.make_async_copy(a, b, sems.at[i]) for i, (a, b) in enumerate(pairs)]
    for copy in copies:
        copy.start()
    return copies


def finish_all(copies):
    for copy in copies:
        copy.wait()


def attn_forward_kernel(windows, x_in, gain_ref, shift_ref, w_in, bias_ref, pos_ref, valid_ref,
                        prob_ref, q_ref, k_ref, v_ref, mixed_ref, normed_t_ref,
                        mask_s, q_s, k_s, v_s, mixed_s, x_ref, w_ref, in_sems):
    copies = begin(in_sems, (x_in, x_ref), *[(w_in.at[p], w_ref.at[p]) for p in range(3)])
    mask_s[...] = jnp.zeros(mask_s.shape, F32)
    for h in range(GROUP):
        mask_s[:, h * SLOT : h * SLOT + WIN] = valid_ref[...].astype(F32)
    masks = head_masks()
    ones = block_ones()
    low_half = lax.broadcasted_iota(jnp.int32, (SLOT, LANES), 1) < SLOT
    copies[0].wait()
    x = x_ref[...].astype(F32)
    rows = x.shape[0]
    groups = q_s.shape[0]
    xhat, _ = norm_parts(x)
    normed = (xhat * line(gain_ref) + line(shift_ref)).astype(BF)
    normed_t_ref[...] = normed.T
    for part, scratch in enumerate((q_s, k_s, v_s)):
        copies[1 + part].wait()
        got = mm(normed, w_ref[part])
        if part != 1:
            got = got + bias_ref[part // 2 : part // 2 + 1, :]
        fill(scratch, got.astype(BF).astype(F32), windows)

    def window(w, carry):
        allowed = jnp.broadcast_to(mask_s[pl.ds(w, 1), :], (SLOT, GROUP * SLOT)) > 0.5
        for g in range(groups):
            cols = slice(g * LANES, (g + 1) * LANES)
            places = pl.ds(w, SLOT, stride=windows + 1)
            q = q_s[g, places, :].astype(BF)
            k = k_s[g, places, :].astype(BF)
            v = v_s[g, places, :].astype(BF)
            q_ref[w, :, cols] = q
            k_ref[w, :, cols] = k
            v_ref[w, :, cols] = v
            scores = mm(q, spread(k, masks), LAST_LAST) * SCALING + pos_ref[g]
            scores = jnp.where(allowed, scores, -1000000000.0)
            top = jnp.concatenate([row_max(scores[:, :LANES], low_half), row_max(scores[:, LANES:], low_half)], axis=1)
            e = jnp.exp(scores - top)
            total = mm(e.astype(BF), ones)
            inv = pl.reciprocal(total, approx=True)
            prob = (e * (inv * (2.0 - total * inv))).astype(BF)
            prob_ref[w, g] = prob
            mixed_s[g, places, :] = mm(prob, spread(v, masks))
        return carry

    lax.fori_loop(0, windows, window, 0, unroll=2)
    mixed_ref[...] = empty(mixed_s, windows)


def middle_kernel(heads, me_ref, x_in, own_in, peer_in, bias_ref, gain_ref, shift_ref, *refs):
    if heads:
        half_in, rest_in, middle_ref, nm_ref, x_ref, own_ref, peer_ref, proj_ref, sems = refs
        lines = half_in.shape[0]
        core = me_ref[0] & 1
        place = lambda c: proj_ref.at[pl.ds(pl.multiple_of(c * lines, lines), lines), :]
        copies = begin(sems, (peer_in, peer_ref), (half_in, place(core)), (rest_in, place(1 - core)), (x_in, x_ref),
                       (own_in, own_ref))
        finish_all(copies[:3])
        peer = mm(peer_ref[...], proj_ref[...])
        finish_all(copies[3:])
    else:
        middle_ref, nm_ref, x_ref, own_ref, peer_ref, sems = refs
        finish_all(begin(sems, (x_in, x_ref), (own_in, own_ref), (peer_in, peer_ref)))
        peer = peer_ref[...].astype(F32)
    middle = x_ref[...].astype(F32) + (own_ref[...].astype(F32) + peer) + line(bias_ref)
    middle_ref[...] = middle
    xhat, _ = norm_parts(middle)
    nm_ref[...] = (xhat * line(gain_ref) + line(shift_ref)).astype(BF)


def mlp_kernel(nm_ref, cot_ref, fc1_ref, b1_ref, fc2_ref, hid_ref, gpre_ref, out_ref, gmid_ref):
    hidden_size = fc1_ref.shape[1]
    features = fc1_ref.shape[0]
    step = 256 if hidden_size % 256 == 0 else 128
    count = hidden_size // step

    nm = nm_ref[...]
    cot = cot_ref[...]

    def units(c, carry):
        cols = pl.ds(pl.multiple_of(c * step, step), step)
        pre = mm(nm, fc1_ref[:, cols]) + b1_ref[:, cols]
        phi = 0.5 * (1.0 + lax.erf(pre * (0.5 ** 0.5)))
        hid_ref[:, cols] = (pre * phi).astype(BF)
        slope = phi + pre * (jnp.exp(-0.5 * pre * pre) * 0.3989422804014327)
        gpre_ref[:, cols] = (mm(cot, fc2_ref[cols, :], LAST_LAST) * slope).astype(BF)
        return carry

    lax.fori_loop(0, count, units, 0)

    def tile(c, carry):
        cols = pl.ds(pl.multiple_of(c * 256, 256), 256)
        gmid_ref[:, cols] = mm(gpre_ref[...], fc1_ref[cols, :], LAST_LAST).astype(BF)
        out_ref[:, cols] = mm(hid_ref[...], fc2_ref[:, cols]).astype(BF)
        return carry

    lax.fori_loop(0, features // 256, tile, 0)

def mlp_weights_kernel(count, split, me_ref, *refs):
    inputs, refs = refs[: 4 * count], refs[4 * count :]
    n_out = 5 if split else 3
    gb1_ref, *outs = refs[:n_out]
    held = refs[n_out : n_out + 4 * count]
    nts = refs[n_out + 4 * count : n_out + 5 * count]
    g1_ref, g2_ref, in_sems, unit_sems, out_sems = refs[n_out + 5 * count :]
    blocks = [held[4 * b : 4 * b + 4] for b in range(count)]
    hidden_size = g1_ref.shape[1]
    features = g1_ref.shape[0]
    step = 384 if hidden_size % 384 == 0 else 128
    wide = features if hidden_size % features == 0 else step

    def units_in(j):
        cols = ds(j * step, step)
        return [pltpu.make_async_copy(inputs[4 * b + 2].at[:, cols], held[4 * b + 2].at[:, cols], unit_sems.at[b, j])
                for b in range(count)]

    order = [4 * b + k for k in (0, 1) for b in range(count)]
    copies = dict(zip(order, begin(in_sems, *[(inputs[i], held[i]) for i in order])))
    for j in range(hidden_size // step):
        for copy in units_in(j):
            copy.start()
    last = [pltpu.make_async_copy(inputs[4 * b + 3], held[4 * b + 3], in_sems.at[2 * count + b]) for b in range(count)]
    for copy in last:
        copy.start()
    finish_all([copies[4 * b] for b in range(count)])
    for block, nt in zip(blocks, nts):
        nt[...] = block[0][...].T
    finish_all([copies[4 * b + 1] for b in range(count)])

    def second(j, carry):
        finish_all(units_in(j))
        cols = ds(j * step, step)
        g2_ref[cols, :] = sum(mm(hid_ref[:, cols], cot_ref[...], ROWS_ROWS) for _, cot_ref, hid_ref, _ in blocks).astype(BF)
        return carry

    def first(j, carry):
        cols = ds(j * wide, wide)
        g1_ref[:, cols] = sum(mm(nt[...], block[3][:, cols]) for nt, block in zip(nts, blocks)).astype(BF)
        return carry

    lax.fori_loop(0, hidden_size // step, second, 0)
    me = me_ref[0]
    sent = []

    def send(k, source, target):
        sent.append(pltpu.make_async_copy(source, target, out_sems.at[k]))
        sent[-1].start()

    if split:
        for i, (target, y_rel, z_rel, c, y, z) in enumerate(each_block(me, outs[2], outs[3])):
            send(i, g2_ref.at[ds(c * 768 + y * 384 + z * 96, 96), :], target.at[y_rel, z_rel])
    else:
        send(0, g2_ref, outs[1])
    finish_all(last)
    gb1_ref[...] = sum(jnp.sum(block[3][...].astype(F32), axis=0, keepdims=True) for block in blocks)
    lax.fori_loop(0, hidden_size // wide, first, 0)
    if split:
        for i, (target, y_rel, z_rel, c, y, z) in enumerate(each_block(me, outs[0], outs[1])):
            send(16 + i, g1_ref.at[ds(y * 384 + z * 96, 96), ds(c * 768, 768)], target.at[y_rel, z_rel])
    else:
        send(1, g1_ref, outs[0])
    finish_all(sent)


def middle_back_kernel(own_ref, peer_ref, middle_ref, cot_ref, gain_ref, gmiddle_ref, branch_ref, sums_ref):
    upstream = cot_ref[...].astype(F32)
    xhat, inv = norm_parts(middle_ref[...])
    gmid = own_ref[...].astype(F32) + peer_ref[...].astype(F32)
    sums_ref[0:1, :] = jnp.sum(gmid * xhat, axis=0, keepdims=True)
    sums_ref[1:2, :] = jnp.sum(gmid, axis=0, keepdims=True)
    gmiddle = upstream + norm_back(xhat, inv, line(gain_ref), gmid)
    gmiddle_ref[...] = gmiddle
    branch_ref[...] = gmiddle.astype(BF)
    sums_ref[2:3, :] = jnp.sum(gmiddle, axis=0, keepdims=True)
    sums_ref[3:4, :] = jnp.sum(upstream, axis=0, keepdims=True)


def attn_backward_kernel(windows, branch_ref, x_ref, prob_ref, q_ref, k_ref, v_ref, w_ref, proj_ref,
                         grads_ref, gqv_ref, gpos_ref, part_ref, sums_ref, gm_s, gq_s, gk_s, gv_s):
    rows = branch_ref.shape[0]
    groups = gm_s.shape[0]
    gpos_ref[...] = jnp.zeros(gpos_ref.shape, F32)
    masks = head_masks()
    masks_f = [m.astype(F32) for m in masks]
    low_half = lax.broadcasted_iota(jnp.int32, (SLOT, LANES), 1) < SLOT
    fill(gm_s, mm(branch_ref[...], proj_ref[...], LAST_LAST).astype(BF).astype(F32), windows)

    def window(w, carry):
        for g in range(groups):
            cols = slice(g * LANES, (g + 1) * LANES)
            places = pl.ds(w, SLOT, stride=windows + 1)
            gm = gm_s[g, places, :].astype(BF)
            q = q_ref[w, :, cols]
            k = k_ref[w, :, cols]
            v = v_ref[w, :, cols]
            prob = prob_ref[w, g]
            prob_f = prob.astype(F32)
            gprob = mm(gm, spread(v, masks), LAST_LAST)
            both = prob_f * gprob
            delta = jnp.concatenate([row_sum(both[:, :LANES], low_half), row_sum(both[:, LANES:], low_half)], axis=1)
            gs = (both - prob_f * delta).astype(BF)
            gpos_ref[g] += gs.astype(F32)
            gq_s[g, places, :] = mm(gs, spread(k, masks)) * SCALING
            gk_s[g, places, :] = collect(mm(gs, q, ROWS_ROWS), masks_f) * SCALING
            gv_s[g, places, :] = collect(mm(prob, gm, ROWS_ROWS), masks_f)
        return carry

    lax.fori_loop(0, windows, window, 0, unroll=2)
    back = None
    for part, scratch in enumerate((gq_s, gk_s, gv_s)):
        grad = empty(scratch, windows)
        grads_ref[part] = grad
        if part != 1:
            width = grad.shape[1]
            lanes = slice(part // 2 * width, (part // 2 + 1) * width)
            gqv_ref[:, lanes] = jnp.sum(grad.astype(F32), axis=0, keepdims=True)
        term = mm(grad, w_ref[part], LAST_LAST)
        back = term if back is None else back + term
    part_ref[...] = back.astype(BF)
    xhat, _ = norm_parts(x_ref[...].astype(F32))
    sums_ref[0:1, :] = jnp.sum(back * xhat, axis=0, keepdims=True)
    sums_ref[1:2, :] = jnp.sum(back, axis=0, keepdims=True)


def place_offset(i):
    return i // WSIDE * (2 * WSIDE - 1) + i % WSIDE


def offset_picks():
    row = lax.broadcasted_iota(jnp.int32, (2 * LANES, 2 * SLOT), 0)
    col = lax.broadcasted_iota(jnp.int32, (2 * LANES, 2 * SLOT), 1)
    j = col & (SLOT - 1)
    line = (j * 37) >> 8
    offset = place_offset(WIN - 1) - line * (2 * WSIDE - 1) - (j - line * WSIDE)
    hit = ((row & (LANES - 1)) == offset) & ((row >> 7) == (col >> 6)) & (j < WIN)
    return jnp.where(hit, 1.0, 0.0).astype(BF)


def position_kernel(table_ref, pos_ref, table_s, rows_s):
    heads = table_ref.shape[0]
    table_s[...] = jnp.zeros(table_s.shape, F32)
    table_s[0:heads, 0:REL] = table_ref[...]
    table = table_s[...]
    lines = table.shape[0]
    rows_s[WIN * lines :, :] = jnp.zeros((rows_s.shape[0] - WIN * lines, LANES), F32)
    for i in range(WIN):
        turned = pltpu.roll(table, (2 * LANES - place_offset(i)) % (2 * LANES), 1)
        rows_s[i * lines : (i + 1) * lines, :] = turned[:, :LANES]
    picks = offset_picks()
    for pair in range(pos_ref.shape[0] * 2):
        pieces = [rows_s[pl.ds(2 * pair + k, SLOT, stride=lines), :] for k in range(2)]
        rest = jnp.concatenate(pieces, axis=1)
        total = jnp.zeros((SLOT, 2 * SLOT), F32)
        for _ in range(3):
            top = rest.astype(BF)
            total = total + mm(top, picks)
            rest = rest - top.astype(F32)
        pos_ref[pair // 2, :, pair % 2 * LANES : (pair % 2 + 1) * LANES] = total


def attn_weights_kernel(count, split, me_ref, sums2_ref, gb1_ref, *refs):
    blocks, refs = [refs[7 * b : 7 * b + 7] for b in range(count)], refs[7 * count :]
    *outs, small_ref = refs[:3]
    gw_ref, gproj_ref, rows_s, out_sems = refs[3:]
    gproj, gqv, gpos, sums = 0.0, 0.0, 0.0, 0.0
    for _, mixed_ref, branch_ref, _, gqv_ref, gpos_ref, sums_ref in blocks:
        gproj = gproj + mm(mixed_ref[...], branch_ref[...], ROWS_ROWS)
        gqv, gpos, sums = gqv + gqv_ref[...], gpos + gpos_ref[...], sums + sums_ref[...]
    width, features = gproj.shape
    gproj_ref[...] = gproj.astype(BF)
    hidden = gb1_ref.shape[1]
    lines = [sums[k : k + 1] for k in range(2)] + [sums2_ref[k : k + 1, :] for k in range(4)]
    lines.append(gqv)
    lines += [gb1_ref[:, k : min(k + features, hidden)] for k in range(0, hidden, features)]
    small = jnp.concatenate(
        [jnp.concatenate([line, jnp.zeros((1, features - line.shape[1]), F32)], axis=1) if line.shape[1] < features else line
         for line in lines] + [jnp.zeros((12 - len(lines), features), F32)], axis=0)
    picks = offset_picks()
    for pair in range(gpos.shape[0] * 2):
        rest = gpos[pair // 2][:, pair % 2 * LANES : (pair % 2 + 1) * LANES]
        total = jnp.zeros((SLOT, 2 * LANES), F32)
        for _ in range(2):
            top = rest.astype(BF)
            total = total + mm(top, picks, LAST_LAST)
            rest = rest - top.astype(F32)
        for k in range(2):
            rows_s[pl.ds(2 * pair + k, SLOT, stride=16), :] = total[:, k * LANES : (k + 1) * LANES]
    for h in range(gpos.shape[0] * 4, 16):
        rows_s[pl.ds(h, SLOT, stride=16), :] = jnp.zeros((SLOT, LANES), F32)
    table = jnp.zeros((16, 2 * LANES), F32)
    for i in range(WIN):
        row = jnp.concatenate([rows_s[i * 16 : (i + 1) * 16, :], jnp.zeros((16, LANES), F32)], axis=1)
        table = table + (pltpu.roll(row, place_offset(i), 1) if i else row)
    packed = [jnp.concatenate([table[3 * r + k : 3 * r + k + 1] for k in range(3)], axis=1) for r in range(4)]
    small_ref[...] = jnp.concatenate([small] + packed, axis=0).astype(BF)
    sent = []

    def send(k, source, target):
        sent.append(pltpu.make_async_copy(source, target, out_sems.at[k]))
        sent[-1].start()

    if split:
        for i, (target, y_rel, z_rel, c, y, z) in enumerate(each_block(me_ref[0], *outs)):
            send(i, gproj_ref.at[ds((c * 4 + y * 2 + (z >> 1)) * 48, 48), ds((z & 1) * 384, 384)],
                 target.at[y_rel, z_rel, 48:96, 384:768])
    else:
        send(0, gproj_ref, outs[1])
    for part in range(3):
        gw = 0.0
        for normed_t_ref, _, _, grads_ref, _, _, _ in blocks:
            gw = gw + mm(normed_t_ref[...], grads_ref[part])
        gw_ref[part] = gw.astype(BF)
        if split:
            for i, (target, y_rel, z_rel, c, y, z) in enumerate(each_block(me_ref[0], *outs)):
                send(16 * (part + 1) + i, gw_ref.at[part, ds(c * 384 + y * 192 + z * 48, 48), :],
                     target.at[y_rel, z_rel, part // 2 * 48 : part // 2 * 48 + 48, part % 2 * 384 : part % 2 * 384 + 384])
        else:
            send(1 + part, gw_ref.at[part], outs[0].at[part])
    finish_all(sent)


def input_back_kernel(own_ref, peer_ref, x_ref, gain_ref, gmiddle_ref, gpatch_ref):
    gnorm = own_ref[...].astype(F32) + peer_ref[...].astype(F32)
    xhat, inv = norm_parts(x_ref[...].astype(F32))
    gpatch_ref[...] = (gmiddle_ref[...] + norm_back(xhat, inv, line(gain_ref), gnorm)).astype(BF)


def finish_kernel(y_rels, me_ref, *refs):
    sources, refs = refs[:2], refs[2:]
    if y_rels[0] == 1:
        refs = refs[2:]
    outs, held, wide, (in_sems, out_sems) = refs[:2], refs[2:4], refs[4:6], refs[6:]
    copies = begin(in_sems, *zip(sources, held))
    sent = []

    def put(value, k, where):
        wide[k][where] = value.astype(F32)
        sent.append(pltpu.make_async_copy(wide[k].at[where], outs[k].at[where], out_sems.at[len(sent)]))
        sent[-1].start()

    for source, y_rel, z_rel, c, y, z in each_block(me_ref[0], 0, 1):
        if y_rel not in y_rels:
            continue
        if z_rel == 0:
            copies[source].wait()
        piece = held[source].at[z_rel]
        lines = ds(c * 384 + y * 192 + z * 48, 48)
        put(piece[0:48, 0:384], 0, (0, lines, slice(None)))
        put(piece[0:48, 384:768], 0, (1, lines, slice(None)))
        put(piece[48:96, 0:384], 0, (2, lines, slice(None)))
        put(piece[48:96, 384:768], 1, (ds((c * 4 + y * 2 + (z >> 1)) * 48, 48), ds((z & 1) * 384, 384)))
    finish_all(sent)


def finish_mlp_kernel(me_ref, *refs):
    sources, (g1_out, g2_out, small_ref), held, (g1_ref, g2_ref, small_s, in_sems, out_sems) = (
        refs[:4], refs[4:7], refs[7:11], refs[11:])
    copies = begin(in_sems, *zip(sources, held))
    sent = []

    def put(value, k, wide, out, where):
        wide[where] = value.astype(F32)
        sent.append(pltpu.make_async_copy(wide.at[where], out.at[where], out_sems.at[k, len(sent) // 2]))
        sent[-1].start()

    for source, y_rel, z_rel, c, y, z in each_block(me_ref[0], (0, 1), (2, 3)):
        source = source[y_rel]
        if z_rel == 0:
            copies[source].wait()
        piece = held[source].at[z_rel]
        put(piece[0:BLOCK, :], 0, g1_ref, g1_out, (ds(y * 384 + z * 96, 96), ds(c * 768, 768)))
        put(piece[BLOCK : 2 * BLOCK, :], 1, g2_ref, g2_out, (ds(c * 768 + y * 384 + z * 96, 96), slice(None)))
        small_s[z * 4 + y * 2 + c] = piece[2 * BLOCK :, :].astype(F32)
    total = small_s[0]
    for d in range(1, 16):
        total = total + small_s[d]
    small_ref[...] = total
    finish_all(sent)


def shape_of(*dims, dtype=F32):
    return jax.ShapeDtypeStruct(dims, dtype)


def call(kernel, outs, scratch, name, flops, smem, *args, far=(), far_outs=(), limit=VMEM_LIMIT, aliases=None):
    space = lambda is_far: pl.BlockSpec(memory_space=pltpu.HBM if is_far else pltpu.VMEM)
    in_specs = [pl.BlockSpec(memory_space=pltpu.SMEM)] * len(smem) + [space(i in far) for i in range(len(args))]
    return pl.pallas_call(
        kernel,
        out_shape=outs,
        in_specs=in_specs,
        out_specs=[space(i in far_outs) for i in range(len(outs))],
        scratch_shapes=scratch,
        compiler_params=pltpu.CompilerParams(vmem_limit_bytes=limit),
        cost_estimate=pl.CostEstimate(flops=flops, bytes_accessed=flops // 256, transcendentals=0),
        input_output_aliases=aliases or {},
        name=name,
    )(*smem, *args)


def like(*arrays):
    return [pltpu.VMEM(a.shape, a.dtype) for a in arrays]


def dma(*counts):
    return [pltpu.SemaphoreType.DMA(c if isinstance(c, tuple) else (c,)) for c in counts]


SMALL = 1000000


def position(table):
    heads = table.shape[0]
    groups = -(-heads // GROUP)
    return call(position_kernel, [shape_of(groups, SLOT, GROUP * SLOT)],
                [pltpu.VMEM((16, 2 * LANES), F32), pltpu.VMEM((16 * SLOT, LANES), F32)], "position", SMALL, (), table)[0]


def attn_forward(windows, x, ln1, qkv, qv_bias, pos, mask):
    rows, features = x.shape
    width = qkv.shape[2]
    groups = width // LANES
    tile = shape_of(windows, SLOT, width, dtype=BF)
    outs = [shape_of(windows, groups, SLOT, GROUP * SLOT, dtype=BF), tile, tile, tile, shape_of(rows, width, dtype=BF),
            shape_of(features, rows, dtype=BF)]
    scratch = [pltpu.VMEM((windows, GROUP * SLOT), F32)] + [pltpu.VMEM((groups, SLOT * (windows + 1), LANES), F32)] * 4
    scratch += like(x, qkv) + dma(4)
    return call(functools.partial(attn_forward_kernel, windows), outs, scratch, "attn_forward", SMALL, (),
                x, *ln1, qkv, qv_bias, pos, mask, far=(0, 3), limit=ALL_VMEM)


def middle_norm(me, x, own, peer, bias, ln2, halves):
    rows, features = x.shape
    scratch = like(x, own, peer)
    if halves:
        scratch += [pltpu.VMEM((2 * halves[0].shape[0], features), BF)]
    return call(functools.partial(middle_kernel, bool(halves)), [shape_of(rows, features), shape_of(rows, features, dtype=BF)],
                scratch + dma(5), "middle", SMALL, (me,), x, own, peer, bias, *ln2, *halves, far=(0, 1, 2, 6, 7),
                limit=ALL_VMEM)


def mlp(nm, cot, fc1, fc1_bias, fc2):
    rows, features = nm.shape
    hidden = fc2.shape[0]
    outs = [shape_of(rows, hidden, dtype=BF)] * 2 + [shape_of(rows, features, dtype=BF)] * 2
    return call(mlp_kernel, outs, [], "mlp", SMALL, (), nm, cot, fc1, fc1_bias, fc2)


def mlp_weights(split, me, blocks):
    rows, features = blocks[0][0].shape
    hidden = blocks[0][2].shape[1]
    grads = [shape_of(features, hidden, dtype=BF), shape_of(hidden, features, dtype=BF)]
    outs = [shape_of(1, hidden)] + ([shape_of(2, 4, BLOCK, features, dtype=BF)] * 4 if split else grads)
    flat = [a for b in blocks for a in b]
    scratch = like(*flat) + [pltpu.VMEM((features, rows), BF)] * len(blocks) + like(*grads) + dma(3 * len(blocks), (len(blocks), hidden // 128), 32)
    return call(functools.partial(mlp_weights_kernel, len(blocks), split), outs, scratch, "mlp_weights", SMALL,
                (me,), *flat, far=range(len(flat)), far_outs=range(1, len(outs)), limit=ALL_VMEM)


def middle_back(own, peer, middle, cot, gain):
    rows, features = middle.shape
    return call(
        middle_back_kernel, [shape_of(rows, features), shape_of(rows, features, dtype=BF), shape_of(4, features)], [],
        "middle_back", 20000 * SMALL, (), own, peer, middle, cot, gain)


def attn_backward(windows, branch, x, kept, qkv, proj):
    rows, features = branch.shape
    width = proj.shape[0]
    groups = width // LANES
    outs = [shape_of(3, rows, width, dtype=BF), shape_of(1, 2 * width), shape_of(groups, SLOT, GROUP * SLOT),
            shape_of(rows, features, dtype=BF), shape_of(2, features)]
    scratch = [pltpu.VMEM((groups, SLOT * (windows + 1), LANES), F32)] * 4
    return call(functools.partial(attn_backward_kernel, windows), outs, scratch, "attn_backward", SMALL, (),
                branch, x, *kept, qkv, proj)


def attn_weights(split, me, sums2, gb1, blocks):
    features = blocks[0][0].shape[0]
    width = blocks[0][1].shape[1]
    grads = [shape_of(3, features, width, dtype=BF), shape_of(width, features, dtype=BF)]
    outs = ([shape_of(2, 4, BLOCK, features, dtype=BF)] * 2 if split else grads) + [shape_of(16, features, dtype=BF)]
    scratch = like(*grads) + [pltpu.VMEM((16 * SLOT, LANES), F32)]
    flat = [a for b in blocks for a in b]
    return call(functools.partial(attn_weights_kernel, len(blocks), split), outs, scratch + dma(64),
                "attn_weights", SMALL, (me,), sums2, gb1, *flat, far_outs=(0, 1))


def input_back(own, peer, x, gain, gmiddle):
    rows, features = x.shape
    return call(input_back_kernel, [shape_of(rows, features, dtype=BF)], [], "input_back", SMALL, (),
                own, peer, x, gain, gmiddle)[0]


def finish(me, y_rel, sources, outs, before=()):
    scratch = like(*sources, *outs) + dma(2, 8 * 4)
    return call(functools.partial(finish_kernel, (y_rel,)), list(outs), scratch, "finish", SMALL, (me,), *sources, *before,
                far=range(2 + len(before)), far_outs=range(len(outs)), aliases={3: 0, 4: 1} if before else {})


def finish_mlp(me, sources):
    features = sources[0].shape[2]
    outs = [shape_of(features, 2 * features), shape_of(2 * features, features), shape_of(16, features)]
    scratch = like(*sources, *outs[:2]) + [pltpu.VMEM((16, 16, features), F32)] + dma(4, (2, 16))
    return call(finish_mlp_kernel, outs, scratch, "finish_mlp", SMALL, (me,), *sources, far=range(4), far_outs=(0, 1))


def across(v):
    return lax.ppermute(v, "mp", [(0, 1), (1, 0)])


def flip(v, bits):
    return lax.ppermute(v, "dp", [(i, i ^ bits) for i in range(16)])


def after(v, *others):
    return lax.optimization_barrier((v, *others))[0]


def total_of(terms):
    total = terms[0].astype(F32)
    for t in terms[1:]:
        total = total + t.astype(F32)
    return total.astype(BF)


def side_send(keep, got):
    return total_of([keep[1], got[1]])


def line_sends(keep, got, side):
    return [total_of([keep[0, k], got[0, k], side[k]]) for k in (1, 2, 3)]


def own_piece(keep, got, side, line):
    return total_of([keep[0, 0], got[0, 0], side[0], *line])


def flip_line(pieces):
    return [flip(p, LINE * k) for k, p in zip((1, 2, 3), pieces)]


def gather_line(piece):
    far = flip(piece, 2 * LINE)
    return [flip(piece, LINE), far, flip(far, LINE)]


def shards(
    dp_size,
    mp_size,
    patches,
    token_valid,
    ln1_gain,
    ln1_shift,
    qkv_weight,
    qv_bias,
    bias_table,
    proj_weight,
    proj_bias,
    ln2_gain,
    ln2_shift,
    fc1_weight,
    fc1_bias,
    fc2_weight,
    fc2_bias,
    cotangent,
):
    windows, _, features = patches.shape
    rows = windows * WIN
    width = proj_weight.shape[0]
    heads = width // HEAD
    fast = mp_size == 2 and dp_size == 16 and features == 768
    x = patches.transpose(1, 0, 2).reshape(rows, features)
    cot = cotangent.transpose(1, 0, 2).reshape(rows, features)
    row = lambda a: a.reshape(1, -1)
    extra = -width % LANES
    qkv = jnp.pad(qkv_weight.transpose(1, 0, 2), ((0, 0), (0, 0), (0, extra)))
    proj = jnp.pad(proj_weight, ((0, extra), (0, 0)))
    pos = position(bias_table.T)
    bias = jnp.pad(qv_bias, ((0, 0), (0, extra)))
    valid = token_valid.astype(F32)
    ln1, ln2 = (ln1_gain, ln1_shift), (ln2_gain, ln2_shift)

    def blocks_of(v):
        return [v, across(v)] if fast else list(lax.all_gather(v, "mp"))

    def own_sums(parts):
        if fast:
            return parts[0], across(parts[1])
        own = lax.psum_scatter(jnp.concatenate(parts), "mp", scatter_dimension=0, tiled=True)
        return own, jnp.zeros_like(own)

    index = lax.axis_index("dp").astype(jnp.int32)
    me = index.reshape(1)
    valids = blocks_of(valid)
    kept, xs = [], []
    for x_b, valid_b in zip(blocks_of(x), valids):
        if kept:
            x_b = after(x_b, kept[0][4])
        xs.append(x_b)
        kept.append(attn_forward(windows, x_b, ln1, qkv, bias, pos, valid_b))
    project = lambda mixed, weight: jnp.dot(mixed, weight, preferred_element_type=F32).astype(BF)
    if fast:
        core = index & 1
        half = across(lax.dynamic_slice_in_dim(after(proj, valids[1]), core * (width // 2), width // 2, 0))
        cots = [cot, across(after(cot, valids[1]))]
        mixed = across(after(kept[1][4], cots[1], half))
        half = after(half, kept[1][4])
        rest = flip(half, CORE)
        parts, halves = (project(kept[0][4], proj), mixed), (half, rest)
    else:
        parts, halves = own_sums([project(k[4], proj) for k in kept]), ()
        cots = blocks_of(cot)
    middle, nm = middle_norm(me, x, *parts, proj_bias, ln2, halves)

    blocks, outs, gmids = [], [], []
    for nm_b, cot_b in zip(blocks_of(nm), cots):
        if blocks:
            nm_b = after(nm_b, gmids[-1])
        hid, gpre, out_b, gmid_b = mlp(nm_b, cot_b, fc1_weight, row(fc1_bias), fc2_weight)
        blocks.append((nm_b, cot_b, hid, gpre))
        outs.append(out_b)
        gmids.append(gmid_b)
    gmid_own, gmid_peer = own_sums(gmids)
    gb1, *g_mlp = mlp_weights(fast, me, blocks)
    outs = own_sums(outs)
    gmid_peer = after(gmid_peer, gb1)
    gmiddle, branch, sums2 = middle_back(gmid_own, gmid_peer, middle, cot, ln2[0])
    branches = blocks_of(branch)
    if fast:
        keep1, send1, keep2, send2 = g_mlp
        got1, got2 = after(flip(send1, CORE), branch), after(flip(send2, CORE), branch)
        side1, side2 = side_send(keep1, got1), side_send(keep2, got2)
        branches[0] = after(branches[0], side1, side2)
    backs, gparts = [], []
    for b, kept_b in enumerate(kept):
        if b == 1 and fast:
            side1 = after(flip(side1, SIDE), gparts[0])
            line1 = line_sends(keep1, got1, side1)
            branches[1] = after(branches[1], *line1, gparts[0])
        *back, gpart, gsum = attn_backward(windows, branches[b], xs[b], kept_b[:4], qkv, proj)
        backs.append((*back, gsum))
        gparts.append(gpart)
    if fast:
        side2 = after(flip(side2, SIDE), gparts[1])
        line2 = line_sends(keep2, got2, side2)
        line1 = [after(r, gparts[1]) for r in flip_line(line1)]
        piece1 = own_piece(keep1, got1, side1, line1)
        branches[0] = after(branches[0], piece1, *line2, outs[1])
    *g_attn, small = attn_weights(
        fast, me, sums2, gb1, [(k[5], k[4], br, *back) for k, br, back in zip(kept, branches, backs)])
    gnorms = own_sums(gparts)
    gpatch = input_back(*gnorms, x, ln1[0], gmiddle)
    output = (middle + outs[0].astype(F32) + outs[1].astype(F32) + row(fc2_bias)).astype(BF)

    if fast:
        line2 = [after(r, small) for r in flip_line(line2)]
        piece2 = own_piece(keep2, got2, side2, line2)
        keep, send = g_attn
        got = flip(after(send, piece2), CORE)
        side = after(flip(side_send(keep, got), SIDE), gnorms[1])
        fc = jnp.concatenate([piece1, piece2, small], axis=0)
        near, far, both = line_sends(keep, got, side)
        both = flip(both, LINE)
        fc_quad = jnp.stack([fc] + [after(r, both) for r in gather_line(fc)])
        line = [after(flip(near, LINE), output, gpatch), flip(total_of([far, both]), 2 * LINE)]
        piece = own_piece(keep, got, side, line)
        quad = jnp.stack([piece] + gather_line(piece))
        fc_pair = after(flip(fc_quad, SIDE), quad)
        g_fc1, g_fc2, small = finish_mlp(me, (fc_quad, fc_pair, after(flip(fc_quad, CORE), quad), after(flip(fc_pair, CORE), quad)))
        totals = small[0:6] + across(small[0:6])
        pair = after(flip(quad, SIDE), totals)
        shapes = shape_of(3, features, width), shape_of(width, features)
        half_done = finish(me, 0, (quad, flip(quad, CORE)), shapes)
        pair = after(pair, half_done[0])
        gw, gproj = finish(me, 1, (pair, flip(pair, CORE)), shapes, half_done)
    else:
        g_fc1, g_fc2, gw, gproj = [g.astype(F32) for g in lax.psum((*g_mlp, *g_attn), "dp")]
        gw, gproj = gw[:, :, :width], gproj[:width]
        small = lax.psum(small, "dp").astype(F32)
        totals = lax.psum(small[0:6], "mp")
    padded = width + extra
    gqv = jnp.stack([small[6, :width], small[6, padded : padded + width]])
    gb1 = small[7:12].reshape(-1)[: gb1.size]
    gt = small[12:].reshape(12, 2 * LANES)[:heads, :REL].T

    unrow = lambda a: a.reshape(WIN, windows, features).transpose(1, 0, 2)
    return (
        unrow(output),
        unrow(gpatch),
        totals[0],
        totals[1],
        gw.transpose(1, 0, 2),
        gqv,
        gt,
        gproj,
        totals[4],
        totals[2],
        totals[3],
        g_fc1,
        gb1,
        g_fc2,
        totals[5],
    )


def solution(mesh):
    placed = (
        P(("dp", "mp"), None, None),
        P(("dp", "mp"), None),
        P(),
        P(),
        P(None, None, "mp"),
        P(None, "mp"),
        P(None, "mp"),
        P("mp", None),
        P(),
        P(),
        P(),
        P(None, "mp"),
        P("mp"),
        P("mp", None),
        P(),
        P(("dp", "mp"), None, None),
    )
    return jax.shard_map(
        functools.partial(shards, mesh.shape["dp"], mesh.shape["mp"]),
        mesh=mesh,
        in_specs=placed,
        out_specs=(
            P(("dp", "mp"), None, None),
            P(("dp", "mp"), None, None),
            P(),
            P(),
            P(None, None, "mp"),
            P(None, "mp"),
            P(None, "mp"),
            P("mp", None),
            P(),
            P(),
            P(),
            P(None, "mp"),
            P("mp"),
            P("mp", None),
            P(),
        ),
        check_vma=False,
    )
```

```python
import functools

import jax
import jax.numpy as jnp
from jax import lax
from jax.experimental import pallas as pl
from jax.experimental.pallas import tpu as pltpu
from jax.sharding import PartitionSpec as P

HEAD = 32
WSIDE = 7
WIN = 49
REL = 169
SLOT = 64
GROUP = 4
LANES = 128
EPS = 1e-05
SCALING = HEAD ** (-0.5)
BF = jnp.bfloat16
F32 = jnp.float32
HIGH = lax.Precision.HIGHEST
VMEM_LIMIT = 28 * 1024 * 1024
ALL_VMEM = 58 * 1024 * 1024
BLOCK = 96
CORE, SIDE, LINE = 1, 2, 4

ROW_COL = (((1,), (0,)), ((), ()))
LAST_LAST = (((1,), (1,)), ((), ()))
ROWS_ROWS = (((0,), (0,)), ((), ()))


def mm(a, b, dims=ROW_COL):
    return lax.dot_general(a, b, dims, preferred_element_type=F32)


def norm_parts(rows):
    mean = jnp.mean(rows, axis=-1, keepdims=True)
    centred = rows - mean
    variance = jnp.mean(centred * centred, axis=-1, keepdims=True)
    inv = lax.rsqrt(variance + EPS)
    return centred * inv, inv


def norm_back(xhat, inv, gain, upstream):
    z = upstream * gain
    mean_z = jnp.mean(z, axis=-1, keepdims=True)
    mean_zx = jnp.mean(z * xhat, axis=-1, keepdims=True)
    return (z - mean_z - xhat * mean_zx) * inv


def head_masks():
    lane = lax.broadcasted_iota(jnp.int32, (SLOT, LANES), 1)
    return [jnp.where((lane >> 5) == h, 1.0, 0.0).astype(BF) for h in range(GROUP)]


def block_ones():
    row = lax.broadcasted_iota(jnp.int32, (GROUP * SLOT, GROUP * SLOT), 0)
    col = lax.broadcasted_iota(jnp.int32, (GROUP * SLOT, GROUP * SLOT), 1)
    return jnp.where((row >> 6) == (col >> 6), 1.0, 0.0).astype(BF)


def spread(tile, masks):
    return jnp.concatenate([tile * m for m in masks], axis=0)


def collect(full, masks_f):
    total = full[0:SLOT] * masks_f[0]
    for h in range(1, GROUP):
        total = total + full[h * SLOT : (h + 1) * SLOT] * masks_f[h]
    return total


def fill(scratch, rows, windows):
    pitch = windows + 1
    for g in range(scratch.shape[0]):
        for place in range(WIN):
            scratch[g, place * pitch : place * pitch + windows, :] = rows[
                place * windows : (place + 1) * windows, g * LANES : (g + 1) * LANES]
        scratch[g, WIN * pitch :, :] = jnp.zeros((scratch.shape[1] - WIN * pitch, LANES), rows.dtype)


def empty(scratch, windows):
    pitch = windows + 1
    planes = [
        jnp.concatenate([scratch[g, place * pitch : place * pitch + windows, :] for place in range(WIN)], axis=0)
        for g in range(scratch.shape[0])
    ]
    return jnp.concatenate(planes, axis=1).astype(BF)


def row_max(tile, low_half):
    low = jnp.max(jnp.where(low_half, tile, -3e38), axis=-1, keepdims=True)
    high = jnp.max(jnp.where(low_half, -3e38, tile), axis=-1, keepdims=True)
    return jnp.where(low_half, low, high)


def row_sum(tile, low_half):
    low = jnp.sum(jnp.where(low_half, tile, 0.0), axis=-1, keepdims=True)
    high = jnp.sum(jnp.where(low_half, 0.0, tile), axis=-1, keepdims=True)
    return jnp.where(low_half, low, high)


def ds(start, size):
    unit = 384 if size % 384 == 0 else 48
    return pl.ds(pl.multiple_of(start, unit), size)


def each_block(me, *by_core):
    for c_rel, target in enumerate(by_core):
        for y_rel in range(2):
            for z_rel in range(4):
                yield target, y_rel, z_rel, (me & 1) ^ c_rel, ((me >> 1) & 1) ^ y_rel, (me >> 2) ^ z_rel


def line(ref):
    return ref[...].reshape(1, -1)


def begin(sems, *pairs):
    copies = [pltpu.make_async_copy(a, b, sems.at[i]) for i, (a, b) in enumerate(pairs)]
    for copy in copies:
        copy.start()
    return copies


def finish_all(copies):
    for copy in copies:
        copy.wait()


def attn_forward_kernel(windows, x_in, gain_ref, shift_ref, w_in, bias_ref, pos_ref, valid_ref,
                        prob_ref, q_ref, k_ref, v_ref, mixed_ref, normed_t_ref,
                        mask_s, q_s, k_s, v_s, mixed_s, x_ref, w_ref, in_sems):
    copies = begin(in_sems, (x_in, x_ref), *[(w_in.at[p], w_ref.at[p]) for p in range(3)])
    mask_s[...] = jnp.zeros(mask_s.shape, F32)
    for h in range(GROUP):
        mask_s[:, h * SLOT : h * SLOT + WIN] = valid_ref[...].astype(F32)
    masks = head_masks()
    ones = block_ones()
    low_half = lax.broadcasted_iota(jnp.int32, (SLOT, LANES), 1) < SLOT
    copies[0].wait()
    x = x_ref[...].astype(F32)
    rows = x.shape[0]
    groups = q_s.shape[0]
    xhat, _ = norm_parts(x)
    normed = (xhat * line(gain_ref) + line(shift_ref)).astype(BF)
    normed_t_ref[...] = normed.T
    for part, scratch in enumerate((q_s, k_s, v_s)):
        copies[1 + part].wait()
        got = mm(normed, w_ref[part])
        if part != 1:
            got = got + bias_ref[part // 2 : part // 2 + 1, :]
        fill(scratch, got.astype(BF).astype(F32), windows)

    def window(w, carry):
        allowed = jnp.broadcast_to(mask_s[pl.ds(w, 1), :], (SLOT, GROUP * SLOT)) > 0.5
        for g in range(groups):
            cols = slice(g * LANES, (g + 1) * LANES)
            places = pl.ds(w, SLOT, stride=windows + 1)
            q = q_s[g, places, :].astype(BF)
            k = k_s[g, places, :].astype(BF)
            v = v_s[g, places, :].astype(BF)
            q_ref[w, :, cols] = q
            k_ref[w, :, cols] = k
            v_ref[w, :, cols] = v
            scores = mm(q, spread(k, masks), LAST_LAST) * SCALING + pos_ref[g]
            scores = jnp.where(allowed, scores, -1000000000.0)
            top = jnp.concatenate([row_max(scores[:, :LANES], low_half), row_max(scores[:, LANES:], low_half)], axis=1)
            e = jnp.exp(scores - top)
            total = mm(e.astype(BF), ones)
            inv = pl.reciprocal(total, approx=True)
            prob = (e * (inv * (2.0 - total * inv))).astype(BF)
            prob_ref[w, g] = prob
            mixed_s[g, places, :] = mm(prob, spread(v, masks))
        return carry

    lax.fori_loop(0, windows, window, 0, unroll=2)
    mixed_ref[...] = empty(mixed_s, windows)


def middle_kernel(heads, me_ref, x_in, own_in, peer_in, bias_ref, gain_ref, shift_ref, *refs):
    if heads:
        half_in, rest_in, middle_ref, nm_ref, x_ref, own_ref, peer_ref, proj_ref, sems = refs
        lines = half_in.shape[0]
        core = me_ref[0] & 1
        place = lambda c: proj_ref.at[pl.ds(pl.multiple_of(c * lines, lines), lines), :]
        copies = begin(sems, (peer_in, peer_ref), (half_in, place(core)), (rest_in, place(1 - core)), (x_in, x_ref),
                       (own_in, own_ref))
        finish_all(copies[:3])
        peer = mm(peer_ref[...], proj_ref[...])
        finish_all(copies[3:])
    else:
        middle_ref, nm_ref, x_ref, own_ref, peer_ref, sems = refs
        finish_all(begin(sems, (x_in, x_ref), (own_in, own_ref), (peer_in, peer_ref)))
        peer = peer_ref[...].astype(F32)
    middle = x_ref[...].astype(F32) + (own_ref[...].astype(F32) + peer) + line(bias_ref)
    middle_ref[...] = middle
    xhat, _ = norm_parts(middle)
    nm_ref[...] = (xhat * line(gain_ref) + line(shift_ref)).astype(BF)


def mlp_kernel(nm_ref, cot_ref, fc1_ref, b1_ref, fc2_ref, hid_ref, gpre_ref, out_ref, gmid_ref):
    hidden_size = fc1_ref.shape[1]
    features = fc1_ref.shape[0]
    step = 256 if hidden_size % 256 == 0 else 128
    count = hidden_size // step

    nm = nm_ref[...]
    cot = cot_ref[...]

    def units(c, carry):
        cols = pl.ds(pl.multiple_of(c * step, step), step)
        pre = mm(nm, fc1_ref[:, cols]) + b1_ref[:, cols]
        phi = 0.5 * (1.0 + lax.erf(pre * (0.5 ** 0.5)))
        hid_ref[:, cols] = (pre * phi).astype(BF)
        slope = phi + pre * (jnp.exp(-0.5 * pre * pre) * 0.3989422804014327)
        gpre_ref[:, cols] = (mm(cot, fc2_ref[cols, :], LAST_LAST) * slope).astype(BF)
        return carry

    lax.fori_loop(0, count, units, 0)

    def tile(c, carry):
        cols = pl.ds(pl.multiple_of(c * 256, 256), 256)
        gmid_ref[:, cols] = mm(gpre_ref[...], fc1_ref[cols, :], LAST_LAST).astype(BF)
        out_ref[:, cols] = mm(hid_ref[...], fc2_ref[:, cols]).astype(BF)
        return carry

    lax.fori_loop(0, features // 256, tile, 0)

def mlp_weights_kernel(count, split, me_ref, *refs):
    inputs, refs = refs[: 4 * count], refs[4 * count :]
    n_out = 5 if split else 3
    gb1_ref, *outs = refs[:n_out]
    held = refs[n_out : n_out + 4 * count]
    nts = refs[n_out + 4 * count : n_out + 5 * count]
    g1_ref, g2_ref, in_sems, unit_sems, out_sems = refs[n_out + 5 * count :]
    blocks = [held[4 * b : 4 * b + 4] for b in range(count)]
    hidden_size = g1_ref.shape[1]
    features = g1_ref.shape[0]
    step = 384 if hidden_size % 384 == 0 else 128
    wide = features if hidden_size % features == 0 else step

    def units_in(j):
        cols = ds(j * step, step)
        return [pltpu.make_async_copy(inputs[4 * b + 2].at[:, cols], held[4 * b + 2].at[:, cols], unit_sems.at[b, j])
                for b in range(count)]

    order = [4 * b + k for k in (0, 1) for b in range(count)]
    copies = dict(zip(order, begin(in_sems, *[(inputs[i], held[i]) for i in order])))
    for j in range(hidden_size // step):
        for copy in units_in(j):
            copy.start()
    last = [pltpu.make_async_copy(inputs[4 * b + 3], held[4 * b + 3], in_sems.at[2 * count + b]) for b in range(count)]
    for copy in last:
        copy.start()
    finish_all([copies[4 * b] for b in range(count)])
    for block, nt in zip(blocks, nts):
        nt[...] = block[0][...].T
    finish_all([copies[4 * b + 1] for b in range(count)])

    def second(j, carry):
        finish_all(units_in(j))
        cols = ds(j * step, step)
        g2_ref[cols, :] = sum(mm(hid_ref[:, cols], cot_ref[...], ROWS_ROWS) for _, cot_ref, hid_ref, _ in blocks).astype(BF)
        return carry

    def first(j, carry):
        cols = ds(j * wide, wide)
        g1_ref[:, cols] = sum(mm(nt[...], block[3][:, cols]) for nt, block in zip(nts, blocks)).astype(BF)
        return carry

    lax.fori_loop(0, hidden_size // step, second, 0)
    me = me_ref[0]
    sent = []

    def send(k, source, target):
        sent.append(pltpu.make_async_copy(source, target, out_sems.at[k]))
        sent[-1].start()

    if split:
        for i, (target, y_rel, z_rel, c, y, z) in enumerate(each_block(me, outs[2], outs[3])):
            send(i, g2_ref.at[ds(c * 768 + y * 384 + z * 96, 96), :], target.at[y_rel, z_rel])
    else:
        send(0, g2_ref, outs[1])
    finish_all(last)
    gb1_ref[...] = sum(jnp.sum(block[3][...].astype(F32), axis=0, keepdims=True) for block in blocks)
    lax.fori_loop(0, hidden_size // wide, first, 0)
    if split:
        for i, (target, y_rel, z_rel, c, y, z) in enumerate(each_block(me, outs[0], outs[1])):
            send(16 + i, g1_ref.at[ds(y * 384 + z * 96, 96), ds(c * 768, 768)], target.at[y_rel, z_rel])
    else:
        send(1, g1_ref, outs[0])
    finish_all(sent)


def middle_back_kernel(own_ref, peer_ref, middle_ref, cot_ref, gain_ref, gmiddle_ref, branch_ref, sums_ref):
    upstream = cot_ref[...].astype(F32)
    xhat, inv = norm_parts(middle_ref[...])
    gmid = own_ref[...].astype(F32) + peer_ref[...].astype(F32)
    sums_ref[0:1, :] = jnp.sum(gmid * xhat, axis=0, keepdims=True)
    sums_ref[1:2, :] = jnp.sum(gmid, axis=0, keepdims=True)
    gmiddle = upstream + norm_back(xhat, inv, line(gain_ref), gmid)
    gmiddle_ref[...] = gmiddle
    branch_ref[...] = gmiddle.astype(BF)
    sums_ref[2:3, :] = jnp.sum(gmiddle, axis=0, keepdims=True)
    sums_ref[3:4, :] = jnp.sum(upstream, axis=0, keepdims=True)


def attn_backward_kernel(windows, branch_ref, x_ref, prob_ref, q_ref, k_ref, v_ref, w_ref, proj_ref,
                         grads_ref, gqv_ref, gpos_ref, part_ref, sums_ref, gm_s, gq_s, gk_s, gv_s):
    rows = branch_ref.shape[0]
    groups = gm_s.shape[0]
    gpos_ref[...] = jnp.zeros(gpos_ref.shape, F32)
    masks = head_masks()
    masks_f = [m.astype(F32) for m in masks]
    low_half = lax.broadcasted_iota(jnp.int32, (SLOT, LANES), 1) < SLOT
    fill(gm_s, mm(branch_ref[...], proj_ref[...], LAST_LAST).astype(BF).astype(F32), windows)

    def window(w, carry):
        for g in range(groups):
            cols = slice(g * LANES, (g + 1) * LANES)
            places = pl.ds(w, SLOT, stride=windows + 1)
            gm = gm_s[g, places, :].astype(BF)
            q = q_ref[w, :, cols]
            k = k_ref[w, :, cols]
            v = v_ref[w, :, cols]
            prob = prob_ref[w, g]
            prob_f = prob.astype(F32)
            gprob = mm(gm, spread(v, masks), LAST_LAST)
            both = prob_f * gprob
            delta = jnp.concatenate([row_sum(both[:, :LANES], low_half), row_sum(both[:, LANES:], low_half)], axis=1)
            gs = (both - prob_f * delta).astype(BF)
            gpos_ref[g] += gs.astype(F32)
            gq_s[g, places, :] = mm(gs, spread(k, masks)) * SCALING
            gk_s[g, places, :] = collect(mm(gs, q, ROWS_ROWS), masks_f) * SCALING
            gv_s[g, places, :] = collect(mm(prob, gm, ROWS_ROWS), masks_f)
        return carry

    lax.fori_loop(0, windows, window, 0, unroll=2)
    back = None
    for part, scratch in enumerate((gq_s, gk_s, gv_s)):
        grad = empty(scratch, windows)
        grads_ref[part] = grad
        if part != 1:
            width = grad.shape[1]
            lanes = slice(part // 2 * width, (part // 2 + 1) * width)
            gqv_ref[:, lanes] = jnp.sum(grad.astype(F32), axis=0, keepdims=True)
        term = mm(grad, w_ref[part], LAST_LAST)
        back = term if back is None else back + term
    part_ref[...] = back.astype(BF)
    xhat, _ = norm_parts(x_ref[...].astype(F32))
    sums_ref[0:1, :] = jnp.sum(back * xhat, axis=0, keepdims=True)
    sums_ref[1:2, :] = jnp.sum(back, axis=0, keepdims=True)


def place_offset(i):
    return i // WSIDE * (2 * WSIDE - 1) + i % WSIDE


def offset_picks():
    row = lax.broadcasted_iota(jnp.int32, (2 * LANES, 2 * SLOT), 0)
    col = lax.broadcasted_iota(jnp.int32, (2 * LANES, 2 * SLOT), 1)
    j = col & (SLOT - 1)
    line = (j * 37) >> 8
    offset = place_offset(WIN - 1) - line * (2 * WSIDE - 1) - (j - line * WSIDE)
    hit = ((row & (LANES - 1)) == offset) & ((row >> 7) == (col >> 6)) & (j < WIN)
    return jnp.where(hit, 1.0, 0.0).astype(BF)


def position_kernel(table_ref, pos_ref, table_s, rows_s):
    heads = table_ref.shape[0]
    table_s[...] = jnp.zeros(table_s.shape, F32)
    table_s[0:heads, 0:REL] = table_ref[...]
    table = table_s[...]
    lines = table.shape[0]
    rows_s[WIN * lines :, :] = jnp.zeros((rows_s.shape[0] - WIN * lines, LANES), F32)
    for i in range(WIN):
        turned = pltpu.roll(table, (2 * LANES - place_offset(i)) % (2 * LANES), 1)
        rows_s[i * lines : (i + 1) * lines, :] = turned[:, :LANES]
    picks = offset_picks()
    for pair in range(pos_ref.shape[0] * 2):
        pieces = [rows_s[pl.ds(2 * pair + k, SLOT, stride=lines), :] for k in range(2)]
        rest = jnp.concatenate(pieces, axis=1)
        total = jnp.zeros((SLOT, 2 * SLOT), F32)
        for _ in range(3):
            top = rest.astype(BF)
            total = total + mm(top, picks)
            rest = rest - top.astype(F32)
        pos_ref[pair // 2, :, pair % 2 * LANES : (pair % 2 + 1) * LANES] = total


def attn_weights_kernel(count, split, me_ref, sums2_ref, gb1_ref, *refs):
    blocks, refs = [refs[7 * b : 7 * b + 7] for b in range(count)], refs[7 * count :]
    *outs, small_ref = refs[:3]
    gw_ref, gproj_ref, rows_s, out_sems = refs[3:]
    gproj, gqv, gpos, sums = 0.0, 0.0, 0.0, 0.0
    for _, mixed_ref, branch_ref, _, gqv_ref, gpos_ref, sums_ref in blocks:
        gproj = gproj + mm(mixed_ref[...], branch_ref[...], ROWS_ROWS)
        gqv, gpos, sums = gqv + gqv_ref[...], gpos + gpos_ref[...], sums + sums_ref[...]
    width, features = gproj.shape
    gproj_ref[...] = gproj.astype(BF)
    hidden = gb1_ref.shape[1]
    lines = [sums[k : k + 1] for k in range(2)] + [sums2_ref[k : k + 1, :] for k in range(4)]
    lines.append(gqv)
    lines += [gb1_ref[:, k : min(k + features, hidden)] for k in range(0, hidden, features)]
    small = jnp.concatenate(
        [jnp.concatenate([line, jnp.zeros((1, features - line.shape[1]), F32)], axis=1) if line.shape[1] < features else line
         for line in lines] + [jnp.zeros((12 - len(lines), features), F32)], axis=0)
    picks = offset_picks()
    for pair in range(gpos.shape[0] * 2):
        rest = gpos[pair // 2][:, pair % 2 * LANES : (pair % 2 + 1) * LANES]
        total = jnp.zeros((SLOT, 2 * LANES), F32)
        for _ in range(2):
            top = rest.astype(BF)
            total = total + mm(top, picks, LAST_LAST)
            rest = rest - top.astype(F32)
        for k in range(2):
            rows_s[pl.ds(2 * pair + k, SLOT, stride=16), :] = total[:, k * LANES : (k + 1) * LANES]
    for h in range(gpos.shape[0] * 4, 16):
        rows_s[pl.ds(h, SLOT, stride=16), :] = jnp.zeros((SLOT, LANES), F32)
    table = jnp.zeros((16, 2 * LANES), F32)
    for i in range(WIN):
        row = jnp.concatenate([rows_s[i * 16 : (i + 1) * 16, :], jnp.zeros((16, LANES), F32)], axis=1)
        table = table + (pltpu.roll(row, place_offset(i), 1) if i else row)
    packed = [jnp.concatenate([table[3 * r + k : 3 * r + k + 1] for k in range(3)], axis=1) for r in range(4)]
    small_ref[...] = jnp.concatenate([small] + packed, axis=0).astype(BF)
    sent = []

    def send(k, source, target):
        sent.append(pltpu.make_async_copy(source, target, out_sems.at[k]))
        sent[-1].start()

    if split:
        for i, (target, y_rel, z_rel, c, y, z) in enumerate(each_block(me_ref[0], *outs)):
            send(i, gproj_ref.at[ds((c * 4 + y * 2 + (z >> 1)) * 48, 48), ds((z & 1) * 384, 384)],
                 target.at[y_rel, z_rel, 48:96, 384:768])
    else:
        send(0, gproj_ref, outs[1])
    for part in range(3):
        gw = 0.0
        for normed_t_ref, _, _, grads_ref, _, _, _ in blocks:
            gw = gw + mm(normed_t_ref[...], grads_ref[part])
        gw_ref[part] = gw.astype(BF)
        if split:
            for i, (target, y_rel, z_rel, c, y, z) in enumerate(each_block(me_ref[0], *outs)):
                send(16 * (part + 1) + i, gw_ref.at[part, ds(c * 384 + y * 192 + z * 48, 48), :],
                     target.at[y_rel, z_rel, part // 2 * 48 : part // 2 * 48 + 48, part % 2 * 384 : part % 2 * 384 + 384])
        else:
            send(1 + part, gw_ref.at[part], outs[0].at[part])
    finish_all(sent)


def input_back_kernel(own_ref, peer_ref, x_ref, gain_ref, gmiddle_ref, gpatch_ref):
    gnorm = own_ref[...].astype(F32) + peer_ref[...].astype(F32)
    xhat, inv = norm_parts(x_ref[...].astype(F32))
    gpatch_ref[...] = (gmiddle_ref[...] + norm_back(xhat, inv, line(gain_ref), gnorm)).astype(BF)


def finish_kernel(y_rels, me_ref, *refs):
    sources, refs = refs[:2], refs[2:]
    if y_rels[0] == 1:
        refs = refs[2:]
    outs, held, wide, (in_sems, out_sems) = refs[:2], refs[2:4], refs[4:6], refs[6:]
    copies = begin(in_sems, *zip(sources, held))
    sent = []

    def put(value, k, where):
        wide[k][where] = value.astype(F32)
        sent.append(pltpu.make_async_copy(wide[k].at[where], outs[k].at[where], out_sems.at[len(sent)]))
        sent[-1].start()

    for source, y_rel, z_rel, c, y, z in each_block(me_ref[0], 0, 1):
        if y_rel not in y_rels:
            continue
        if z_rel == 0:
            copies[source].wait()
        piece = held[source].at[z_rel]
        lines = ds(c * 384 + y * 192 + z * 48, 48)
        put(piece[0:48, 0:384], 0, (0, lines, slice(None)))
        put(piece[0:48, 384:768], 0, (1, lines, slice(None)))
        put(piece[48:96, 0:384], 0, (2, lines, slice(None)))
        put(piece[48:96, 384:768], 1, (ds((c * 4 + y * 2 + (z >> 1)) * 48, 48), ds((z & 1) * 384, 384)))
    finish_all(sent)


def finish_mlp_kernel(me_ref, *refs):
    sources, (g1_out, g2_out, small_ref), held, (g1_ref, g2_ref, small_s, in_sems, out_sems) = (
        refs[:4], refs[4:7], refs[7:11], refs[11:])
    copies = begin(in_sems, *zip(sources, held))
    sent = []

    def put(value, k, wide, out, where):
        wide[where] = value.astype(F32)
        sent.append(pltpu.make_async_copy(wide.at[where], out.at[where], out_sems.at[k, len(sent) // 2]))
        sent[-1].start()

    for source, y_rel, z_rel, c, y, z in each_block(me_ref[0], (0, 1), (2, 3)):
        source = source[y_rel]
        if z_rel == 0:
            copies[source].wait()
        piece = held[source].at[z_rel]
        put(piece[0:BLOCK, :], 0, g1_ref, g1_out, (ds(y * 384 + z * 96, 96), ds(c * 768, 768)))
        put(piece[BLOCK : 2 * BLOCK, :], 1, g2_ref, g2_out, (ds(c * 768 + y * 384 + z * 96, 96), slice(None)))
        small_s[z * 4 + y * 2 + c] = piece[2 * BLOCK :, :].astype(F32)
    total = small_s[0]
    for d in range(1, 16):
        total = total + small_s[d]
    small_ref[...] = total
    finish_all(sent)


def shape_of(*dims, dtype=F32):
    return jax.ShapeDtypeStruct(dims, dtype)


def call(kernel, outs, scratch, name, flops, smem, *args, far=(), far_outs=(), limit=VMEM_LIMIT, aliases=None):
    space = lambda is_far: pl.BlockSpec(memory_space=pltpu.HBM if is_far else pltpu.VMEM)
    in_specs = [pl.BlockSpec(memory_space=pltpu.SMEM)] * len(smem) + [space(i in far) for i in range(len(args))]
    return pl.pallas_call(
        kernel,
        out_shape=outs,
        in_specs=in_specs,
        out_specs=[space(i in far_outs) for i in range(len(outs))],
        scratch_shapes=scratch,
        compiler_params=pltpu.CompilerParams(vmem_limit_bytes=limit),
        cost_estimate=pl.CostEstimate(flops=flops, bytes_accessed=flops // 256, transcendentals=0),
        input_output_aliases=aliases or {},
        name=name,
    )(*smem, *args)


def like(*arrays):
    return [pltpu.VMEM(a.shape, a.dtype) for a in arrays]


def dma(*counts):
    return [pltpu.SemaphoreType.DMA(c if isinstance(c, tuple) else (c,)) for c in counts]


SMALL = 1000000


def position(table):
    heads = table.shape[0]
    groups = -(-heads // GROUP)
    return call(position_kernel, [shape_of(groups, SLOT, GROUP * SLOT)],
                [pltpu.VMEM((16, 2 * LANES), F32), pltpu.VMEM((16 * SLOT, LANES), F32)], "position", SMALL, (), table)[0]


def attn_forward(windows, x, ln1, qkv, qv_bias, pos, mask):
    rows, features = x.shape
    width = qkv.shape[2]
    groups = width // LANES
    tile = shape_of(windows, SLOT, width, dtype=BF)
    outs = [shape_of(windows, groups, SLOT, GROUP * SLOT, dtype=BF), tile, tile, tile, shape_of(rows, width, dtype=BF),
            shape_of(features, rows, dtype=BF)]
    scratch = [pltpu.VMEM((windows, GROUP * SLOT), F32)] + [pltpu.VMEM((groups, SLOT * (windows + 1), LANES), F32)] * 4
    scratch += like(x, qkv) + dma(4)
    return call(functools.partial(attn_forward_kernel, windows), outs, scratch, "attn_forward", SMALL, (),
                x, *ln1, qkv, qv_bias, pos, mask, far=(0, 3), limit=ALL_VMEM)


def middle_norm(me, x, own, peer, bias, ln2, halves):
    rows, features = x.shape
    scratch = like(x, own, peer)
    if halves:
        scratch += [pltpu.VMEM((2 * halves[0].shape[0], features), BF)]
    return call(functools.partial(middle_kernel, bool(halves)), [shape_of(rows, features), shape_of(rows, features, dtype=BF)],
                scratch + dma(5), "middle", SMALL, (me,), x, own, peer, bias, *ln2, *halves, far=(0, 1, 2, 6, 7),
                limit=ALL_VMEM)


def mlp(nm, cot, fc1, fc1_bias, fc2):
    rows, features = nm.shape
    hidden = fc2.shape[0]
    outs = [shape_of(rows, hidden, dtype=BF)] * 2 + [shape_of(rows, features, dtype=BF)] * 2
    return call(mlp_kernel, outs, [], "mlp", SMALL, (), nm, cot, fc1, fc1_bias, fc2)


def mlp_weights(split, me, blocks):
    rows, features = blocks[0][0].shape
    hidden = blocks[0][2].shape[1]
    grads = [shape_of(features, hidden, dtype=BF), shape_of(hidden, features, dtype=BF)]
    outs = [shape_of(1, hidden)] + ([shape_of(2, 4, BLOCK, features, dtype=BF)] * 4 if split else grads)
    flat = [a for b in blocks for a in b]
    scratch = like(*flat) + [pltpu.VMEM((features, rows), BF)] * len(blocks) + like(*grads) + dma(3 * len(blocks), (len(blocks), hidden // 128), 32)
    return call(functools.partial(mlp_weights_kernel, len(blocks), split), outs, scratch, "mlp_weights", SMALL,
                (me,), *flat, far=range(len(flat)), far_outs=range(1, len(outs)), limit=ALL_VMEM)


def middle_back(own, peer, middle, cot, gain):
    rows, features = middle.shape
    return call(
        middle_back_kernel, [shape_of(rows, features), shape_of(rows, features, dtype=BF), shape_of(4, features)], [],
        "middle_back", 20000 * SMALL, (), own, peer, middle, cot, gain)


def attn_backward(windows, branch, x, kept, qkv, proj):
    rows, features = branch.shape
    width = proj.shape[0]
    groups = width // LANES
    outs = [shape_of(3, rows, width, dtype=BF), shape_of(1, 2 * width), shape_of(groups, SLOT, GROUP * SLOT),
            shape_of(rows, features, dtype=BF), shape_of(2, features)]
    scratch = [pltpu.VMEM((groups, SLOT * (windows + 1), LANES), F32)] * 4
    return call(functools.partial(attn_backward_kernel, windows), outs, scratch, "attn_backward", SMALL, (),
                branch, x, *kept, qkv, proj)


def attn_weights(split, me, sums2, gb1, blocks):
    features = blocks[0][0].shape[0]
    width = blocks[0][1].shape[1]
    grads = [shape_of(3, features, width, dtype=BF), shape_of(width, features, dtype=BF)]
    outs = ([shape_of(2, 4, BLOCK, features, dtype=BF)] * 2 if split else grads) + [shape_of(16, features, dtype=BF)]
    scratch = like(*grads) + [pltpu.VMEM((16 * SLOT, LANES), F32)]
    flat = [a for b in blocks for a in b]
    return call(functools.partial(attn_weights_kernel, len(blocks), split), outs, scratch + dma(64),
                "attn_weights", SMALL, (me,), sums2, gb1, *flat, far_outs=(0, 1))


def input_back(own, peer, x, gain, gmiddle):
    rows, features = x.shape
    return call(input_back_kernel, [shape_of(rows, features, dtype=BF)], [], "input_back", SMALL, (),
                own, peer, x, gain, gmiddle)[0]


def finish(me, y_rel, sources, outs, before=()):
    scratch = like(*sources, *outs) + dma(2, 8 * 4)
    return call(functools.partial(finish_kernel, (y_rel,)), list(outs), scratch, "finish", SMALL, (me,), *sources, *before,
                far=range(2 + len(before)), far_outs=range(len(outs)), aliases={3: 0, 4: 1} if before else {})


def finish_mlp(me, sources):
    features = sources[0].shape[2]
    outs = [shape_of(features, 2 * features), shape_of(2 * features, features), shape_of(16, features)]
    scratch = like(*sources, *outs[:2]) + [pltpu.VMEM((16, 16, features), F32)] + dma(4, (2, 16))
    return call(finish_mlp_kernel, outs, scratch, "finish_mlp", SMALL, (me,), *sources, far=range(4), far_outs=(0, 1))


def across(v):
    return lax.ppermute(v, "mp", [(0, 1), (1, 0)])


def flip(v, bits):
    return lax.ppermute(v, "dp", [(i, i ^ bits) for i in range(16)])


def after(v, *others):
    return lax.optimization_barrier((v, *others))[0]


def total_of(terms):
    total = terms[0].astype(F32)
    for t in terms[1:]:
        total = total + t.astype(F32)
    return total.astype(BF)


def side_send(keep, got):
    return total_of([keep[1], got[1]])


def line_sends(keep, got, side):
    return [total_of([keep[0, k], got[0, k], side[k]]) for k in (1, 2, 3)]


def own_piece(keep, got, side, line):
    return total_of([keep[0, 0], got[0, 0], side[0], *line])


def flip_line(pieces):
    return [flip(p, LINE * k) for k, p in zip((1, 2, 3), pieces)]


def sum_line(sends):
    near, far, both = sends
    return [flip(near, LINE), flip(total_of([far, flip(both, LINE)]), 2 * LINE)]


def gather_line(piece):
    far = flip(piece, 2 * LINE)
    return [flip(piece, LINE), far, flip(far, LINE)]


def shards(
    dp_size,
    mp_size,
    patches,
    token_valid,
    ln1_gain,
    ln1_shift,
    qkv_weight,
    qv_bias,
    bias_table,
    proj_weight,
    proj_bias,
    ln2_gain,
    ln2_shift,
    fc1_weight,
    fc1_bias,
    fc2_weight,
    fc2_bias,
    cotangent,
):
    windows, _, features = patches.shape
    rows = windows * WIN
    width = proj_weight.shape[0]
    heads = width // HEAD
    fast = mp_size == 2 and dp_size == 16 and features == 768
    x = patches.transpose(1, 0, 2).reshape(rows, features)
    cot = cotangent.transpose(1, 0, 2).reshape(rows, features)
    row = lambda a: a.reshape(1, -1)
    extra = -width % LANES
    qkv = jnp.pad(qkv_weight.transpose(1, 0, 2), ((0, 0), (0, 0), (0, extra)))
    proj = jnp.pad(proj_weight, ((0, extra), (0, 0)))
    pos = position(bias_table.T)
    bias = jnp.pad(qv_bias, ((0, 0), (0, extra)))
    valid = token_valid.astype(F32)
    ln1, ln2 = (ln1_gain, ln1_shift), (ln2_gain, ln2_shift)

    def blocks_of(v):
        return [v, across(v)] if fast else list(lax.all_gather(v, "mp"))

    def own_sums(parts):
        if fast:
            return parts[0], across(parts[1])
        own = lax.psum_scatter(jnp.concatenate(parts), "mp", scatter_dimension=0, tiled=True)
        return own, jnp.zeros_like(own)

    index = lax.axis_index("dp").astype(jnp.int32)
    me = index.reshape(1)
    valids = blocks_of(valid)
    kept, xs = [], []
    for x_b, valid_b in zip(blocks_of(x), valids):
        if kept:
            x_b = after(x_b, kept[0][4])
        xs.append(x_b)
        kept.append(attn_forward(windows, x_b, ln1, qkv, bias, pos, valid_b))
    project = lambda mixed, weight: jnp.dot(mixed, weight, preferred_element_type=F32).astype(BF)
    if fast:
        core = index & 1
        half = across(lax.dynamic_slice_in_dim(after(proj, valids[1]), core * (width // 2), width // 2, 0))
        cots = [cot, across(after(cot, valids[1]))]
        mixed = across(after(kept[1][4], cots[1], half))
        half = after(half, kept[1][4])
        rest = flip(half, CORE)
        parts, halves = (project(kept[0][4], proj), mixed), (half, rest)
    else:
        parts, halves = own_sums([project(k[4], proj) for k in kept]), ()
        cots = blocks_of(cot)
    middle, nm = middle_norm(me, x, *parts, proj_bias, ln2, halves)

    blocks, outs, gmids = [], [], []
    for nm_b, cot_b in zip(blocks_of(nm), cots):
        if blocks:
            nm_b = after(nm_b, gmids[-1])
        hid, gpre, out_b, gmid_b = mlp(nm_b, cot_b, fc1_weight, row(fc1_bias), fc2_weight)
        blocks.append((nm_b, cot_b, hid, gpre))
        outs.append(out_b)
        gmids.append(gmid_b)
    gmid_own, gmid_peer = own_sums(gmids)
    gb1, *g_mlp = mlp_weights(fast, me, blocks)
    outs = own_sums(outs)
    gmid_peer = after(gmid_peer, gb1)
    gmiddle, branch, sums2 = middle_back(gmid_own, gmid_peer, middle, cot, ln2[0])
    branches = blocks_of(branch)
    if fast:
        keep1, send1, keep2, send2 = g_mlp
        got1, got2 = after(flip(send1, CORE), branch), after(flip(send2, CORE), branch)
        side1, side2 = side_send(keep1, got1), side_send(keep2, got2)
        branches[0] = after(branches[0], side1, side2)
    backs, gparts = [], []
    for b, kept_b in enumerate(kept):
        if b == 1 and fast:
            side1 = after(flip(side1, SIDE), gparts[0])
            line1 = line_sends(keep1, got1, side1)
            branches[1] = after(branches[1], *line1, gparts[0])
        *back, gpart, gsum = attn_backward(windows, branches[b], xs[b], kept_b[:4], qkv, proj)
        backs.append((*back, gsum))
        gparts.append(gpart)
    if fast:
        side2 = after(flip(side2, SIDE), gparts[1])
        line2 = line_sends(keep2, got2, side2)
        line1 = [after(r, gparts[1]) for r in flip_line(line1)]
        piece1 = own_piece(keep1, got1, side1, line1)
        branches[0] = after(branches[0], piece1, *line2, outs[1])
    *g_attn, small = attn_weights(
        fast, me, sums2, gb1, [(k[5], k[4], br, *back) for k, br, back in zip(kept, branches, backs)])
    gnorms = own_sums(gparts)
    gpatch = input_back(*gnorms, x, ln1[0], gmiddle)
    output = (middle + outs[0].astype(F32) + outs[1].astype(F32) + row(fc2_bias)).astype(BF)

    if fast:
        line2 = [after(r, small) for r in flip_line(line2)]
        piece2 = own_piece(keep2, got2, side2, line2)
        keep, send = g_attn
        got = flip(after(send, piece2), CORE)
        side = flip(side_send(keep, got), SIDE)
        fc = jnp.concatenate([piece1, piece2, small], axis=0)
        fc_quad = jnp.stack([fc] + [after(r, output, gpatch) for r in gather_line(fc)])
        side = after(side, fc_quad, output, gpatch)
        line = sum_line(line_sends(keep, got, side))
        piece = own_piece(keep, got, side, line)
        quad = jnp.stack([piece] + gather_line(piece))
        fc_pair = after(flip(fc_quad, SIDE), quad)
        g_fc1, g_fc2, small = finish_mlp(me, (fc_quad, fc_pair, after(flip(fc_quad, CORE), quad), after(flip(fc_pair, CORE), quad)))
        totals = small[0:6] + across(small[0:6])
        pair = after(flip(quad, SIDE), totals)
        shapes = shape_of(3, features, width), shape_of(width, features)
        half_done = finish(me, 0, (quad, flip(quad, CORE)), shapes)
        pair = after(pair, half_done[0])
        gw, gproj = finish(me, 1, (pair, flip(pair, CORE)), shapes, half_done)
    else:
        g_fc1, g_fc2, gw, gproj = [g.astype(F32) for g in lax.psum((*g_mlp, *g_attn), "dp")]
        gw, gproj = gw[:, :, :width], gproj[:width]
        small = lax.psum(small, "dp").astype(F32)
        totals = lax.psum(small[0:6], "mp")
    padded = width + extra
    gqv = jnp.stack([small[6, :width], small[6, padded : padded + width]])
    gb1 = small[7:12].reshape(-1)[: gb1.size]
    gt = small[12:].reshape(12, 2 * LANES)[:heads, :REL].T

    unrow = lambda a: a.reshape(WIN, windows, features).transpose(1, 0, 2)
    return (
        unrow(output),
        unrow(gpatch),
        totals[0],
        totals[1],
        gw.transpose(1, 0, 2),
        gqv,
        gt,
        gproj,
        totals[4],
        totals[2],
        totals[3],
        g_fc1,
        gb1,
        g_fc2,
        totals[5],
    )


def solution(mesh):
    placed = (
        P(("dp", "mp"), None, None),
        P(("dp", "mp"), None),
        P(),
        P(),
        P(None, None, "mp"),
        P(None, "mp"),
        P(None, "mp"),
        P("mp", None),
        P(),
        P(),
        P(),
        P(None, "mp"),
        P("mp"),
        P("mp", None),
        P(),
        P(("dp", "mp"), None, None),
    )
    return jax.shard_map(
        functools.partial(shards, mesh.shape["dp"], mesh.shape["mp"]),
        mesh=mesh,
        in_specs=placed,
        out_specs=(
            P(("dp", "mp"), None, None),
            P(("dp", "mp"), None, None),
            P(),
            P(),
            P(None, None, "mp"),
            P(None, "mp"),
            P(None, "mp"),
            P("mp", None),
            P(),
            P(),
            P(),
            P(None, "mp"),
            P("mp"),
            P("mp", None),
            P(),
        ),
        check_vma=False,
    )
```

```python
import functools

import jax
import jax.numpy as jnp
from jax import lax
from jax.experimental import pallas as pl
from jax.experimental.pallas import tpu as pltpu
from jax.sharding import PartitionSpec as P

HEAD = 32
WSIDE = 7
WIN = 49
REL = 169
SLOT = 64
GROUP = 4
LANES = 128
EPS = 1e-05
SCALING = HEAD ** (-0.5)
BF = jnp.bfloat16
F32 = jnp.float32
HIGH = lax.Precision.HIGHEST
VMEM_LIMIT = 28 * 1024 * 1024
ALL_VMEM = 58 * 1024 * 1024
BLOCK = 96
CORE, SIDE, LINE = 1, 2, 4

ROW_COL = (((1,), (0,)), ((), ()))
LAST_LAST = (((1,), (1,)), ((), ()))
ROWS_ROWS = (((0,), (0,)), ((), ()))


def mm(a, b, dims=ROW_COL):
    return lax.dot_general(a, b, dims, preferred_element_type=F32)


def norm_parts(rows):
    mean = jnp.mean(rows, axis=-1, keepdims=True)
    centred = rows - mean
    variance = jnp.mean(centred * centred, axis=-1, keepdims=True)
    inv = lax.rsqrt(variance + EPS)
    return centred * inv, inv


def norm_back(xhat, inv, gain, upstream):
    z = upstream * gain
    mean_z = jnp.mean(z, axis=-1, keepdims=True)
    mean_zx = jnp.mean(z * xhat, axis=-1, keepdims=True)
    return (z - mean_z - xhat * mean_zx) * inv


def head_masks():
    lane = lax.broadcasted_iota(jnp.int32, (SLOT, LANES), 1)
    return [jnp.where((lane >> 5) == h, 1.0, 0.0).astype(BF) for h in range(GROUP)]


def block_ones():
    row = lax.broadcasted_iota(jnp.int32, (GROUP * SLOT, GROUP * SLOT), 0)
    col = lax.broadcasted_iota(jnp.int32, (GROUP * SLOT, GROUP * SLOT), 1)
    return jnp.where((row >> 6) == (col >> 6), 1.0, 0.0).astype(BF)


def spread(tile, masks):
    return jnp.concatenate([tile * m for m in masks], axis=0)


def collect(full, masks_f):
    total = full[0:SLOT] * masks_f[0]
    for h in range(1, GROUP):
        total = total + full[h * SLOT : (h + 1) * SLOT] * masks_f[h]
    return total


def fill(scratch, rows, windows):
    pitch = windows + 1
    for g in range(scratch.shape[0]):
        for place in range(WIN):
            scratch[g, place * pitch : place * pitch + windows, :] = rows[
                place * windows : (place + 1) * windows, g * LANES : (g + 1) * LANES]
        scratch[g, WIN * pitch :, :] = jnp.zeros((scratch.shape[1] - WIN * pitch, LANES), rows.dtype)


def empty(scratch, windows):
    pitch = windows + 1
    planes = [
        jnp.concatenate([scratch[g, place * pitch : place * pitch + windows, :] for place in range(WIN)], axis=0)
        for g in range(scratch.shape[0])
    ]
    return jnp.concatenate(planes, axis=1).astype(BF)


def row_max(tile, low_half):
    low = jnp.max(jnp.where(low_half, tile, -3e38), axis=-1, keepdims=True)
    high = jnp.max(jnp.where(low_half, -3e38, tile), axis=-1, keepdims=True)
    return jnp.where(low_half, low, high)


def row_sum(tile, low_half):
    low = jnp.sum(jnp.where(low_half, tile, 0.0), axis=-1, keepdims=True)
    high = jnp.sum(jnp.where(low_half, 0.0, tile), axis=-1, keepdims=True)
    return jnp.where(low_half, low, high)


def ds(start, size):
    unit = 384 if size % 384 == 0 else 48
    return pl.ds(pl.multiple_of(start, unit), size)


def each_block(me, *by_core):
    for c_rel, target in enumerate(by_core):
        for y_rel in range(2):
            for z_rel in range(4):
                yield target, y_rel, z_rel, (me & 1) ^ c_rel, ((me >> 1) & 1) ^ y_rel, (me >> 2) ^ z_rel


def line(ref):
    return ref[...].reshape(1, -1)


def begin(sems, *pairs):
    copies = [pltpu.make_async_copy(a, b, sems.at[i]) for i, (a, b) in enumerate(pairs)]
    for copy in copies:
        copy.start()
    return copies


def finish_all(copies):
    for copy in copies:
        copy.wait()


def attn_forward_kernel(windows, x_in, gain_ref, shift_ref, w_in, bias_in, pos_ref, valid_ref,
                        prob_ref, q_ref, k_ref, v_ref, mixed_ref, normed_t_ref,
                        mask_s, q_s, k_s, v_s, mixed_s, x_ref, w_ref, bias_ref, in_sems):
    copies = begin(in_sems, (x_in, x_ref), *[(w_in.at[p], w_ref.at[p]) for p in range(3)], (bias_in, bias_ref))
    mask_s[...] = jnp.zeros(mask_s.shape, F32)
    for h in range(GROUP):
        mask_s[:, h * SLOT : h * SLOT + WIN] = valid_ref[...].astype(F32)
    masks = head_masks()
    ones = block_ones()
    low_half = lax.broadcasted_iota(jnp.int32, (SLOT, LANES), 1) < SLOT
    copies[0].wait()
    copies[4].wait()
    x = x_ref[...].astype(F32)
    rows = x.shape[0]
    groups = q_s.shape[0]
    xhat, _ = norm_parts(x)
    normed = (xhat * line(gain_ref) + line(shift_ref)).astype(BF)
    normed_t_ref[...] = normed.T
    for part, scratch in enumerate((q_s, k_s, v_s)):
        copies[1 + part].wait()
        got = mm(normed, w_ref[part])
        if part != 1:
            got = got + bias_ref[part // 2 : part // 2 + 1, :]
        fill(scratch, got.astype(BF).astype(F32), windows)

    def window(w, carry):
        allowed = jnp.broadcast_to(mask_s[pl.ds(w, 1), :], (SLOT, GROUP * SLOT)) > 0.5
        for g in range(groups):
            cols = slice(g * LANES, (g + 1) * LANES)
            places = pl.ds(w, SLOT, stride=windows + 1)
            q = q_s[g, places, :].astype(BF)
            k = k_s[g, places, :].astype(BF)
            v = v_s[g, places, :].astype(BF)
            q_ref[w, :, cols] = q
            k_ref[w, :, cols] = k
            v_ref[w, :, cols] = v
            scores = mm(q, spread(k, masks), LAST_LAST) * SCALING + pos_ref[g]
            scores = jnp.where(allowed, scores, -1000000000.0)
            top = jnp.concatenate([row_max(scores[:, :LANES], low_half), row_max(scores[:, LANES:], low_half)], axis=1)
            e = jnp.exp(scores - top)
            total = mm(e.astype(BF), ones)
            inv = pl.reciprocal(total, approx=True)
            prob = (e * (inv * (2.0 - total * inv))).astype(BF)
            prob_ref[w, g] = prob
            mixed_s[g, places, :] = mm(prob, spread(v, masks))
        return carry

    lax.fori_loop(0, windows, window, 0, unroll=2)
    mixed_ref[...] = empty(mixed_s, windows)


def middle_kernel(heads, me_ref, x_in, own_in, peer_in, bias_ref, gain_ref, shift_ref, *refs):
    if heads:
        half_in, rest_in, middle_ref, nm_ref, x_ref, own_ref, peer_ref, proj_ref, sems = refs
        lines = half_in.shape[0]
        core = me_ref[0] & 1
        place = lambda c: proj_ref.at[pl.ds(pl.multiple_of(c * lines, lines), lines), :]
        copies = begin(sems, (peer_in, peer_ref), (half_in, place(core)), (rest_in, place(1 - core)), (x_in, x_ref),
                       (own_in, own_ref))
        finish_all(copies[:3])
        peer = mm(peer_ref[...], proj_ref[...])
        finish_all(copies[3:])
    else:
        middle_ref, nm_ref, x_ref, own_ref, peer_ref, sems = refs
        finish_all(begin(sems, (x_in, x_ref), (own_in, own_ref), (peer_in, peer_ref)))
        peer = peer_ref[...].astype(F32)
    middle = x_ref[...].astype(F32) + (own_ref[...].astype(F32) + peer) + line(bias_ref)
    middle_ref[...] = middle
    xhat, _ = norm_parts(middle)
    nm_ref[...] = (xhat * line(gain_ref) + line(shift_ref)).astype(BF)


def mlp_kernel(nm_ref, cot_ref, fc1_ref, b1_ref, fc2_ref, hid_ref, gpre_ref, out_ref, gmid_ref):
    hidden_size = fc1_ref.shape[1]
    features = fc1_ref.shape[0]
    step = 256 if hidden_size % 256 == 0 else 128
    count = hidden_size // step

    nm = nm_ref[...]
    cot = cot_ref[...]

    def units(c, carry):
        cols = pl.ds(pl.multiple_of(c * step, step), step)
        pre = mm(nm, fc1_ref[:, cols]) + b1_ref[:, cols]
        phi = 0.5 * (1.0 + lax.erf(pre * (0.5 ** 0.5)))
        hid_ref[:, cols] = (pre * phi).astype(BF)
        slope = phi + pre * (jnp.exp(-0.5 * pre * pre) * 0.3989422804014327)
        gpre_ref[:, cols] = (mm(cot, fc2_ref[cols, :], LAST_LAST) * slope).astype(BF)
        return carry

    lax.fori_loop(0, count, units, 0)

    def tile(c, carry):
        cols = pl.ds(pl.multiple_of(c * 256, 256), 256)
        gmid_ref[:, cols] = mm(gpre_ref[...], fc1_ref[cols, :], LAST_LAST).astype(BF)
        out_ref[:, cols] = mm(hid_ref[...], fc2_ref[:, cols]).astype(BF)
        return carry

    lax.fori_loop(0, features // 256, tile, 0)

def mlp_weights_kernel(count, split, me_ref, *refs):
    inputs, refs = refs[: 4 * count], refs[4 * count :]
    n_out = 5 if split else 3
    gb1_ref, *outs = refs[:n_out]
    held = refs[n_out : n_out + 4 * count]
    nts = refs[n_out + 4 * count : n_out + 5 * count]
    g1_ref, g2_ref, in_sems, unit_sems, out_sems = refs[n_out + 5 * count :]
    blocks = [held[4 * b : 4 * b + 4] for b in range(count)]
    hidden_size = g1_ref.shape[1]
    features = g1_ref.shape[0]
    step = 384 if hidden_size % 384 == 0 else 128
    wide = features if hidden_size % features == 0 else step

    def units_in(j):
        cols = ds(j * step, step)
        return [pltpu.make_async_copy(inputs[4 * b + 2].at[:, cols], held[4 * b + 2].at[:, cols], unit_sems.at[b, j])
                for b in range(count)]

    order = [4 * b + k for k in (0, 1) for b in range(count)]
    copies = dict(zip(order, begin(in_sems, *[(inputs[i], held[i]) for i in order])))
    for j in range(hidden_size // step):
        for copy in units_in(j):
            copy.start()
    last = [pltpu.make_async_copy(inputs[4 * b + 3], held[4 * b + 3], in_sems.at[2 * count + b]) for b in range(count)]
    for copy in last:
        copy.start()
    finish_all([copies[4 * b] for b in range(count)])
    for block, nt in zip(blocks, nts):
        nt[...] = block[0][...].T
    finish_all([copies[4 * b + 1] for b in range(count)])

    def second(j, carry):
        finish_all(units_in(j))
        cols = ds(j * step, step)
        g2_ref[cols, :] = sum(mm(hid_ref[:, cols], cot_ref[...], ROWS_ROWS) for _, cot_ref, hid_ref, _ in blocks).astype(BF)
        return carry

    def first(j, carry):
        cols = ds(j * wide, wide)
        g1_ref[:, cols] = sum(mm(nt[...], block[3][:, cols]) for nt, block in zip(nts, blocks)).astype(BF)
        return carry

    lax.fori_loop(0, hidden_size // step, second, 0)
    me = me_ref[0]
    sent = []

    def send(k, source, target):
        sent.append(pltpu.make_async_copy(source, target, out_sems.at[k]))
        sent[-1].start()

    if split:
        for i, (target, y_rel, z_rel, c, y, z) in enumerate(each_block(me, outs[2], outs[3])):
            send(i, g2_ref.at[ds(c * 768 + y * 384 + z * 96, 96), :], target.at[y_rel, z_rel])
    else:
        send(0, g2_ref, outs[1])
    finish_all(last)
    gb1_ref[...] = sum(jnp.sum(block[3][...].astype(F32), axis=0, keepdims=True) for block in blocks)
    lax.fori_loop(0, hidden_size // wide, first, 0)
    if split:
        for i, (target, y_rel, z_rel, c, y, z) in enumerate(each_block(me, outs[0], outs[1])):
            send(16 + i, g1_ref.at[ds(y * 384 + z * 96, 96), ds(c * 768, 768)], target.at[y_rel, z_rel])
    else:
        send(1, g1_ref, outs[0])
    finish_all(sent)


def middle_back_kernel(own_ref, peer_ref, middle_ref, cot_ref, gain_ref, gmiddle_ref, branch_ref, sums_ref):
    upstream = cot_ref[...].astype(F32)
    xhat, inv = norm_parts(middle_ref[...])
    gmid = own_ref[...].astype(F32) + peer_ref[...].astype(F32)
    sums_ref[0:1, :] = jnp.sum(gmid * xhat, axis=0, keepdims=True)
    sums_ref[1:2, :] = jnp.sum(gmid, axis=0, keepdims=True)
    gmiddle = upstream + norm_back(xhat, inv, line(gain_ref), gmid)
    gmiddle_ref[...] = gmiddle
    branch_ref[...] = gmiddle.astype(BF)
    sums_ref[2:3, :] = jnp.sum(gmiddle, axis=0, keepdims=True)
    sums_ref[3:4, :] = jnp.sum(upstream, axis=0, keepdims=True)


def attn_backward_kernel(windows, branch_ref, x_ref, prob_ref, q_ref, k_ref, v_ref, w_ref, proj_ref,
                         grads_ref, gqv_ref, gpos_ref, part_ref, sums_ref, gm_s, gq_s, gk_s, gv_s):
    rows = branch_ref.shape[0]
    groups = gm_s.shape[0]
    gpos_ref[...] = jnp.zeros(gpos_ref.shape, F32)
    masks = head_masks()
    masks_f = [m.astype(F32) for m in masks]
    low_half = lax.broadcasted_iota(jnp.int32, (SLOT, LANES), 1) < SLOT
    fill(gm_s, mm(branch_ref[...], proj_ref[...], LAST_LAST).astype(BF).astype(F32), windows)

    def window(w, carry):
        for g in range(groups):
            cols = slice(g * LANES, (g + 1) * LANES)
            places = pl.ds(w, SLOT, stride=windows + 1)
            gm = gm_s[g, places, :].astype(BF)
            q = q_ref[w, :, cols]
            k = k_ref[w, :, cols]
            v = v_ref[w, :, cols]
            prob = prob_ref[w, g]
            prob_f = prob.astype(F32)
            gprob = mm(gm, spread(v, masks), LAST_LAST)
            both = prob_f * gprob
            delta = jnp.concatenate([row_sum(both[:, :LANES], low_half), row_sum(both[:, LANES:], low_half)], axis=1)
            gs = (both - prob_f * delta).astype(BF)
            gpos_ref[g] += gs.astype(F32)
            gq_s[g, places, :] = mm(gs, spread(k, masks)) * SCALING
            gk_s[g, places, :] = collect(mm(gs, q, ROWS_ROWS), masks_f) * SCALING
            gv_s[g, places, :] = collect(mm(prob, gm, ROWS_ROWS), masks_f)
        return carry

    lax.fori_loop(0, windows, window, 0, unroll=2)
    back = None
    for part, scratch in enumerate((gq_s, gk_s, gv_s)):
        grad = empty(scratch, windows)
        grads_ref[part] = grad
        if part != 1:
            width = grad.shape[1]
            lanes = slice(part // 2 * width, (part // 2 + 1) * width)
            gqv_ref[:, lanes] = jnp.sum(grad.astype(F32), axis=0, keepdims=True)
        term = mm(grad, w_ref[part], LAST_LAST)
        back = term if back is None else back + term
    part_ref[...] = back.astype(BF)
    xhat, _ = norm_parts(x_ref[...].astype(F32))
    sums_ref[0:1, :] = jnp.sum(back * xhat, axis=0, keepdims=True)
    sums_ref[1:2, :] = jnp.sum(back, axis=0, keepdims=True)


def place_offset(i):
    return i // WSIDE * (2 * WSIDE - 1) + i % WSIDE


def offset_picks():
    row = lax.broadcasted_iota(jnp.int32, (2 * LANES, 2 * SLOT), 0)
    col = lax.broadcasted_iota(jnp.int32, (2 * LANES, 2 * SLOT), 1)
    j = col & (SLOT - 1)
    line = (j * 37) >> 8
    offset = place_offset(WIN - 1) - line * (2 * WSIDE - 1) - (j - line * WSIDE)
    hit = ((row & (LANES - 1)) == offset) & ((row >> 7) == (col >> 6)) & (j < WIN)
    return jnp.where(hit, 1.0, 0.0).astype(BF)


def position_kernel(table_ref, pos_ref, table_s, rows_s):
    heads = table_ref.shape[0]
    table_s[...] = jnp.zeros(table_s.shape, F32)
    table_s[0:heads, 0:REL] = table_ref[...]
    table = table_s[...]
    lines = table.shape[0]
    rows_s[WIN * lines :, :] = jnp.zeros((rows_s.shape[0] - WIN * lines, LANES), F32)
    for i in range(WIN):
        turned = pltpu.roll(table, (2 * LANES - place_offset(i)) % (2 * LANES), 1)
        rows_s[i * lines : (i + 1) * lines, :] = turned[:, :LANES]
    picks = offset_picks()
    for pair in range(pos_ref.shape[0] * 2):
        pieces = [rows_s[pl.ds(2 * pair + k, SLOT, stride=lines), :] for k in range(2)]
        rest = jnp.concatenate(pieces, axis=1)
        total = jnp.zeros((SLOT, 2 * SLOT), F32)
        for _ in range(3):
            top = rest.astype(BF)
            total = total + mm(top, picks)
            rest = rest - top.astype(F32)
        pos_ref[pair // 2, :, pair % 2 * LANES : (pair % 2 + 1) * LANES] = total


def attn_weights_kernel(count, split, me_ref, sums2_ref, gb1_ref, *refs):
    blocks, refs = [refs[7 * b : 7 * b + 7] for b in range(count)], refs[7 * count :]
    *outs, small_ref = refs[:3]
    gw_ref, gproj_ref, rows_s, out_sems = refs[3:]
    gproj, gqv, gpos, sums = 0.0, 0.0, 0.0, 0.0
    for _, mixed_ref, branch_ref, _, gqv_ref, gpos_ref, sums_ref in blocks:
        gproj = gproj + mm(mixed_ref[...], branch_ref[...], ROWS_ROWS)
        gqv, gpos, sums = gqv + gqv_ref[...], gpos + gpos_ref[...], sums + sums_ref[...]
    width, features = gproj.shape
    gproj_ref[...] = gproj.astype(BF)
    hidden = gb1_ref.shape[1]
    lines = [sums[k : k + 1] for k in range(2)] + [sums2_ref[k : k + 1, :] for k in range(4)]
    lines.append(gqv)
    lines += [gb1_ref[:, k : min(k + features, hidden)] for k in range(0, hidden, features)]
    small = jnp.concatenate(
        [jnp.concatenate([line, jnp.zeros((1, features - line.shape[1]), F32)], axis=1) if line.shape[1] < features else line
         for line in lines] + [jnp.zeros((12 - len(lines), features), F32)], axis=0)
    picks = offset_picks()
    for pair in range(gpos.shape[0] * 2):
        rest = gpos[pair // 2][:, pair % 2 * LANES : (pair % 2 + 1) * LANES]
        total = jnp.zeros((SLOT, 2 * LANES), F32)
        for _ in range(2):
            top = rest.astype(BF)
            total = total + mm(top, picks, LAST_LAST)
            rest = rest - top.astype(F32)
        for k in range(2):
            rows_s[pl.ds(2 * pair + k, SLOT, stride=16), :] = total[:, k * LANES : (k + 1) * LANES]
    for h in range(gpos.shape[0] * 4, 16):
        rows_s[pl.ds(h, SLOT, stride=16), :] = jnp.zeros((SLOT, LANES), F32)
    table = jnp.zeros((16, 2 * LANES), F32)
    for i in range(WIN):
        row = jnp.concatenate([rows_s[i * 16 : (i + 1) * 16, :], jnp.zeros((16, LANES), F32)], axis=1)
        table = table + (pltpu.roll(row, place_offset(i), 1) if i else row)
    packed = [jnp.concatenate([table[3 * r + k : 3 * r + k + 1] for k in range(3)], axis=1) for r in range(4)]
    small_ref[...] = jnp.concatenate([small] + packed, axis=0).astype(BF)
    sent = []

    def send(k, source, target):
        sent.append(pltpu.make_async_copy(source, target, out_sems.at[k]))
        sent[-1].start()

    if split:
        for i, (target, y_rel, z_rel, c, y, z) in enumerate(each_block(me_ref[0], *outs)):
            send(i, gproj_ref.at[ds((c * 4 + y * 2 + (z >> 1)) * 48, 48), ds((z & 1) * 384, 384)],
                 target.at[y_rel, z_rel, 48:96, 384:768])
    else:
        send(0, gproj_ref, outs[1])
    for part in range(3):
        gw = 0.0
        for normed_t_ref, _, _, grads_ref, _, _, _ in blocks:
            gw = gw + mm(normed_t_ref[...], grads_ref[part])
        gw_ref[part] = gw.astype(BF)
        if split:
            for i, (target, y_rel, z_rel, c, y, z) in enumerate(each_block(me_ref[0], *outs)):
                send(16 * (part + 1) + i, gw_ref.at[part, ds(c * 384 + y * 192 + z * 48, 48), :],
                     target.at[y_rel, z_rel, part // 2 * 48 : part // 2 * 48 + 48, part % 2 * 384 : part % 2 * 384 + 384])
        else:
            send(1 + part, gw_ref.at[part], outs[0].at[part])
    finish_all(sent)


def input_back_kernel(own_ref, peer_ref, x_ref, gain_ref, gmiddle_ref, gpatch_ref):
    gnorm = own_ref[...].astype(F32) + peer_ref[...].astype(F32)
    xhat, inv = norm_parts(x_ref[...].astype(F32))
    gpatch_ref[...] = (gmiddle_ref[...] + norm_back(xhat, inv, line(gain_ref), gnorm)).astype(BF)


def finish_kernel(y_rels, me_ref, *refs):
    sources, refs = refs[:2], refs[2:]
    if y_rels[0] == 1:
        refs = refs[2:]
    outs, held, wide, (in_sems, out_sems) = refs[:2], refs[2:4], refs[4:6], refs[6:]
    copies = begin(in_sems, *zip(sources, held))
    sent = []

    def put(value, k, where):
        wide[k][where] = value.astype(F32)
        sent.append(pltpu.make_async_copy(wide[k].at[where], outs[k].at[where], out_sems.at[len(sent)]))
        sent[-1].start()

    for source, y_rel, z_rel, c, y, z in each_block(me_ref[0], 0, 1):
        if y_rel not in y_rels:
            continue
        if z_rel == 0:
            copies[source].wait()
        piece = held[source].at[z_rel]
        lines = ds(c * 384 + y * 192 + z * 48, 48)
        put(piece[0:48, 0:384], 0, (0, lines, slice(None)))
        put(piece[0:48, 384:768], 0, (1, lines, slice(None)))
        put(piece[48:96, 0:384], 0, (2, lines, slice(None)))
        put(piece[48:96, 384:768], 1, (ds((c * 4 + y * 2 + (z >> 1)) * 48, 48), ds((z & 1) * 384, 384)))
    finish_all(sent)


def finish_mlp_kernel(me_ref, *refs):
    sources, (g1_out, g2_out, small_ref), held, (g1_ref, g2_ref, small_s, in_sems, out_sems) = (
        refs[:4], refs[4:7], refs[7:11], refs[11:])
    copies = begin(in_sems, *zip(sources, held))
    sent = []

    def put(value, k, wide, out, where):
        wide[where] = value.astype(F32)
        sent.append(pltpu.make_async_copy(wide.at[where], out.at[where], out_sems.at[k, len(sent) // 2]))
        sent[-1].start()

    for source, y_rel, z_rel, c, y, z in each_block(me_ref[0], (0, 1), (2, 3)):
        source = source[y_rel]
        if z_rel == 0:
            copies[source].wait()
        piece = held[source].at[z_rel]
        put(piece[0:BLOCK, :], 0, g1_ref, g1_out, (ds(y * 384 + z * 96, 96), ds(c * 768, 768)))
        put(piece[BLOCK : 2 * BLOCK, :], 1, g2_ref, g2_out, (ds(c * 768 + y * 384 + z * 96, 96), slice(None)))
        small_s[z * 4 + y * 2 + c] = piece[2 * BLOCK :, :].astype(F32)
    total = small_s[0]
    for d in range(1, 16):
        total = total + small_s[d]
    small_ref[...] = total
    finish_all(sent)


def shape_of(*dims, dtype=F32):
    return jax.ShapeDtypeStruct(dims, dtype)


def call(kernel, outs, scratch, name, flops, smem, *args, far=(), far_outs=(), limit=VMEM_LIMIT, aliases=None):
    space = lambda is_far: pl.BlockSpec(memory_space=pltpu.HBM if is_far else pltpu.VMEM)
    in_specs = [pl.BlockSpec(memory_space=pltpu.SMEM)] * len(smem) + [space(i in far) for i in range(len(args))]
    return pl.pallas_call(
        kernel,
        out_shape=outs,
        in_specs=in_specs,
        out_specs=[space(i in far_outs) for i in range(len(outs))],
        scratch_shapes=scratch,
        compiler_params=pltpu.CompilerParams(vmem_limit_bytes=limit),
        cost_estimate=pl.CostEstimate(flops=flops, bytes_accessed=flops // 256, transcendentals=0),
        input_output_aliases=aliases or {},
        name=name,
    )(*smem, *args)


def like(*arrays):
    return [pltpu.VMEM(a.shape, a.dtype) for a in arrays]


def dma(*counts):
    return [pltpu.SemaphoreType.DMA(c if isinstance(c, tuple) else (c,)) for c in counts]


SMALL = 1000000


def position(table):
    heads = table.shape[0]
    groups = -(-heads // GROUP)
    return call(position_kernel, [shape_of(groups, SLOT, GROUP * SLOT)],
                [pltpu.VMEM((16, 2 * LANES), F32), pltpu.VMEM((16 * SLOT, LANES), F32)], "position", SMALL, (), table)[0]


def attn_forward(windows, x, ln1, qkv, qv_bias, pos, mask):
    rows, features = x.shape
    width = qkv.shape[2]
    groups = width // LANES
    tile = shape_of(windows, SLOT, width, dtype=BF)
    outs = [shape_of(windows, groups, SLOT, GROUP * SLOT, dtype=BF), tile, tile, tile, shape_of(rows, width, dtype=BF),
            shape_of(features, rows, dtype=BF)]
    scratch = [pltpu.VMEM((windows, GROUP * SLOT), F32)] + [pltpu.VMEM((groups, SLOT * (windows + 1), LANES), F32)] * 4
    scratch += like(x, qkv, qv_bias) + dma(5)
    return call(functools.partial(attn_forward_kernel, windows), outs, scratch, "attn_forward", SMALL, (),
                x, *ln1, qkv, qv_bias, pos, mask, far=(0, 3, 4), limit=ALL_VMEM)


def middle_norm(me, x, own, peer, bias, ln2, halves):
    rows, features = x.shape
    scratch = like(x, own, peer)
    if halves:
        scratch += [pltpu.VMEM((2 * halves[0].shape[0], features), BF)]
    return call(functools.partial(middle_kernel, bool(halves)), [shape_of(rows, features), shape_of(rows, features, dtype=BF)],
                scratch + dma(5), "middle", SMALL, (me,), x, own, peer, bias, *ln2, *halves, far=(0, 1, 2, 6, 7),
                limit=ALL_VMEM)


def mlp(nm, cot, fc1, fc1_bias, fc2):
    rows, features = nm.shape
    hidden = fc2.shape[0]
    outs = [shape_of(rows, hidden, dtype=BF)] * 2 + [shape_of(rows, features, dtype=BF)] * 2
    return call(mlp_kernel, outs, [], "mlp", SMALL, (), nm, cot, fc1, fc1_bias, fc2)


def mlp_weights(split, me, blocks):
    rows, features = blocks[0][0].shape
    hidden = blocks[0][2].shape[1]
    grads = [shape_of(features, hidden, dtype=BF), shape_of(hidden, features, dtype=BF)]
    outs = [shape_of(1, hidden)] + ([shape_of(2, 4, BLOCK, features, dtype=BF)] * 4 if split else grads)
    flat = [a for b in blocks for a in b]
    scratch = like(*flat) + [pltpu.VMEM((features, rows), BF)] * len(blocks) + like(*grads) + dma(3 * len(blocks), (len(blocks), hidden // 128), 32)
    return call(functools.partial(mlp_weights_kernel, len(blocks), split), outs, scratch, "mlp_weights", SMALL,
                (me,), *flat, far=range(len(flat)), far_outs=range(1, len(outs)), limit=ALL_VMEM)


def middle_back(own, peer, middle, cot, gain):
    rows, features = middle.shape
    return call(
        middle_back_kernel, [shape_of(rows, features), shape_of(rows, features, dtype=BF), shape_of(4, features)], [],
        "middle_back", 20000 * SMALL, (), own, peer, middle, cot, gain)


def attn_backward(windows, branch, x, kept, qkv, proj):
    rows, features = branch.shape
    width = proj.shape[0]
    groups = width // LANES
    outs = [shape_of(3, rows, width, dtype=BF), shape_of(1, 2 * width), shape_of(groups, SLOT, GROUP * SLOT),
            shape_of(rows, features, dtype=BF), shape_of(2, features)]
    scratch = [pltpu.VMEM((groups, SLOT * (windows + 1), LANES), F32)] * 4
    return call(functools.partial(attn_backward_kernel, windows), outs, scratch, "attn_backward", SMALL, (),
                branch, x, *kept, qkv, proj)


def attn_weights(split, me, sums2, gb1, blocks):
    features = blocks[0][0].shape[0]
    width = blocks[0][1].shape[1]
    grads = [shape_of(3, features, width, dtype=BF), shape_of(width, features, dtype=BF)]
    outs = ([shape_of(2, 4, BLOCK, features, dtype=BF)] * 2 if split else grads) + [shape_of(16, features, dtype=BF)]
    scratch = like(*grads) + [pltpu.VMEM((16 * SLOT, LANES), F32)]
    flat = [a for b in blocks for a in b]
    return call(functools.partial(attn_weights_kernel, len(blocks), split), outs, scratch + dma(64),
                "attn_weights", SMALL, (me,), sums2, gb1, *flat, far_outs=(0, 1))


def input_back(own, peer, x, gain, gmiddle):
    rows, features = x.shape
    return call(input_back_kernel, [shape_of(rows, features, dtype=BF)], [], "input_back", SMALL, (),
                own, peer, x, gain, gmiddle)[0]


def finish(me, y_rel, sources, outs, before=()):
    scratch = like(*sources, *outs) + dma(2, 8 * 4)
    return call(functools.partial(finish_kernel, (y_rel,)), list(outs), scratch, "finish", SMALL, (me,), *sources, *before,
                far=range(2 + len(before)), far_outs=range(len(outs)), aliases={3: 0, 4: 1} if before else {})


def finish_mlp(me, sources):
    features = sources[0].shape[2]
    outs = [shape_of(features, 2 * features), shape_of(2 * features, features), shape_of(16, features)]
    scratch = like(*sources, *outs[:2]) + [pltpu.VMEM((16, 16, features), F32)] + dma(4, (2, 16))
    return call(finish_mlp_kernel, outs, scratch, "finish_mlp", SMALL, (me,), *sources, far=range(4), far_outs=(0, 1))


def across(v):
    return lax.ppermute(v, "mp", [(0, 1), (1, 0)])


def flip(v, bits):
    return lax.ppermute(v, "dp", [(i, i ^ bits) for i in range(16)])


def after(v, *others):
    return lax.optimization_barrier((v, *others))[0]


def total_of(terms):
    total = terms[0].astype(F32)
    for t in terms[1:]:
        total = total + t.astype(F32)
    return total.astype(BF)


def side_send(keep, got):
    return total_of([keep[1], got[1]])


def line_sends(keep, got, side):
    return [total_of([keep[0, k], got[0, k], side[k]]) for k in (1, 2, 3)]


def own_piece(keep, got, side, line):
    return total_of([keep[0, 0], got[0, 0], side[0], *line])


def flip_line(pieces):
    return [flip(p, LINE * k) for k, p in zip((1, 2, 3), pieces)]


def sum_line(sends):
    near, far, both = sends
    return [flip(near, LINE), flip(total_of([far, flip(both, LINE)]), 2 * LINE)]


def gather_line(piece):
    far = flip(piece, 2 * LINE)
    return [flip(piece, LINE), far, flip(far, LINE)]


def shards(
    dp_size,
    mp_size,
    patches,
    token_valid,
    ln1_gain,
    ln1_shift,
    qkv_weight,
    qv_bias,
    bias_table,
    proj_weight,
    proj_bias,
    ln2_gain,
    ln2_shift,
    fc1_weight,
    fc1_bias,
    fc2_weight,
    fc2_bias,
    cotangent,
):
    windows, _, features = patches.shape
    rows = windows * WIN
    width = proj_weight.shape[0]
    heads = width // HEAD
    fast = mp_size == 2 and dp_size == 16 and features == 768
    x = patches.transpose(1, 0, 2).reshape(rows, features)
    cot = cotangent.transpose(1, 0, 2).reshape(rows, features)
    row = lambda a: a.reshape(1, -1)
    extra = -width % LANES
    qkv = jnp.pad(qkv_weight.transpose(1, 0, 2), ((0, 0), (0, 0), (0, extra)))
    proj = jnp.pad(proj_weight, ((0, extra), (0, 0)))
    pos = position(bias_table.T)
    bias = jnp.pad(qv_bias, ((0, 0), (0, extra)))
    valid = token_valid.astype(F32)
    ln1, ln2 = (ln1_gain, ln1_shift), (ln2_gain, ln2_shift)

    def blocks_of(v):
        return [v, across(v)] if fast else list(lax.all_gather(v, "mp"))

    def own_sums(parts):
        if fast:
            return parts[0], across(parts[1])
        own = lax.psum_scatter(jnp.concatenate(parts), "mp", scatter_dimension=0, tiled=True)
        return own, jnp.zeros_like(own)

    index = lax.axis_index("dp").astype(jnp.int32)
    me = index.reshape(1)
    valids = blocks_of(valid)
    kept, xs = [], []
    for x_b, valid_b in zip(blocks_of(x), valids):
        if kept:
            x_b = after(x_b, kept[0][4])
        xs.append(x_b)
        kept.append(attn_forward(windows, x_b, ln1, qkv, bias, pos, valid_b))
    project = lambda mixed, weight: jnp.dot(mixed, weight, preferred_element_type=F32).astype(BF)
    if fast:
        core = index & 1
        half = across(lax.dynamic_slice_in_dim(after(proj, valids[1], pos), core * (width // 2), width // 2, 0))
        cots = [cot, across(after(cot, valids[1], pos))]
        mixed = across(after(kept[1][4], cots[1], half))
        half = after(half, kept[1][4])
        rest = flip(half, CORE)
        parts, halves = (project(kept[0][4], proj), mixed), (half, rest)
    else:
        parts, halves = own_sums([project(k[4], proj) for k in kept]), ()
        cots = blocks_of(cot)
    middle, nm = middle_norm(me, x, *parts, proj_bias, ln2, halves)

    blocks, outs, gmids = [], [], []
    for nm_b, cot_b in zip(blocks_of(nm), cots):
        if blocks:
            nm_b = after(nm_b, gmids[-1])
        hid, gpre, out_b, gmid_b = mlp(nm_b, cot_b, fc1_weight, row(fc1_bias), fc2_weight)
        blocks.append((nm_b, cot_b, hid, gpre))
        outs.append(out_b)
        gmids.append(gmid_b)
    gmid_own, gmid_peer = own_sums(gmids)
    gb1, *g_mlp = mlp_weights(fast, me, blocks)
    outs = own_sums(outs)
    gmid_peer = after(gmid_peer, gb1)
    gmiddle, branch, sums2 = middle_back(gmid_own, gmid_peer, middle, cot, ln2[0])
    branches = blocks_of(branch)
    if fast:
        keep1, send1, keep2, send2 = g_mlp
        got1, got2 = after(flip(send1, CORE), branch), after(flip(send2, CORE), branch)
        side1, side2 = side_send(keep1, got1), side_send(keep2, got2)
        branches[0] = after(branches[0], side1, side2)
    backs, gparts = [], []
    for b, kept_b in enumerate(kept):
        if b == 1 and fast:
            side1 = after(flip(side1, SIDE), gparts[0])
            line1 = line_sends(keep1, got1, side1)
            branches[1] = after(branches[1], *line1, gparts[0])
        *back, gpart, gsum = attn_backward(windows, branches[b], xs[b], kept_b[:4], qkv, proj)
        backs.append((*back, gsum))
        gparts.append(gpart)
    if fast:
        side2 = after(flip(side2, SIDE), gparts[1])
        line2 = line_sends(keep2, got2, side2)
        line1 = [after(r, gparts[1]) for r in flip_line(line1)]
        piece1 = own_piece(keep1, got1, side1, line1)
        branches[0] = after(branches[0], piece1, *line2, outs[1])
    *g_attn, small = attn_weights(
        fast, me, sums2, gb1, [(k[5], k[4], br, *back) for k, br, back in zip(kept, branches, backs)])
    gnorms = own_sums(gparts)
    gpatch = input_back(*gnorms, x, ln1[0], gmiddle)
    output = (middle + outs[0].astype(F32) + outs[1].astype(F32) + row(fc2_bias)).astype(BF)

    if fast:
        line2 = [after(r, small) for r in flip_line(line2)]
        piece2 = own_piece(keep2, got2, side2, line2)
        keep, send = g_attn
        got = flip(after(send, piece2), CORE)
        side = flip(side_send(keep, got), SIDE)
        fc = jnp.concatenate([piece1, piece2, small], axis=0)
        fc_quad = jnp.stack([fc] + [after(r, output, gpatch) for r in gather_line(fc)])
        side = after(side, fc_quad, output, gpatch)
        line = sum_line(line_sends(keep, got, side))
        piece = own_piece(keep, got, side, line)
        quad = jnp.stack([piece] + gather_line(piece))
        fc_pair = after(flip(fc_quad, SIDE), quad)
        g_fc1, g_fc2, small = finish_mlp(me, (fc_quad, fc_pair, after(flip(fc_quad, CORE), quad), after(flip(fc_pair, CORE), quad)))
        totals = small[0:6] + across(small[0:6])
        pair = after(flip(quad, SIDE), totals)
        shapes = shape_of(3, features, width), shape_of(width, features)
        half_done = finish(me, 0, (quad, flip(quad, CORE)), shapes)
        pair = after(pair, half_done[0])
        gw, gproj = finish(me, 1, (pair, flip(pair, CORE)), shapes, half_done)
    else:
        g_fc1, g_fc2, gw, gproj = [g.astype(F32) for g in lax.psum((*g_mlp, *g_attn), "dp")]
        gw, gproj = gw[:, :, :width], gproj[:width]
        small = lax.psum(small, "dp").astype(F32)
        totals = lax.psum(small[0:6], "mp")
    padded = width + extra
    gqv = jnp.stack([small[6, :width], small[6, padded : padded + width]])
    gb1 = small[7:12].reshape(-1)[: gb1.size]
    gt = small[12:].reshape(12, 2 * LANES)[:heads, :REL].T

    unrow = lambda a: a.reshape(WIN, windows, features).transpose(1, 0, 2)
    return (
        unrow(output),
        unrow(gpatch),
        totals[0],
        totals[1],
        gw.transpose(1, 0, 2),
        gqv,
        gt,
        gproj,
        totals[4],
        totals[2],
        totals[3],
        g_fc1,
        gb1,
        g_fc2,
        totals[5],
    )


def solution(mesh):
    placed = (
        P(("dp", "mp"), None, None),
        P(("dp", "mp"), None),
        P(),
        P(),
        P(None, None, "mp"),
        P(None, "mp"),
        P(None, "mp"),
        P("mp", None),
        P(),
        P(),
        P(),
        P(None, "mp"),
        P("mp"),
        P("mp", None),
        P(),
        P(("dp", "mp"), None, None),
    )
    return jax.shard_map(
        functools.partial(shards, mesh.shape["dp"], mesh.shape["mp"]),
        mesh=mesh,
        in_specs=placed,
        out_specs=(
            P(("dp", "mp"), None, None),
            P(("dp", "mp"), None, None),
            P(),
            P(),
            P(None, None, "mp"),
            P(None, "mp"),
            P(None, "mp"),
            P("mp", None),
            P(),
            P(),
            P(),
            P(None, "mp"),
            P("mp"),
            P("mp", None),
            P(),
        ),
        check_vma=False,
    )
```

```python
import functools

import jax
import jax.numpy as jnp
from jax import lax
from jax.experimental import pallas as pl
from jax.experimental.pallas import tpu as pltpu
from jax.sharding import PartitionSpec as P

HEAD = 32
WSIDE = 7
WIN = 49
REL = 169
SLOT = 64
GROUP = 4
LANES = 128
EPS = 1e-05
SCALING = HEAD ** (-0.5)
BF = jnp.bfloat16
F32 = jnp.float32
HIGH = lax.Precision.HIGHEST
VMEM_LIMIT = 28 * 1024 * 1024
ALL_VMEM = 58 * 1024 * 1024
BLOCK = 96
CORE, SIDE, LINE = 1, 2, 4

ROW_COL = (((1,), (0,)), ((), ()))
LAST_LAST = (((1,), (1,)), ((), ()))
ROWS_ROWS = (((0,), (0,)), ((), ()))


def mm(a, b, dims=ROW_COL):
    return lax.dot_general(a, b, dims, preferred_element_type=F32)


def norm_parts(rows):
    mean = jnp.mean(rows, axis=-1, keepdims=True)
    centred = rows - mean
    variance = jnp.mean(centred * centred, axis=-1, keepdims=True)
    inv = lax.rsqrt(variance + EPS)
    return centred * inv, inv


def norm_back(xhat, inv, gain, upstream):
    z = upstream * gain
    mean_z = jnp.mean(z, axis=-1, keepdims=True)
    mean_zx = jnp.mean(z * xhat, axis=-1, keepdims=True)
    return (z - mean_z - xhat * mean_zx) * inv


def head_masks():
    lane = lax.broadcasted_iota(jnp.int32, (SLOT, LANES), 1)
    return [jnp.where((lane >> 5) == h, 1.0, 0.0).astype(BF) for h in range(GROUP)]


def block_ones():
    row = lax.broadcasted_iota(jnp.int32, (GROUP * SLOT, GROUP * SLOT), 0)
    col = lax.broadcasted_iota(jnp.int32, (GROUP * SLOT, GROUP * SLOT), 1)
    return jnp.where((row >> 6) == (col >> 6), 1.0, 0.0).astype(BF)


def spread(tile, masks):
    return jnp.concatenate([tile * m for m in masks], axis=0)


def collect(full, masks_f):
    total = full[0:SLOT] * masks_f[0]
    for h in range(1, GROUP):
        total = total + full[h * SLOT : (h + 1) * SLOT] * masks_f[h]
    return total


def fill(scratch, rows, windows):
    pitch = windows + 1
    for g in range(scratch.shape[0]):
        for place in range(WIN):
            scratch[g, place * pitch : place * pitch + windows, :] = rows[
                place * windows : (place + 1) * windows, g * LANES : (g + 1) * LANES]
        scratch[g, WIN * pitch :, :] = jnp.zeros((scratch.shape[1] - WIN * pitch, LANES), rows.dtype)


def empty(scratch, windows):
    pitch = windows + 1
    planes = [
        jnp.concatenate([scratch[g, place * pitch : place * pitch + windows, :] for place in range(WIN)], axis=0)
        for g in range(scratch.shape[0])
    ]
    return jnp.concatenate(planes, axis=1).astype(BF)


def row_max(tile, low_half):
    low = jnp.max(jnp.where(low_half, tile, -3e38), axis=-1, keepdims=True)
    high = jnp.max(jnp.where(low_half, -3e38, tile), axis=-1, keepdims=True)
    return jnp.where(low_half, low, high)


def row_sum(tile, low_half):
    low = jnp.sum(jnp.where(low_half, tile, 0.0), axis=-1, keepdims=True)
    high = jnp.sum(jnp.where(low_half, 0.0, tile), axis=-1, keepdims=True)
    return jnp.where(low_half, low, high)


def ds(start, size):
    unit = 384 if size % 384 == 0 else 48
    return pl.ds(pl.multiple_of(start, unit), size)


def each_block(me, *by_core):
    for c_rel, target in enumerate(by_core):
        for y_rel in range(2):
            for z_rel in range(4):
                yield target, y_rel, z_rel, (me & 1) ^ c_rel, ((me >> 1) & 1) ^ y_rel, (me >> 2) ^ z_rel


def line(ref):
    return ref[...].reshape(1, -1)


def begin(sems, *pairs):
    copies = [pltpu.make_async_copy(a, b, sems.at[i]) for i, (a, b) in enumerate(pairs)]
    for copy in copies:
        copy.start()
    return copies


def finish_all(copies):
    for copy in copies:
        copy.wait()


def attn_forward_kernel(windows, x_in, gain_ref, shift_ref, w_in, bias_in, pos_ref, valid_ref,
                        prob_ref, q_ref, k_ref, v_ref, mixed_ref, normed_t_ref,
                        mask_s, q_s, k_s, v_s, mixed_s, x_ref, w_ref, bias_ref, in_sems):
    copies = begin(in_sems, (x_in, x_ref), *[(w_in.at[p], w_ref.at[p]) for p in range(3)], (bias_in, bias_ref))
    mask_s[...] = jnp.zeros(mask_s.shape, F32)
    for h in range(GROUP):
        mask_s[:, h * SLOT : h * SLOT + WIN] = valid_ref[...].astype(F32)
    masks = head_masks()
    ones = block_ones()
    low_half = lax.broadcasted_iota(jnp.int32, (SLOT, LANES), 1) < SLOT
    copies[0].wait()
    copies[4].wait()
    x = x_ref[...].astype(F32)
    rows = x.shape[0]
    groups = q_s.shape[0]
    xhat, _ = norm_parts(x)
    normed = (xhat * line(gain_ref) + line(shift_ref)).astype(BF)
    normed_t_ref[...] = normed.T
    for part, scratch in enumerate((q_s, k_s, v_s)):
        copies[1 + part].wait()
        got = mm(normed, w_ref[part])
        if part != 1:
            got = got + bias_ref[part // 2 : part // 2 + 1, :]
        fill(scratch, got.astype(BF).astype(F32), windows)

    def window(w, carry):
        allowed = jnp.broadcast_to(mask_s[pl.ds(w, 1), :], (SLOT, GROUP * SLOT)) > 0.5
        for g in range(groups):
            cols = slice(g * LANES, (g + 1) * LANES)
            places = pl.ds(w, SLOT, stride=windows + 1)
            q = q_s[g, places, :].astype(BF)
            k = k_s[g, places, :].astype(BF)
            v = v_s[g, places, :].astype(BF)
            q_ref[w, :, cols] = q
            k_ref[w, :, cols] = k
            v_ref[w, :, cols] = v
            scores = mm(q, spread(k, masks), LAST_LAST) * SCALING + pos_ref[g]
            scores = jnp.where(allowed, scores, -1000000000.0)
            top = jnp.concatenate([row_max(scores[:, :LANES], low_half), row_max(scores[:, LANES:], low_half)], axis=1)
            e = jnp.exp(scores - top)
            total = mm(e.astype(BF), ones)
            inv = pl.reciprocal(total, approx=True)
            prob = (e * (inv * (2.0 - total * inv))).astype(BF)
            prob_ref[w, g] = prob
            mixed_s[g, places, :] = mm(prob, spread(v, masks))
        return carry

    lax.fori_loop(0, windows, window, 0, unroll=2)
    mixed_ref[...] = empty(mixed_s, windows)


def middle_kernel(heads, me_ref, x_in, own_in, peer_in, bias_ref, gain_ref, shift_ref, *refs):
    if heads:
        half_in, rest_in, middle_ref, nm_ref, x_ref, own_ref, peer_ref, proj_ref, sems = refs
        lines = half_in.shape[0]
        core = me_ref[0] & 1
        place = lambda c: proj_ref.at[pl.ds(pl.multiple_of(c * lines, lines), lines), :]
        copies = begin(sems, (peer_in, peer_ref), (half_in, place(core)), (rest_in, place(1 - core)), (x_in, x_ref),
                       (own_in, own_ref))
        finish_all(copies[:3])
        peer = mm(peer_ref[...], proj_ref[...])
        finish_all(copies[3:])
    else:
        middle_ref, nm_ref, x_ref, own_ref, peer_ref, sems = refs
        finish_all(begin(sems, (x_in, x_ref), (own_in, own_ref), (peer_in, peer_ref)))
        peer = peer_ref[...].astype(F32)
    middle = x_ref[...].astype(F32) + (own_ref[...].astype(F32) + peer) + line(bias_ref)
    middle_ref[...] = middle
    xhat, _ = norm_parts(middle)
    nm_ref[...] = (xhat * line(gain_ref) + line(shift_ref)).astype(BF)


def mlp_kernel(nm_ref, cot_ref, fc1_ref, b1_ref, fc2_ref, hid_ref, gpre_ref, out_ref, gmid_ref):
    hidden_size = fc1_ref.shape[1]
    features = fc1_ref.shape[0]
    step = 256 if hidden_size % 256 == 0 else 128
    count = hidden_size // step

    nm = nm_ref[...]
    cot = cot_ref[...]

    def units(c, carry):
        cols = pl.ds(pl.multiple_of(c * step, step), step)
        pre = mm(nm, fc1_ref[:, cols]) + b1_ref[:, cols]
        phi = 0.5 * (1.0 + lax.erf(pre * (0.5 ** 0.5)))
        hid_ref[:, cols] = (pre * phi).astype(BF)
        slope = phi + pre * (jnp.exp(-0.5 * pre * pre) * 0.3989422804014327)
        gpre_ref[:, cols] = (mm(cot, fc2_ref[cols, :], LAST_LAST) * slope).astype(BF)
        return carry

    lax.fori_loop(0, count, units, 0)

    def tile(c, carry):
        cols = pl.ds(pl.multiple_of(c * 256, 256), 256)
        gmid_ref[:, cols] = mm(gpre_ref[...], fc1_ref[cols, :], LAST_LAST).astype(BF)
        out_ref[:, cols] = mm(hid_ref[...], fc2_ref[:, cols]).astype(BF)
        return carry

    lax.fori_loop(0, features // 256, tile, 0)

def mlp_weights_kernel(count, split, me_ref, *refs):
    inputs, refs = refs[: 4 * count], refs[4 * count :]
    n_out = 5 if split else 3
    gb1_ref, *outs = refs[:n_out]
    held = refs[n_out : n_out + 4 * count]
    nts = refs[n_out + 4 * count : n_out + 5 * count]
    g1_ref, g2_ref, in_sems, unit_sems, out_sems = refs[n_out + 5 * count :]
    blocks = [held[4 * b : 4 * b + 4] for b in range(count)]
    hidden_size = g1_ref.shape[1]
    features = g1_ref.shape[0]
    step = 384 if hidden_size % 384 == 0 else 128
    wide = features if hidden_size % features == 0 else step

    def units_in(j):
        cols = ds(j * step, step)
        return [pltpu.make_async_copy(inputs[4 * b + 2].at[:, cols], held[4 * b + 2].at[:, cols], unit_sems.at[b, j])
                for b in range(count)]

    order = [4 * b + k for k in (0, 1) for b in range(count)]
    copies = dict(zip(order, begin(in_sems, *[(inputs[i], held[i]) for i in order])))
    for j in range(hidden_size // step):
        for copy in units_in(j):
            copy.start()
    last = [pltpu.make_async_copy(inputs[4 * b + 3], held[4 * b + 3], in_sems.at[2 * count + b]) for b in range(count)]
    for copy in last:
        copy.start()
    finish_all([copies[4 * b] for b in range(count)])
    for block, nt in zip(blocks, nts):
        nt[...] = block[0][...].T
    finish_all([copies[4 * b + 1] for b in range(count)])

    def second(j, carry):
        finish_all(units_in(j))
        cols = ds(j * step, step)
        g2_ref[cols, :] = sum(mm(hid_ref[:, cols], cot_ref[...], ROWS_ROWS) for _, cot_ref, hid_ref, _ in blocks).astype(BF)
        return carry

    def first(j, carry):
        cols = ds(j * wide, wide)
        g1_ref[:, cols] = sum(mm(nt[...], block[3][:, cols]) for nt, block in zip(nts, blocks)).astype(BF)
        return carry

    lax.fori_loop(0, hidden_size // step, second, 0)
    me = me_ref[0]
    sent = []

    def send(k, source, target):
        sent.append(pltpu.make_async_copy(source, target, out_sems.at[k]))
        sent[-1].start()

    if split:
        for i, (target, y_rel, z_rel, c, y, z) in enumerate(each_block(me, outs[2], outs[3])):
            send(i, g2_ref.at[ds(c * 768 + y * 384 + z * 96, 96), :], target.at[y_rel, z_rel])
    else:
        send(0, g2_ref, outs[1])
    finish_all(last)
    gb1_ref[...] = sum(jnp.sum(block[3][...].astype(F32), axis=0, keepdims=True) for block in blocks)
    lax.fori_loop(0, hidden_size // wide, first, 0)
    if split:
        for i, (target, y_rel, z_rel, c, y, z) in enumerate(each_block(me, outs[0], outs[1])):
            send(16 + i, g1_ref.at[ds(y * 384 + z * 96, 96), ds(c * 768, 768)], target.at[y_rel, z_rel])
    else:
        send(1, g1_ref, outs[0])
    finish_all(sent)


def middle_back_kernel(own_ref, peer_ref, middle_ref, cot_ref, gain_ref, gmiddle_ref, branch_ref, sums_ref):
    upstream = cot_ref[...].astype(F32)
    xhat, inv = norm_parts(middle_ref[...])
    gmid = own_ref[...].astype(F32) + peer_ref[...].astype(F32)
    sums_ref[0:1, :] = jnp.sum(gmid * xhat, axis=0, keepdims=True)
    sums_ref[1:2, :] = jnp.sum(gmid, axis=0, keepdims=True)
    gmiddle = upstream + norm_back(xhat, inv, line(gain_ref), gmid)
    gmiddle_ref[...] = gmiddle
    branch_ref[...] = gmiddle.astype(BF)
    sums_ref[2:3, :] = jnp.sum(gmiddle, axis=0, keepdims=True)
    sums_ref[3:4, :] = jnp.sum(upstream, axis=0, keepdims=True)


def attn_backward_kernel(windows, branch_ref, x_ref, prob_ref, q_ref, k_ref, v_ref, w_ref, proj_ref,
                         grads_ref, gqv_ref, gpos_ref, part_ref, sums_ref, gm_s, gq_s, gk_s, gv_s):
    rows = branch_ref.shape[0]
    groups = gm_s.shape[0]
    gpos_ref[...] = jnp.zeros(gpos_ref.shape, F32)
    masks = head_masks()
    masks_f = [m.astype(F32) for m in masks]
    low_half = lax.broadcasted_iota(jnp.int32, (SLOT, LANES), 1) < SLOT
    fill(gm_s, mm(branch_ref[...], proj_ref[...], LAST_LAST).astype(BF).astype(F32), windows)

    def window(w, carry):
        for g in range(groups):
            cols = slice(g * LANES, (g + 1) * LANES)
            places = pl.ds(w, SLOT, stride=windows + 1)
            gm = gm_s[g, places, :].astype(BF)
            q = q_ref[w, :, cols]
            k = k_ref[w, :, cols]
            v = v_ref[w, :, cols]
            prob = prob_ref[w, g]
            prob_f = prob.astype(F32)
            gprob = mm(gm, spread(v, masks), LAST_LAST)
            both = prob_f * gprob
            delta = jnp.concatenate([row_sum(both[:, :LANES], low_half), row_sum(both[:, LANES:], low_half)], axis=1)
            gs = (both - prob_f * delta).astype(BF)
            gpos_ref[g] += gs.astype(F32)
            gq_s[g, places, :] = mm(gs, spread(k, masks)) * SCALING
            gk_s[g, places, :] = collect(mm(gs, q, ROWS_ROWS), masks_f) * SCALING
            gv_s[g, places, :] = collect(mm(prob, gm, ROWS_ROWS), masks_f)
        return carry

    lax.fori_loop(0, windows, window, 0, unroll=2)
    back = None
    for part, scratch in enumerate((gq_s, gk_s, gv_s)):
        grad = empty(scratch, windows)
        grads_ref[part] = grad
        if part != 1:
            width = grad.shape[1]
            lanes = slice(part // 2 * width, (part // 2 + 1) * width)
            gqv_ref[:, lanes] = jnp.sum(grad.astype(F32), axis=0, keepdims=True)
        term = mm(grad, w_ref[part], LAST_LAST)
        back = term if back is None else back + term
    part_ref[...] = back.astype(BF)
    xhat, _ = norm_parts(x_ref[...].astype(F32))
    sums_ref[0:1, :] = jnp.sum(back * xhat, axis=0, keepdims=True)
    sums_ref[1:2, :] = jnp.sum(back, axis=0, keepdims=True)


def place_offset(i):
    return i // WSIDE * (2 * WSIDE - 1) + i % WSIDE


def offset_picks():
    row = lax.broadcasted_iota(jnp.int32, (2 * LANES, 2 * SLOT), 0)
    col = lax.broadcasted_iota(jnp.int32, (2 * LANES, 2 * SLOT), 1)
    j = col & (SLOT - 1)
    line = (j * 37) >> 8
    offset = place_offset(WIN - 1) - line * (2 * WSIDE - 1) - (j - line * WSIDE)
    hit = ((row & (LANES - 1)) == offset) & ((row >> 7) == (col >> 6)) & (j < WIN)
    return jnp.where(hit, 1.0, 0.0).astype(BF)


def position_kernel(table_ref, pos_ref, table_s, rows_s):
    heads = table_ref.shape[0]
    table_s[...] = jnp.zeros(table_s.shape, F32)
    table_s[0:heads, 0:REL] = table_ref[...]
    table = table_s[...]
    lines = table.shape[0]
    rows_s[WIN * lines :, :] = jnp.zeros((rows_s.shape[0] - WIN * lines, LANES), F32)
    for i in range(WIN):
        turned = pltpu.roll(table, (2 * LANES - place_offset(i)) % (2 * LANES), 1)
        rows_s[i * lines : (i + 1) * lines, :] = turned[:, :LANES]
    picks = offset_picks()
    for pair in range(pos_ref.shape[0] * 2):
        pieces = [rows_s[pl.ds(2 * pair + k, SLOT, stride=lines), :] for k in range(2)]
        rest = jnp.concatenate(pieces, axis=1)
        total = jnp.zeros((SLOT, 2 * SLOT), F32)
        for _ in range(3):
            top = rest.astype(BF)
            total = total + mm(top, picks)
            rest = rest - top.astype(F32)
        pos_ref[pair // 2, :, pair % 2 * LANES : (pair % 2 + 1) * LANES] = total


def attn_weights_kernel(count, split, me_ref, sums2_ref, gb1_ref, *refs):
    blocks, refs = [refs[7 * b : 7 * b + 7] for b in range(count)], refs[7 * count :]
    *outs, small_ref = refs[:3]
    gw_ref, gproj_ref, rows_s, out_sems = refs[3:]
    gproj, gqv, gpos, sums = 0.0, 0.0, 0.0, 0.0
    for _, mixed_ref, branch_ref, _, gqv_ref, gpos_ref, sums_ref in blocks:
        gproj = gproj + mm(mixed_ref[...], branch_ref[...], ROWS_ROWS)
        gqv, gpos, sums = gqv + gqv_ref[...], gpos + gpos_ref[...], sums + sums_ref[...]
    width, features = gproj.shape
    gproj_ref[...] = gproj.astype(BF)
    hidden = gb1_ref.shape[1]
    lines = [sums[k : k + 1] for k in range(2)] + [sums2_ref[k : k + 1, :] for k in range(4)]
    lines.append(gqv)
    lines += [gb1_ref[:, k : min(k + features, hidden)] for k in range(0, hidden, features)]
    small = jnp.concatenate(
        [jnp.concatenate([line, jnp.zeros((1, features - line.shape[1]), F32)], axis=1) if line.shape[1] < features else line
         for line in lines] + [jnp.zeros((12 - len(lines), features), F32)], axis=0)
    picks = offset_picks()
    for pair in range(gpos.shape[0] * 2):
        rest = gpos[pair // 2][:, pair % 2 * LANES : (pair % 2 + 1) * LANES]
        total = jnp.zeros((SLOT, 2 * LANES), F32)
        for _ in range(2):
            top = rest.astype(BF)
            total = total + mm(top, picks, LAST_LAST)
            rest = rest - top.astype(F32)
        for k in range(2):
            rows_s[pl.ds(2 * pair + k, SLOT, stride=16), :] = total[:, k * LANES : (k + 1) * LANES]
    for h in range(gpos.shape[0] * 4, 16):
        rows_s[pl.ds(h, SLOT, stride=16), :] = jnp.zeros((SLOT, LANES), F32)
    table = jnp.zeros((16, 2 * LANES), F32)
    for i in range(WIN):
        row = jnp.concatenate([rows_s[i * 16 : (i + 1) * 16, :], jnp.zeros((16, LANES), F32)], axis=1)
        table = table + (pltpu.roll(row, place_offset(i), 1) if i else row)
    packed = [jnp.concatenate([table[3 * r + k : 3 * r + k + 1] for k in range(3)], axis=1) for r in range(4)]
    small_ref[...] = jnp.concatenate([small] + packed, axis=0).astype(BF)
    sent = []

    def send(k, source, target):
        sent.append(pltpu.make_async_copy(source, target, out_sems.at[k]))
        sent[-1].start()

    if split:
        for i, (target, y_rel, z_rel, c, y, z) in enumerate(each_block(me_ref[0], *outs)):
            send(i, gproj_ref.at[ds((c * 4 + y * 2 + (z >> 1)) * 48, 48), ds((z & 1) * 384, 384)],
                 target.at[y_rel, z_rel, 48:96, 384:768])
    else:
        send(0, gproj_ref, outs[1])
    for part in range(3):
        gw = 0.0
        for normed_t_ref, _, _, grads_ref, _, _, _ in blocks:
            gw = gw + mm(normed_t_ref[...], grads_ref[part])
        gw_ref[part] = gw.astype(BF)
        if split:
            for i, (target, y_rel, z_rel, c, y, z) in enumerate(each_block(me_ref[0], *outs)):
                send(16 * (part + 1) + i, gw_ref.at[part, ds(c * 384 + y * 192 + z * 48, 48), :],
                     target.at[y_rel, z_rel, part // 2 * 48 : part // 2 * 48 + 48, part % 2 * 384 : part % 2 * 384 + 384])
        else:
            send(1 + part, gw_ref.at[part], outs[0].at[part])
    finish_all(sent)


def input_back_kernel(own_ref, peer_ref, x_ref, gain_ref, gmiddle_ref, gpatch_ref):
    gnorm = own_ref[...].astype(F32) + peer_ref[...].astype(F32)
    xhat, inv = norm_parts(x_ref[...].astype(F32))
    gpatch_ref[...] = (gmiddle_ref[...] + norm_back(xhat, inv, line(gain_ref), gnorm)).astype(BF)


def finish_kernel(y_rels, me_ref, *refs):
    sources, refs = refs[:2], refs[2:]
    if y_rels[0] == 1:
        refs = refs[2:]
    outs, held, wide, (in_sems, out_sems) = refs[:2], refs[2:4], refs[4:6], refs[6:]
    copies = begin(in_sems, *zip(sources, held))
    sent = []

    def put(value, k, where):
        wide[k][where] = value.astype(F32)
        sent.append(pltpu.make_async_copy(wide[k].at[where], outs[k].at[where], out_sems.at[len(sent)]))
        sent[-1].start()

    for source, y_rel, z_rel, c, y, z in each_block(me_ref[0], 0, 1):
        if y_rel not in y_rels:
            continue
        if z_rel == 0:
            copies[source].wait()
        piece = held[source].at[z_rel]
        lines = ds(c * 384 + y * 192 + z * 48, 48)
        put(piece[0:48, 0:384], 0, (0, lines, slice(None)))
        put(piece[0:48, 384:768], 0, (1, lines, slice(None)))
        put(piece[48:96, 0:384], 0, (2, lines, slice(None)))
        put(piece[48:96, 384:768], 1, (ds((c * 4 + y * 2 + (z >> 1)) * 48, 48), ds((z & 1) * 384, 384)))
    finish_all(sent)


def finish_mlp_kernel(me_ref, *refs):
    sources, (g1_out, g2_out, small_ref), held, (g1_ref, g2_ref, small_s, in_sems, out_sems) = (
        refs[:4], refs[4:7], refs[7:11], refs[11:])
    copies = begin(in_sems, *zip(sources, held))
    sent = []

    def put(value, k, wide, out, where):
        wide[where] = value.astype(F32)
        sent.append(pltpu.make_async_copy(wide.at[where], out.at[where], out_sems.at[k, len(sent) // 2]))
        sent[-1].start()

    for source, y_rel, z_rel, c, y, z in each_block(me_ref[0], (0, 1), (2, 3)):
        source = source[y_rel]
        if z_rel == 0:
            copies[source].wait()
        piece = held[source].at[z_rel]
        put(piece[0:BLOCK, :], 0, g1_ref, g1_out, (ds(y * 384 + z * 96, 96), ds(c * 768, 768)))
        put(piece[BLOCK : 2 * BLOCK, :], 1, g2_ref, g2_out, (ds(c * 768 + y * 384 + z * 96, 96), slice(None)))
        small_s[z * 4 + y * 2 + c] = piece[2 * BLOCK :, :].astype(F32)
    total = small_s[0]
    for d in range(1, 16):
        total = total + small_s[d]
    small_ref[...] = total
    finish_all(sent)


def shape_of(*dims, dtype=F32):
    return jax.ShapeDtypeStruct(dims, dtype)


def call(kernel, outs, scratch, name, flops, smem, *args, far=(), far_outs=(), limit=VMEM_LIMIT, aliases=None):
    space = lambda is_far: pl.BlockSpec(memory_space=pltpu.HBM if is_far else pltpu.VMEM)
    in_specs = [pl.BlockSpec(memory_space=pltpu.SMEM)] * len(smem) + [space(i in far) for i in range(len(args))]
    return pl.pallas_call(
        kernel,
        out_shape=outs,
        in_specs=in_specs,
        out_specs=[space(i in far_outs) for i in range(len(outs))],
        scratch_shapes=scratch,
        compiler_params=pltpu.CompilerParams(vmem_limit_bytes=limit),
        cost_estimate=pl.CostEstimate(flops=flops, bytes_accessed=flops // 256, transcendentals=0),
        input_output_aliases=aliases or {},
        name=name,
    )(*smem, *args)


def like(*arrays):
    return [pltpu.VMEM(a.shape, a.dtype) for a in arrays]


def dma(*counts):
    return [pltpu.SemaphoreType.DMA(c if isinstance(c, tuple) else (c,)) for c in counts]


SMALL = 1000000


def position(table):
    heads = table.shape[0]
    groups = -(-heads // GROUP)
    return call(position_kernel, [shape_of(groups, SLOT, GROUP * SLOT)],
                [pltpu.VMEM((16, 2 * LANES), F32), pltpu.VMEM((16 * SLOT, LANES), F32)], "position", SMALL, (), table)[0]


def attn_forward(windows, x, ln1, qkv, qv_bias, pos, mask):
    rows, features = x.shape
    width = qkv.shape[2]
    groups = width // LANES
    tile = shape_of(windows, SLOT, width, dtype=BF)
    outs = [shape_of(windows, groups, SLOT, GROUP * SLOT, dtype=BF), tile, tile, tile, shape_of(rows, width, dtype=BF),
            shape_of(features, rows, dtype=BF)]
    scratch = [pltpu.VMEM((windows, GROUP * SLOT), F32)] + [pltpu.VMEM((groups, SLOT * (windows + 1), LANES), F32)] * 4
    scratch += like(x, qkv, qv_bias) + dma(5)
    return call(functools.partial(attn_forward_kernel, windows), outs, scratch, "attn_forward", SMALL, (),
                x, *ln1, qkv, qv_bias, pos, mask, far=(0, 3, 4), limit=ALL_VMEM)


def middle_norm(me, x, own, peer, bias, ln2, halves):
    rows, features = x.shape
    scratch = like(x, own, peer)
    if halves:
        scratch += [pltpu.VMEM((2 * halves[0].shape[0], features), BF)]
    return call(functools.partial(middle_kernel, bool(halves)), [shape_of(rows, features), shape_of(rows, features, dtype=BF)],
                scratch + dma(5), "middle", SMALL, (me,), x, own, peer, bias, *ln2, *halves, far=(0, 1, 2, 6, 7),
                limit=ALL_VMEM)


def mlp(nm, cot, fc1, fc1_bias, fc2):
    rows, features = nm.shape
    hidden = fc2.shape[0]
    outs = [shape_of(rows, hidden, dtype=BF)] * 2 + [shape_of(rows, features, dtype=BF)] * 2
    return call(mlp_kernel, outs, [], "mlp", SMALL, (), nm, cot, fc1, fc1_bias, fc2)


def mlp_weights(split, me, blocks):
    rows, features = blocks[0][0].shape
    hidden = blocks[0][2].shape[1]
    grads = [shape_of(features, hidden, dtype=BF), shape_of(hidden, features, dtype=BF)]
    outs = [shape_of(1, hidden)] + ([shape_of(2, 4, BLOCK, features, dtype=BF)] * 4 if split else grads)
    flat = [a for b in blocks for a in b]
    scratch = like(*flat) + [pltpu.VMEM((features, rows), BF)] * len(blocks) + like(*grads) + dma(3 * len(blocks), (len(blocks), hidden // 128), 32)
    return call(functools.partial(mlp_weights_kernel, len(blocks), split), outs, scratch, "mlp_weights", SMALL,
                (me,), *flat, far=range(len(flat)), far_outs=range(1, len(outs)), limit=ALL_VMEM)


def middle_back(own, peer, middle, cot, gain):
    rows, features = middle.shape
    return call(
        middle_back_kernel, [shape_of(rows, features), shape_of(rows, features, dtype=BF), shape_of(4, features)], [],
        "middle_back", 20000 * SMALL, (), own, peer, middle, cot, gain)


def attn_backward(windows, branch, x, kept, qkv, proj):
    rows, features = branch.shape
    width = proj.shape[0]
    groups = width // LANES
    outs = [shape_of(3, rows, width, dtype=BF), shape_of(1, 2 * width), shape_of(groups, SLOT, GROUP * SLOT),
            shape_of(rows, features, dtype=BF), shape_of(2, features)]
    scratch = [pltpu.VMEM((groups, SLOT * (windows + 1), LANES), F32)] * 4
    return call(functools.partial(attn_backward_kernel, windows), outs, scratch, "attn_backward", SMALL, (),
                branch, x, *kept, qkv, proj)


def attn_weights(split, me, sums2, gb1, blocks):
    features = blocks[0][0].shape[0]
    width = blocks[0][1].shape[1]
    grads = [shape_of(3, features, width, dtype=BF), shape_of(width, features, dtype=BF)]
    outs = ([shape_of(2, 4, BLOCK, features, dtype=BF)] * 2 if split else grads) + [shape_of(16, features, dtype=BF)]
    scratch = like(*grads) + [pltpu.VMEM((16 * SLOT, LANES), F32)]
    flat = [a for b in blocks for a in b]
    return call(functools.partial(attn_weights_kernel, len(blocks), split), outs, scratch + dma(64),
                "attn_weights", SMALL, (me,), sums2, gb1, *flat, far_outs=(0, 1))


def input_back(own, peer, x, gain, gmiddle):
    rows, features = x.shape
    return call(input_back_kernel, [shape_of(rows, features, dtype=BF)], [], "input_back", SMALL, (),
                own, peer, x, gain, gmiddle)[0]


def finish(me, y_rel, sources, outs, before=()):
    scratch = like(*sources, *outs) + dma(2, 8 * 4)
    return call(functools.partial(finish_kernel, (y_rel,)), list(outs), scratch, "finish", SMALL, (me,), *sources, *before,
                far=range(2 + len(before)), far_outs=range(len(outs)), aliases={3: 0, 4: 1} if before else {})


def finish_mlp(me, sources):
    features = sources[0].shape[2]
    outs = [shape_of(features, 2 * features), shape_of(2 * features, features), shape_of(16, features)]
    scratch = like(*sources, *outs[:2]) + [pltpu.VMEM((16, 16, features), F32)] + dma(4, (2, 16))
    return call(finish_mlp_kernel, outs, scratch, "finish_mlp", SMALL, (me,), *sources, far=range(4), far_outs=(0, 1))


def across(v):
    return lax.ppermute(v, "mp", [(0, 1), (1, 0)])


def flip(v, bits):
    return lax.ppermute(v, "dp", [(i, i ^ bits) for i in range(16)])


def after(v, *others):
    return lax.optimization_barrier((v, *others))[0]


def total_of(terms):
    total = terms[0].astype(F32)
    for t in terms[1:]:
        total = total + t.astype(F32)
    return total.astype(BF)


def side_send(keep, got):
    return total_of([keep[1], got[1]])


def line_sends(keep, got, side):
    return [total_of([keep[0, k], got[0, k], side[k]]) for k in (1, 2, 3)]


def own_piece(keep, got, side, line):
    return total_of([keep[0, 0], got[0, 0], side[0], *line])


def flip_line(pieces):
    return [flip(p, LINE * k) for k, p in zip((1, 2, 3), pieces)]


def sum_line(sends):
    near, far, both = sends
    return [flip(near, LINE), flip(total_of([far, flip(both, LINE)]), 2 * LINE)]


def gather_line(piece):
    far = flip(piece, 2 * LINE)
    return [flip(piece, LINE), far, flip(far, LINE)]


def shards(
    dp_size,
    mp_size,
    patches,
    token_valid,
    ln1_gain,
    ln1_shift,
    qkv_weight,
    qv_bias,
    bias_table,
    proj_weight,
    proj_bias,
    ln2_gain,
    ln2_shift,
    fc1_weight,
    fc1_bias,
    fc2_weight,
    fc2_bias,
    cotangent,
):
    windows, _, features = patches.shape
    rows = windows * WIN
    width = proj_weight.shape[0]
    heads = width // HEAD
    fast = mp_size == 2 and dp_size == 16 and features == 768
    x = patches.transpose(1, 0, 2).reshape(rows, features)
    cot = cotangent.transpose(1, 0, 2).reshape(rows, features)
    row = lambda a: a.reshape(1, -1)
    extra = -width % LANES
    qkv = jnp.pad(qkv_weight.transpose(1, 0, 2), ((0, 0), (0, 0), (0, extra)))
    proj = jnp.pad(proj_weight, ((0, extra), (0, 0)))
    pos = position(bias_table.T)
    bias = jnp.pad(qv_bias, ((0, 0), (0, extra)))
    valid = token_valid.astype(F32)
    ln1, ln2 = (ln1_gain, ln1_shift), (ln2_gain, ln2_shift)

    def blocks_of(v):
        return [v, across(v)] if fast else list(lax.all_gather(v, "mp"))

    def own_sums(parts):
        if fast:
            return parts[0], across(parts[1])
        own = lax.psum_scatter(jnp.concatenate(parts), "mp", scatter_dimension=0, tiled=True)
        return own, jnp.zeros_like(own)

    index = lax.axis_index("dp").astype(jnp.int32)
    me = index.reshape(1)
    valids = blocks_of(valid)
    kept, xs = [], []
    for x_b, valid_b in zip([x, across(after(x, valids[1]))] if fast else blocks_of(x), valids):
        if kept:
            x_b = after(x_b, kept[0][4])
        xs.append(x_b)
        kept.append(attn_forward(windows, x_b, ln1, qkv, bias, pos, valid_b))
    project = lambda mixed, weight: jnp.dot(mixed, weight, preferred_element_type=F32).astype(BF)
    if fast:
        core = index & 1
        half = across(lax.dynamic_slice_in_dim(after(proj, valids[1], pos), core * (width // 2), width // 2, 0))
        cots = [cot, across(after(cot, valids[1], pos))]
        mixed = across(kept[1][4])
        half = after(half, kept[1][4])
        rest = flip(half, CORE)
        parts, halves = (project(after(kept[0][4], cots[1], half), proj), mixed), (half, rest)
    else:
        parts, halves = own_sums([project(k[4], proj) for k in kept]), ()
        cots = blocks_of(cot)
    middle, nm = middle_norm(me, x, *parts, proj_bias, ln2, halves)

    blocks, outs, gmids = [], [], []
    for nm_b, cot_b in zip(blocks_of(nm), cots):
        if blocks:
            nm_b = after(nm_b, gmids[-1])
        hid, gpre, out_b, gmid_b = mlp(nm_b, cot_b, fc1_weight, row(fc1_bias), fc2_weight)
        blocks.append((nm_b, cot_b, hid, gpre))
        outs.append(out_b)
        gmids.append(gmid_b)
    gmid_own, gmid_peer = own_sums(gmids)
    gb1, *g_mlp = mlp_weights(fast, me, blocks)
    outs = own_sums(outs)
    gmid_peer = after(gmid_peer, gb1)
    gmiddle, branch, sums2 = middle_back(gmid_own, gmid_peer, middle, cot, ln2[0])
    branches = blocks_of(branch)
    if fast:
        keep1, send1, keep2, send2 = g_mlp
        got1, got2 = after(flip(send1, CORE), branch), after(flip(send2, CORE), branch)
        side1, side2 = side_send(keep1, got1), side_send(keep2, got2)
        branches[0] = after(branches[0], side1, side2)
    backs, gparts = [], []
    for b, kept_b in enumerate(kept):
        if b == 1 and fast:
            side1 = after(flip(side1, SIDE), gparts[0])
            line1 = line_sends(keep1, got1, side1)
            branches[1] = after(branches[1], *line1, gparts[0])
        *back, gpart, gsum = attn_backward(windows, branches[b], xs[b], kept_b[:4], qkv, proj)
        backs.append((*back, gsum))
        gparts.append(gpart)
    if fast:
        side2 = after(flip(side2, SIDE), gparts[1])
        line2 = line_sends(keep2, got2, side2)
        line1 = [after(r, gparts[1]) for r in flip_line(line1)]
        piece1 = own_piece(keep1, got1, side1, line1)
        branches[0] = after(branches[0], piece1, *line2, outs[1])
    *g_attn, small = attn_weights(
        fast, me, sums2, gb1, [(k[5], k[4], br, *back) for k, br, back in zip(kept, branches, backs)])
    gnorms = own_sums(gparts)
    gpatch = input_back(*gnorms, x, ln1[0], gmiddle)
    output = (middle + outs[0].astype(F32) + outs[1].astype(F32) + row(fc2_bias)).astype(BF)

    if fast:
        line2 = [after(r, small) for r in flip_line(line2)]
        piece2 = own_piece(keep2, got2, side2, line2)
        keep, send = g_attn
        got = flip(after(send, piece2), CORE)
        side = flip(side_send(keep, got), SIDE)
        fc = jnp.concatenate([piece1, piece2, small], axis=0)
        fc_quad = jnp.stack([fc] + [after(r, output, gpatch) for r in gather_line(fc)])
        side = after(side, fc_quad, output, gpatch)
        line = sum_line(line_sends(keep, got, side))
        piece = own_piece(keep, got, side, line)
        quad = jnp.stack([piece] + gather_line(piece))
        fc_pair = after(flip(fc_quad, SIDE), quad)
        g_fc1, g_fc2, small = finish_mlp(me, (fc_quad, fc_pair, after(flip(fc_quad, CORE), quad), after(flip(fc_pair, CORE), quad)))
        totals = small[0:6] + across(small[0:6])
        pair = after(flip(quad, SIDE), totals)
        shapes = shape_of(3, features, width), shape_of(width, features)
        half_done = finish(me, 0, (quad, flip(quad, CORE)), shapes)
        pair = after(pair, half_done[0])
        gw, gproj = finish(me, 1, (pair, flip(pair, CORE)), shapes, half_done)
    else:
        g_fc1, g_fc2, gw, gproj = [g.astype(F32) for g in lax.psum((*g_mlp, *g_attn), "dp")]
        gw, gproj = gw[:, :, :width], gproj[:width]
        small = lax.psum(small, "dp").astype(F32)
        totals = lax.psum(small[0:6], "mp")
    padded = width + extra
    gqv = jnp.stack([small[6, :width], small[6, padded : padded + width]])
    gb1 = small[7:12].reshape(-1)[: gb1.size]
    gt = small[12:].reshape(12, 2 * LANES)[:heads, :REL].T

    unrow = lambda a: a.reshape(WIN, windows, features).transpose(1, 0, 2)
    return (
        unrow(output),
        unrow(gpatch),
        totals[0],
        totals[1],
        gw.transpose(1, 0, 2),
        gqv,
        gt,
        gproj,
        totals[4],
        totals[2],
        totals[3],
        g_fc1,
        gb1,
        g_fc2,
        totals[5],
    )


def solution(mesh):
    placed = (
        P(("dp", "mp"), None, None),
        P(("dp", "mp"), None),
        P(),
        P(),
        P(None, None, "mp"),
        P(None, "mp"),
        P(None, "mp"),
        P("mp", None),
        P(),
        P(),
        P(),
        P(None, "mp"),
        P("mp"),
        P("mp", None),
        P(),
        P(("dp", "mp"), None, None),
    )
    return jax.shard_map(
        functools.partial(shards, mesh.shape["dp"], mesh.shape["mp"]),
        mesh=mesh,
        in_specs=placed,
        out_specs=(
            P(("dp", "mp"), None, None),
            P(("dp", "mp"), None, None),
            P(),
            P(),
            P(None, None, "mp"),
            P(None, "mp"),
            P(None, "mp"),
            P("mp", None),
            P(),
            P(),
            P(),
            P(None, "mp"),
            P("mp"),
            P("mp", None),
            P(),
        ),
        check_vma=False,
    )
```
